32 devices in a mesh: ctx: 8 (over z, x), fsdp: 4 (over y, core).
Axes of the slice: x: 2, y: 2, z: 4, core: 2. Of those that a mesh axis runs over, the one named last changes fastest.
Arguments:
- hidden_in: bfloat16 [4, 2048, 640], P('fsdp', 'ctx'), may hold values from -6 to 6
- positions: int32 [4, 2048], P('fsdp', 'ctx'), may hold values from 0 to 2045, as said below
- query_weight: bfloat16 [640, 1024], P('fsdp'), may hold values from -0.25 to 0.25
- key_weight: bfloat16 [640, 256], P('fsdp'), may hold values from -0.25 to 0.25
- value_weight: bfloat16 [640, 256], P('fsdp'), may hold values from -0.25 to 0.25
- output_weight: bfloat16 [1024, 640], P('fsdp'), may hold values from -0.1875 to 0.1875
- gate_weight: bfloat16 [640, 2048], P('fsdp'), may hold values from -0.25 to 0.25
- up_weight: bfloat16 [640, 2048], P('fsdp'), may hold values from -0.25 to 0.25
- down_weight: bfloat16 [2048, 640], P('fsdp'), may hold values from -0.125 to 0.125
- input_gain: bfloat16 [640], P('fsdp'), may hold values from -0.3984375 to 0.3984375
- mixer_gain: bfloat16 [640], P('fsdp'), may hold values from -0.3984375 to 0.3984375
- feed_gain: bfloat16 [640], P('fsdp'), may hold values from -0.3984375 to 0.3984375
- final_gain: bfloat16 [640], P('fsdp'), may hold values from -0.3984375 to 0.3984375
- query_gain: bfloat16 [256], P('fsdp'), may hold values from 0 to 0.796875
- key_gain: bfloat16 [256], P('fsdp'), may hold values from 0 to 0.796875
- out_grad: bfloat16 [4, 2048, 640], P('fsdp', 'ctx'), may hold values from -6 to 6
Outputs:
- hidden_out: bfloat16 [4, 2048, 640], P('fsdp', 'ctx')
- grad_input: float32 [4, 2048, 640], P('fsdp', 'ctx')
- grad_query: float32 [640, 1024], P('fsdp')
- grad_key: float32 [640, 256], P('fsdp')
- grad_value: float32 [640, 256], P('fsdp')
- grad_output: float32 [1024, 640], P('fsdp')
- grad_gate: float32 [640, 2048], P('fsdp')
- grad_up: float32 [640, 2048], P('fsdp')
- grad_down: float32 [2048, 640], P('fsdp')
- grad_input_gain: float32 [640], P('fsdp')
- grad_mixer_gain: float32 [640], P('fsdp')
- grad_feed_gain: float32 [640], P('fsdp')
- grad_final_gain: float32 [640], P('fsdp')
- grad_query_gain: float32 [256], P('fsdp')
- grad_key_gain: float32 [256], P('fsdp')
The draws below stay inside these ranges and needn't reach their ends.
Inputs may be any that keep to these rules, and one draw needn't show every extreme that they name: In each row, positions count up by one from 0 at the start of each of three documents; the second document starts within the first 256 tokens of the row and ends within its last 256 tokens.
All inputs are finite; a program needn't handle non-finite values.
Results may differ from the reference program's by a relative error of at most 0.024.
Values may be sent and summed in bfloat16 or wider, within the bound.
No kernel may reach another device: no remote copies, remote signals or barrier semaphores. Data moves between devices by JAX's collectives and lax.ppermute only.
A program may use at most 256 MiB of HBM per device.

```python
import jax
import jax.numpy as jnp
from jax import lax

D = 640
NH = 4
HD = 256
FF = 2048
TOK_DEV = 256
SEQ = 2048
SEQS = 4


def draw_positions(key, part):
    key = jax.random.fold_in(key, 7)
    head_key, tail_key, pick_key = jax.random.split(key, 3)
    head_length = jax.random.randint(head_key, (SEQS, 1), 1, TOK_DEV)
    tail_length = jax.random.randint(tail_key, (SEQS, 1), 1, TOK_DEV)
    picked = jax.random.randint(pick_key, (), 0, SEQS)
    chosen = (jnp.arange(SEQS, dtype=jnp.int32) == picked)[:, None]
    head_length = jnp.where(chosen, 1, head_length)
    tail_length = jnp.where(chosen, 1, tail_length)
    index = jnp.arange(SEQ, dtype=jnp.int32)[None, :]
    middle_end = SEQ - tail_length
    placed = jnp.where(index < head_length, index, jnp.where(index < middle_end, index - head_length, index - middle_end))
    return placed.astype(jnp.int32)


def level_of(own_key, shape, pieces, smallest, top_value):
    def one(position, shards_of):
        heights = jax.random.uniform(jax.random.fold_in(jax.random.fold_in(own_key, 6), position), (shards_of,), jnp.float32, smallest / len(pieces), top_value / len(pieces))
        return jnp.repeat(jnp.exp(heights), shape[position] // shards_of).reshape((-1,) + (1,) * (len(shape) - position - 1))

    factor_of = one(*pieces[0])
    for cut in pieces[1:]:
        factor_of = factor_of * one(*cut)
    return factor_of


def bell_draw(stream_key, dims, scale, most, pieces=(), kind=jnp.bfloat16):
    level = level_of(stream_key, dims, pieces, -0.22, 0.18) if pieces else 1.0
    values = jax.random.normal(stream_key, dims, jnp.float32) * scale * level
    return jnp.minimum(jnp.maximum(values, -most), most).astype(kind)


def setup_inputs(seed: int = 0) -> dict:
    streams_of = jax.random.split(jax.random.key(seed), 17)
    hidden_in = bell_draw(streams_of[0], (SEQS, SEQ, D), 1.0, 6.0, ((0, 4), (1, 8)))
    positions = draw_positions(jax.random.fold_in(streams_of[16], 71), 0)
    query_weight = bell_draw(streams_of[2], (D, NH * HD), D ** -0.5, 0.25, ((0, 4),))
    key_weight = bell_draw(streams_of[3], (D, HD), D ** -0.5, 0.25, ((0, 4),))
    value_weight = bell_draw(streams_of[4], (D, HD), D ** -0.5, 0.25, ((0, 4),))
    output_weight = bell_draw(streams_of[5], (NH * HD, D), (NH * HD) ** -0.5, 0.1875, ((0, 4),))
    gate_weight = bell_draw(streams_of[6], (D, FF), D ** -0.5, 0.25, ((0, 4),))
    up_weight = bell_draw(streams_of[7], (D, FF), D ** -0.5, 0.25, ((0, 4),))
    down_weight = bell_draw(streams_of[8], (FF, D), FF ** -0.5, 0.125, ((0, 4),))
    input_gain = jnp.clip(jax.random.uniform(streams_of[9], (D,), jnp.float32, -0.3984375, 0.3984375) * level_of(streams_of[9], (D,), ((0, 4),), -0.4, 0.0), -0.3984375, 0.3984375).astype(jnp.bfloat16)
    mixer_gain = jnp.clip(jax.random.uniform(streams_of[10], (D,), jnp.float32, -0.3984375, 0.3984375) * level_of(streams_of[10], (D,), ((0, 4),), -0.4, 0.0), -0.3984375, 0.3984375).astype(jnp.bfloat16)
    feed_gain = jnp.clip(jax.random.uniform(streams_of[11], (D,), jnp.float32, -0.3984375, 0.3984375) * level_of(streams_of[11], (D,), ((0, 4),), -0.4, 0.0), -0.3984375, 0.3984375).astype(jnp.bfloat16)
    final_gain = jnp.clip(jax.random.uniform(streams_of[12], (D,), jnp.float32, -0.3984375, 0.3984375) * level_of(streams_of[12], (D,), ((0, 4),), -0.4, 0.0), -0.3984375, 0.3984375).astype(jnp.bfloat16)
    query_gain = jnp.clip(0.796875 * jax.random.uniform(streams_of[13], (HD,), jnp.float32) ** level_of(streams_of[13], (HD,), ((0, 4),), -0.2, 0.2), 0.0, 0.796875).astype(jnp.bfloat16)
    key_gain = jnp.clip(0.796875 * jax.random.uniform(streams_of[14], (HD,), jnp.float32) ** level_of(streams_of[14], (HD,), ((0, 4),), -0.2, 0.2), 0.0, 0.796875).astype(jnp.bfloat16)
    out_grad = bell_draw(streams_of[15], (SEQS, SEQ, D), 1.0, 6.0, ((0, 4), (1, 8)))
    return {"hidden_in": hidden_in, "positions": positions, "query_weight": query_weight, "key_weight": key_weight, "value_weight": value_weight, "output_weight": output_weight, "gate_weight": gate_weight, "up_weight": up_weight, "down_weight": down_weight, "input_gain": input_gain, "mixer_gain": mixer_gain, "feed_gain": feed_gain, "final_gain": final_gain, "query_gain": query_gain, "key_gain": key_gain, "out_grad": out_grad}


@jax.custom_vjp
def low(v):
    return lax.optimization_barrier(v.astype(jnp.bfloat16)).astype(jnp.float32)

@jax.custom_vjp
def low_back(v):
    return v

def low_keep(v):
    return (low(v), None)

def low_pass(kept, grad):
    return (grad,)

def back_keep(v):
    return (v, None)

def back_low(kept, grad):
    return (low(grad),)
low.defvjp(low_keep, low_pass)
low_back.defvjp(back_keep, back_low)
eps = 1e-06
rope_base = 1000000.0
masked_score = -1e+30

def matmul(left, right):
    return jnp.dot(left, right, precision=lax.Precision.HIGHEST)

def rms_norm(value, gain):
    return value * lax.rsqrt(lax.optimization_barrier(jnp.mean(value * value, axis=-1, keepdims=True)) + eps) * (1.0 + gain)

def rotary_tables(positions, width):
    half = width // 2
    freqs = rope_base ** (-(jnp.arange(half, dtype=jnp.float32) * 2.0) / width)
    angles = positions.astype(jnp.float32)[:, None] * freqs[None, :]
    return (jnp.cos(angles), jnp.sin(angles))

def rotate(value, cosine_table, sine_table):
    half = value.shape[-1] // 2
    first_half = value[..., :half]
    second_half = value[..., half:]
    return jnp.concatenate([first_half * cosine_table - second_half * sine_table, second_half * cosine_table + first_half * sine_table], axis=-1)

def attention(queries, keys, values, positions):
    length = queries.shape[0]
    block_rows = min(512, length)
    blocks = length // block_rows

    def one_block(index):
        first_row = (index * block_rows).astype(jnp.int32)
        query_block = lax.dynamic_slice_in_dim(queries, first_row, block_rows, 0)
        place_block = lax.dynamic_slice_in_dim(positions, first_row, block_rows, 0)
        scores = jnp.einsum('bhd,kd->bhk', query_block, keys, precision=lax.Precision.HIGHEST)
        scores = low_back(scores)
        row_index = first_row + jnp.arange(block_rows, dtype=jnp.int32)
        col_index = jnp.arange(length, dtype=jnp.int32)
        allowed = (col_index[None, :] <= row_index[:, None]) & (col_index[None, :] >= (row_index - place_block)[:, None])
        allowed = allowed[:, None, :]
        scores = jnp.where(allowed, scores, masked_score)
        running_max = lax.optimization_barrier(jnp.max(scores, axis=-1, keepdims=True))
        expo = jnp.where(allowed, jnp.exp(scores - running_max), 0.0)
        running_sum = lax.optimization_barrier(jnp.sum(expo, axis=-1, keepdims=True))
        weighted = jnp.einsum('bhk,kd->bhd', low(expo), values, precision=lax.Precision.HIGHEST)
        return weighted / running_sum
    result = lax.map(jax.checkpoint(one_block), jnp.arange(blocks, dtype=jnp.int32))
    return result.reshape(length, NH, HD)

def layer(stream, query_full, key_full, value_full, output_full, gate_full, up_full, down_full, gain_in, gain_mix, gain_feed, gain_final, gain_query, gain_key, positions):
    length = stream.shape[0]
    normed_in = low(rms_norm(stream, gain_in))
    query_raw = low_back(matmul(normed_in, query_full)).reshape(length, NH, HD)
    key_raw = low_back(matmul(normed_in, key_full))
    values = low(low_back(matmul(normed_in, value_full)))
    cosine_table, sine_table = rotary_tables(positions, HD)
    queries = low(rotate(rms_norm(query_raw, gain_query), cosine_table[:, None, :], sine_table[:, None, :]) * HD ** (-0.5))
    keys = low(rotate(rms_norm(key_raw, gain_key), cosine_table, sine_table))
    mixed = attention(queries, keys, values, positions).reshape(length, NH * HD)
    mixed = low(low_back(mixed))
    projected = low_back(matmul(mixed, output_full))
    after_mix = stream + rms_norm(projected, gain_mix)
    normed_feed = low(rms_norm(after_mix, gain_feed))
    gate_value = low_back(matmul(normed_feed, gate_full))
    up_value = low_back(matmul(normed_feed, up_full))
    activated = low(jax.nn.gelu(gate_value, approximate=True) * up_value)
    down_value = low_back(matmul(activated, down_full))
    return after_mix + rms_norm(down_value, gain_final)

def reference(hidden_in, positions, query_weight, key_weight, value_weight, output_weight, gate_weight, up_weight, down_weight, input_gain, mixer_gain, feed_gain, final_gain, query_gain, key_gain, out_grad):
    weights = (query_weight.astype(jnp.float32), key_weight.astype(jnp.float32), value_weight.astype(jnp.float32), output_weight.astype(jnp.float32), gate_weight.astype(jnp.float32), up_weight.astype(jnp.float32), down_weight.astype(jnp.float32), input_gain.astype(jnp.float32), mixer_gain.astype(jnp.float32), feed_gain.astype(jnp.float32), final_gain.astype(jnp.float32), query_gain.astype(jnp.float32), key_gain.astype(jnp.float32))

    def per_sequence(sums, item):
        stream, places, cotangent = item

        def apply(value, *params):
            return layer(value, *params, places)
        output, pull = jax.vjp(apply, stream.astype(jnp.float32), *weights)
        grads = pull(cotangent.astype(jnp.float32))
        sums = tuple((total + piece for total, piece in zip(sums, grads[1:])))
        return (sums, (output.astype(jnp.bfloat16), grads[0]))
    zeros = tuple((jnp.zeros(w.shape, jnp.float32) for w in weights))
    sums, (hidden_out, grad_input) = lax.scan(per_sequence, zeros, (hidden_in, positions, out_grad))
    return (hidden_out, grad_input, sums[0], sums[1], sums[2], sums[3], sums[4], sums[5], sums[6], sums[7], sums[8], sums[9], sums[10], sums[11], sums[12])
```

```python
import jax
import jax.numpy as jnp
from jax import lax
from jax.sharding import PartitionSpec as P

eps = 1e-06
rope_base = 1000000.0
masked_score = -1e30


def rms_norm(value, gain):
    return value * lax.rsqrt(jnp.mean(value * value, axis=-1, keepdims=True) + eps) * (1.0 + gain)


def rotary_tables(positions, width):
    half = width // 2
    freqs = rope_base ** (-(jnp.arange(half, dtype=jnp.float32) * 2.0) / width)
    angles = positions.astype(jnp.float32)[:, None] * freqs[None, :]
    return (jnp.cos(angles), jnp.sin(angles))


def rotate(value, cosine_table, sine_table):
    half = value.shape[-1] // 2
    first_half = value[..., :half]
    second_half = value[..., half:]
    return jnp.concatenate(
        [
            first_half * cosine_table - second_half * sine_table,
            second_half * cosine_table + first_half * sine_table,
        ],
        axis=-1,
    )


def matmul_plain(left, right):
    return jnp.dot(left, right, preferred_element_type=jnp.float32)


def matmul_against(left, right):
    return jnp.einsum("ab,cb->ac", left, right, preferred_element_type=jnp.float32)


def matmul_outer(left, right):
    return jnp.einsum("ab,ac->bc", left, right, preferred_element_type=jnp.float32)


def gated(gate_value, up_value):
    return jax.nn.gelu(gate_value, approximate=True) * up_value


def visible(row_index, row_edge, start, count):
    col_index = start + jnp.arange(count, dtype=jnp.int32)
    return (col_index[None, :] <= row_index[:, None]) & (col_index[None, :] >= row_edge[:, None])


def block_group(tokens, groups):
    factor = 1
    limit = min(max(1, 2048 // tokens), groups)
    while factor * 2 <= limit and groups % (factor * 2) == 0:
        factor = factor * 2
    return tokens * factor


def sweep(step_fn, carry, keys_all, values_all, block_rows):
    blocks = keys_all.shape[0] // block_rows

    def turn(index, state):
        start = (index * block_rows).astype(jnp.int32)
        key_block = lax.dynamic_slice_in_dim(keys_all, start, block_rows, 0)
        value_block = lax.dynamic_slice_in_dim(values_all, start, block_rows, 0)
        return step_fn(state, (key_block, value_block), start)

    return lax.fori_loop(0, blocks, turn, carry)


def flip(value, axis, bit):
    size = lax.axis_size(axis)
    return lax.ppermute(value, axis, [(i, i ^ bit) for i in range(size)])


def gather_rows(shard):
    me = lax.axis_index("fsdp")
    rows = shard.shape[0]
    far = flip(shard, "fsdp", 2)
    near = flip(shard, "fsdp", 1)
    far_near = flip(far, "fsdp", 1)
    full = jnp.zeros((4 * rows,) + shard.shape[1:], shard.dtype)
    for step, block in enumerate((shard, near, far, far_near)):
        full = lax.dynamic_update_slice_in_dim(full, block, (me ^ step) * rows, 0)
    return full


def take_half(value, which, axis):
    half = value.shape[axis] // 2
    return lax.dynamic_slice_in_dim(value, which * half, half, axis)


def add_low(left, right):
    return (left.astype(jnp.float32) + right.astype(jnp.float32)).astype(jnp.bfloat16)


def reduce_ctx(value, axis):
    me = lax.axis_index("ctx")
    size = lax.axis_size("ctx")
    bits = []
    bit = 1
    while bit < size:
        bits.append(bit)
        bit *= 2
    for bit in bits:
        mine = (me // bit) % 2
        sent = flip(take_half(value, 1 - mine, axis), "ctx", bit)
        value = add_low(take_half(value, mine, axis), sent)
    for bit in reversed(bits):
        mine = (me // bit) % 2
        other = flip(value, "ctx", bit)
        low = jnp.where(mine == 0, value, other)
        high = jnp.where(mine == 0, other, value)
        value = jnp.concatenate([low, high], axis=axis)
    return value


def reduce_weight(grad, axis):
    me = lax.axis_index("fsdp")
    core = me % 2
    side = me // 2
    rows = grad.shape[0] // 4
    cut = grad.astype(jnp.bfloat16).reshape((2, 2, rows) + grad.shape[1:])
    keep = lax.dynamic_index_in_dim(cut, core, 1, keepdims=False)
    send = lax.dynamic_index_in_dim(cut, 1 - core, 1, keepdims=False)
    pair = add_low(keep, flip(send, "fsdp", 1))
    keep = lax.dynamic_index_in_dim(pair, side, 0, keepdims=False)
    send = lax.dynamic_index_in_dim(pair, 1 - side, 0, keepdims=False)
    own = add_low(keep, flip(send, "fsdp", 2))
    return reduce_ctx(own, axis).astype(jnp.float32)


def on_device(
    hidden_in,
    positions,
    query_weight,
    key_weight,
    value_weight,
    output_weight,
    gate_weight,
    up_weight,
    down_weight,
    input_gain,
    mixer_gain,
    feed_gain,
    final_gain,
    query_gain,
    key_gain,
    out_grad,
):
    tokens_dev = hidden_in.shape[1]
    model = hidden_in.shape[2]
    gain_pack = jnp.concatenate(
        [input_gain, mixer_gain, feed_gain, final_gain, query_gain, key_gain]
    )[None]
    gain_rows = gather_rows(jnp.broadcast_to(gain_pack, (16, gain_pack.shape[1]))).reshape(
        4, 16, gain_pack.shape[1]
    )[:, 0]
    piece = input_gain.shape[0]
    head_piece = query_gain.shape[0]
    gain_in, gain_mix, gain_feed, gain_final = [
        gain_rows[:, i * piece : (i + 1) * piece].reshape(-1) for i in range(4)
    ]
    gain_query, gain_key = [
        gain_rows[:, 4 * piece + i * head_piece : 4 * piece + (i + 1) * head_piece].reshape(-1)
        for i in range(2)
    ]
    width = key_weight.shape[1]
    both_full = gather_rows(jnp.concatenate([key_weight, value_weight], axis=1))
    key_full, value_full = both_full[:, :width], both_full[:, width:]
    query_full = gather_rows(query_weight)
    output_full = gather_rows(output_weight)
    gate_full = gather_rows(gate_weight)
    up_full = gather_rows(up_weight)
    down_full = gather_rows(down_weight)
    gain_in = gain_in.astype(jnp.float32)
    gain_mix = gain_mix.astype(jnp.float32)
    gain_feed = gain_feed.astype(jnp.float32)
    gain_final = gain_final.astype(jnp.float32)
    gain_query = gain_query.astype(jnp.float32)
    gain_key = gain_key.astype(jnp.float32)
    head_dim = gain_query.shape[0]
    heads = query_full.shape[1] // head_dim
    query_rows = tokens_dev * heads
    groups = lax.axis_size("ctx")
    block_rows = block_group(tokens_dev, groups)
    stream = hidden_in[0].astype(jnp.float32)
    places = positions[0]
    my_index = lax.axis_index("ctx")
    first_row = my_index * tokens_dev
    token_index = first_row + jnp.arange(tokens_dev, dtype=jnp.int32)
    token_edge = token_index - places
    row_index = jnp.repeat(token_index, heads)
    row_edge = jnp.repeat(token_edge, heads)
    last_row = first_row + tokens_dev - 1
    lowest = jnp.min(token_edge)
    cosine_table, sine_table = rotary_tables(places, head_dim)
    query_scale = head_dim ** (-0.5)
    normed_value, pull_in = jax.vjp(rms_norm, stream, gain_in)
    normed_in = normed_value.astype(jnp.bfloat16)
    query_raw = matmul_plain(normed_in, query_full).reshape(tokens_dev, heads, head_dim)
    key_raw = matmul_plain(normed_in, key_full)
    value_raw = matmul_plain(normed_in, value_full)

    def query_piece(raw, gain):
        return (
            rotate(rms_norm(raw, gain), cosine_table[:, None, :], sine_table[:, None, :])
            * query_scale
        )

    def key_piece(raw, gain):
        return rotate(rms_norm(raw, gain), cosine_table, sine_table)

    query_value, pull_query = jax.vjp(query_piece, query_raw, gain_query)
    key_value, pull_key = jax.vjp(key_piece, key_raw, gain_key)
    queries = query_value.astype(jnp.bfloat16).reshape(query_rows, head_dim)
    keys = key_value.astype(jnp.bfloat16)
    values = value_raw.astype(jnp.bfloat16)
    initial = (
        jnp.full((query_rows,), masked_score, jnp.float32),
        jnp.zeros((query_rows,), jnp.float32),
        jnp.zeros((query_rows, head_dim), jnp.float32),
    )
    start = jnp.int32(0)
    both_block = lax.all_gather(
        jnp.concatenate([keys, values], axis=1), "ctx", axis=0, tiled=True
    )
    key_block, value_block = both_block[:, :head_dim], both_block[:, head_dim:]
    count = key_block.shape[0]

    def forward_update(state):
        running_max, running_sum, weighted = state
        allowed = visible(row_index, row_edge, start, count)
        scores = jnp.where(allowed, matmul_against(queries, key_block), masked_score)
        new_max = jnp.maximum(running_max, jnp.max(scores, axis=1))
        expo = jnp.where(allowed, jnp.exp(scores - new_max[:, None]), 0.0)
        return (
            new_max,
            jnp.sum(expo, axis=1),
            matmul_plain(expo.astype(jnp.bfloat16), value_block),
        )

    live = (start <= last_row) & (start + count > lowest)
    running_max, running_sum, weighted = lax.cond(
        live, forward_update, lambda state: state, initial
    )
    attended = weighted / running_sum[:, None]
    log_total = running_max + jnp.log(running_sum)
    mixed = attended.reshape(tokens_dev, heads * head_dim).astype(jnp.bfloat16)
    projected = matmul_plain(mixed, output_full)
    branch, pull_mix = jax.vjp(rms_norm, projected, gain_mix)
    after_mix = stream + branch
    feed_value, pull_feed = jax.vjp(rms_norm, after_mix, gain_feed)
    normed_feed = feed_value.astype(jnp.bfloat16)
    gate_value = matmul_plain(normed_feed, gate_full)
    up_value = matmul_plain(normed_feed, up_full)
    activated_value, pull_gated = jax.vjp(gated, gate_value, up_value)
    activated = activated_value.astype(jnp.bfloat16)
    down_value = matmul_plain(activated, down_full)
    final_value, pull_final = jax.vjp(rms_norm, down_value, gain_final)
    output = after_mix + final_value
    cotangent = out_grad[0].astype(jnp.float32)
    d_down, d_gain_final = pull_final(cotangent)
    d_down = d_down.astype(jnp.bfloat16)
    grad_down = matmul_outer(activated, d_down)
    d_gate, d_up = pull_gated(matmul_against(d_down, down_full))
    d_gate = d_gate.astype(jnp.bfloat16)
    d_up = d_up.astype(jnp.bfloat16)
    grad_gate = matmul_outer(normed_feed, d_gate)
    grad_up = matmul_outer(normed_feed, d_up)
    d_feed_stream, d_gain_feed = pull_feed(
        matmul_against(d_gate, gate_full) + matmul_against(d_up, up_full)
    )
    d_after_mix = cotangent + d_feed_stream
    d_projected, d_gain_mix = pull_mix(d_after_mix)
    d_projected = d_projected.astype(jnp.bfloat16)
    grad_output = matmul_outer(mixed, d_projected)
    d_mixed = (
        matmul_against(d_projected, output_full).astype(jnp.bfloat16).reshape(query_rows, head_dim)
    )
    row_delta = jnp.sum(d_mixed.astype(jnp.float32) * attended, axis=1)

    def block_grads(query_grads, key_block, value_block, start):
        count = key_block.shape[0]
        allowed = visible(row_index, row_edge, start, count)
        probs = jnp.where(
            allowed, jnp.exp(matmul_against(queries, key_block) - log_total[:, None]), 0.0
        )
        value_grads = matmul_outer(probs.astype(jnp.bfloat16), d_mixed)
        prob_grads = matmul_against(d_mixed, value_block)
        score_grads = (probs * (prob_grads - row_delta[:, None])).astype(jnp.bfloat16)
        query_grads = query_grads + matmul_plain(score_grads, key_block)
        key_grads = matmul_outer(score_grads, queries)
        return (query_grads, jnp.concatenate([key_grads, value_grads], axis=1))

    def backward_block(carry, piece, start):
        key_block, value_block = piece
        count = key_block.shape[0]

        def backward_update(state):
            query_grads, buffer = state
            query_grads, both_grads = block_grads(query_grads, key_block, value_block, start)
            buffer = lax.dynamic_update_slice_in_dim(buffer, both_grads, start, 0)
            return (query_grads, buffer)

        live = (start <= last_row) & (start + count > lowest)
        return lax.cond(live, backward_update, lambda state: state, carry)

    back_keys, back_values = key_block, value_block
    query_start = jnp.zeros((query_rows, head_dim), jnp.float32)
    back_initial = (query_start, jnp.zeros((back_keys.shape[0], 2 * head_dim), jnp.float32))
    query_grads, buffer = sweep(backward_block, back_initial, back_keys, back_values, block_rows)
    kv_grads = lax.psum_scatter(
        buffer.astype(jnp.bfloat16), "ctx", scatter_dimension=0, tiled=True
    ).astype(jnp.float32)
    d_query_raw, d_gain_query = pull_query(query_grads.reshape(tokens_dev, heads, head_dim))
    d_key_raw, d_gain_key = pull_key(kv_grads[:, :head_dim])
    d_query_raw = d_query_raw.reshape(tokens_dev, heads * head_dim).astype(jnp.bfloat16)
    d_key_raw = d_key_raw.astype(jnp.bfloat16)
    d_value_raw = kv_grads[:, head_dim:].astype(jnp.bfloat16)
    grad_query = matmul_outer(normed_in, d_query_raw)
    grad_key = matmul_outer(normed_in, d_key_raw)
    grad_value = matmul_outer(normed_in, d_value_raw)
    d_normed = (
        matmul_against(d_query_raw, query_full)
        + matmul_against(d_key_raw, key_full)
        + matmul_against(d_value_raw, value_full)
    )
    d_in_stream, d_gain_in = pull_in(d_normed)
    grad_input = d_after_mix + d_in_stream
    gain_sums = lax.psum(
        jnp.concatenate(
            [d_gain_in, d_gain_mix, d_gain_feed, d_gain_final, d_gain_query, d_gain_key]
        ),
        ("ctx", "fsdp"),
    )
    me = lax.axis_index("fsdp")
    gain_shards = []
    place = 0
    for size in (model, model, model, model, head_dim, head_dim):
        gain_shards.append(
            lax.dynamic_slice_in_dim(gain_sums, place + me * (size // 4), size // 4, 0)
        )
        place += size
    both_sum = reduce_weight(jnp.concatenate([grad_key, grad_value], axis=1), 1)
    return (
        output.astype(jnp.bfloat16)[None],
        grad_input[None],
        reduce_weight(grad_query, 1),
        both_sum[:, :width],
        both_sum[:, width:],
        reduce_weight(grad_output, 0),
        reduce_weight(grad_gate, 1),
        reduce_weight(grad_up, 1),
        reduce_weight(grad_down, 0),
        *gain_shards,
    )


def solution(mesh):
    return jax.shard_map(
        on_device,
        mesh=mesh,
        in_specs=(
            P("fsdp", "ctx", None),
            P("fsdp", "ctx"),
            P("fsdp", None),
            P("fsdp", None),
            P("fsdp", None),
            P("fsdp", None),
            P("fsdp", None),
            P("fsdp", None),
            P("fsdp", None),
            P("fsdp"),
            P("fsdp"),
            P("fsdp"),
            P("fsdp"),
            P("fsdp"),
            P("fsdp"),
            P("fsdp", "ctx", None),
        ),
        out_specs=(
            P("fsdp", "ctx", None),
            P("fsdp", "ctx", None),
            P("fsdp", None),
            P("fsdp", None),
            P("fsdp", None),
            P("fsdp", None),
            P("fsdp", None),
            P("fsdp", None),
            P("fsdp", None),
            P("fsdp"),
            P("fsdp"),
            P("fsdp"),
            P("fsdp"),
            P("fsdp"),
            P("fsdp"),
        ),
        check_vma=False,
    )
```

```python
import jax
import jax.numpy as jnp
from jax import lax
from jax.experimental import pallas as pl
from jax.experimental.pallas import tpu as pltpu
from jax.sharding import PartitionSpec as P

eps = 1e-06
rope_base = 1000000.0
lanes = 128
order = (0, 2, 1, 3)
vmem_bytes = 48 * 1024 * 1024
f32 = jnp.float32
bf16 = jnp.bfloat16

ANY = pl.BlockSpec(memory_space=pl.ANY)
SMEM = pl.BlockSpec(memory_space=pltpu.SMEM)
VMEM = pl.BlockSpec(memory_space=pltpu.VMEM)


def call(kernel, inputs, specs, outs, scratch=(), flops=0, aliases=None, name=None):
    moved = sum(v.size * v.dtype.itemsize for v in inputs)
    return pl.pallas_call(
        kernel,
        out_shape=tuple(jax.ShapeDtypeStruct(s, d) for s, d in outs),
        in_specs=list(specs),
        out_specs=tuple(VMEM for _ in outs),
        scratch_shapes=list(scratch),
        input_output_aliases=aliases or {},
        compiler_params=pltpu.CompilerParams(vmem_limit_bytes=vmem_bytes),
        cost_estimate=pl.CostEstimate(
            flops=int(flops), bytes_accessed=int(moved), transcendentals=0
        ),
        name=name,
    )(*inputs)


def nn(left, right):
    return lax.dot_general(left, right, (((1,), (0,)), ((), ())), preferred_element_type=f32)


def nt(left, right):
    return lax.dot_general(left, right, (((1,), (1,)), ((), ())), preferred_element_type=f32)


def tn(left, right):
    return lax.dot_general(left, right, (((0,), (0,)), ((), ())), preferred_element_type=f32)


def unit(value):
    inverse = lax.rsqrt(jnp.mean(value * value, axis=-1, keepdims=True) + eps)
    return value * inverse, inverse


def unit_back(hat, inverse, grad_hat):
    return inverse * (grad_hat - hat * jnp.mean(grad_hat * hat, axis=-1, keepdims=True))


def spin(value, cosine, sine):
    half = value.shape[-1] // 2
    first, second = value[:, :half], value[:, half:]
    return jnp.concatenate(
        [first * cosine - second * sine, second * cosine + first * sine], axis=-1
    )


def place(index, blocks, full, sems):
    rows = blocks[0].shape[0]
    copies = []
    for step, block in enumerate(blocks):
        start = pl.multiple_of((index ^ step) * rows, 16)
        copy = pltpu.make_async_copy(block, full.at[pl.ds(start, rows)], sems.at[step])
        copy.start()
        copies.append(copy)
    return copies


def finish(copies):
    for copy in copies:
        copy.wait()


def kv_kernel(
    info, hidden, gain_in, gain_key, cosine, sine,
    k0, k1, k2, k3, v0, v1, v2, v3,
    normed_out, key_raw_out, kv_out,
    key_full, value_full, sems,
):
    index = info[0]
    key_copies = place(index, (k0, k1, k2, k3), key_full, sems.at[0])
    value_copies = place(index, (v0, v1, v2, v3), value_full, sems.at[1])
    hat, _ = unit(hidden[...].astype(f32))
    normed = (hat * (1.0 + gain_in[...])).astype(bf16)
    normed_out[...] = normed
    width = key_full.shape[1]
    finish(key_copies)
    raw = nn(normed, key_full[...])
    key_raw_out[...] = raw
    hat, _ = unit(raw)
    kv_out[:, :width] = spin(hat * (1.0 + gain_key[...]), cosine[...], sine[...]).astype(bf16)
    finish(value_copies)
    kv_out[:, width:] = nn(normed, value_full[...]).astype(bf16)


def query_kernel(
    info, normed, gain_query, cosine, sine, q0, q1, q2, q3,
    raw_out, query_out, query_full, sems,
):
    finish(place(info[0], (q0, q1, q2, q3), query_full, sems))
    head_dim = gain_query.shape[1]
    for start in range(0, query_full.shape[1], head_dim):
        part = slice(start, start + head_dim)
        raw = nn(normed[...], query_full[:, part])
        raw_out[:, part] = raw
        hat, _ = unit(raw)
        turned = spin(hat * (1.0 + gain_query[...]), cosine[...], sine[...])
        query_out[:, part] = (turned * head_dim ** (-0.5)).astype(bf16)


def attend_kernel(first, count, info, queries, places, *refs):
    chunks = refs[:count]
    refs = refs[count:]
    if not first:
        weighted_in, total_in = refs[:2]
        refs = refs[2:]
    weighted, total = refs
    tokens = queries.shape[0]
    head_dim = chunks[0].shape[1] // 2
    heads = queries.shape[1] // head_dim
    if first:
        weighted[...] = jnp.zeros_like(weighted)
        total[...] = jnp.zeros_like(total)
    else:
        weighted[...] = weighted_in[...]
        total[...] = total_in[...]
    first_row = info[1]
    for number, chunk in enumerate(chunks):
        base = info[2 + number]

        @pl.loop(0, chunk.shape[0] // tokens)
        def _(step):
            start = base + step * tokens

            @pl.when((start >= 0) & (start <= first_row))
            def _():
                local = pl.ds(pl.multiple_of(step * tokens, tokens), tokens)
                row = first_row + lax.broadcasted_iota(jnp.int32, (tokens, tokens), 0)
                col = start + lax.broadcasted_iota(jnp.int32, (tokens, tokens), 1)
                allowed = (col <= row) & (col >= row - places[...])
                keys = chunk[local, :head_dim]
                values = chunk[local, head_dim:]
                for head in range(heads):
                    part = slice(head * head_dim, (head + 1) * head_dim)
                    scores = nt(queries[:, part], keys)
                    expo = jnp.where(allowed, jnp.exp(scores), 0.0)
                    spot = slice(head * lanes, (head + 1) * lanes)
                    total[:, spot] += jnp.sum(expo, axis=1, keepdims=True)
                    weighted[:, part] += nn(expo.astype(bf16), values)


def mix_kernel(
    info, weighted, total, hidden, gain_mix, gain_feed,
    o0, o1, o2, o3, g0, g1, g2, g3, u0, u1, u2, u3,
    attended_out, mixed_out, projected_out, after_out, normed_out, gate_out, up_out, act_out,
    output_full, gate_full, up_full, sems,
):
    index = info[0]
    output_copies = place(index, (o0, o1, o2, o3), output_full, sems.at[0])
    gate_copies = place(index, (g0, g1, g2, g3), gate_full, sems.at[1])
    up_copies = place(index, (u0, u1, u2, u3), up_full, sems.at[2])
    heads = total.shape[1] // lanes
    head_dim = weighted.shape[1] // heads
    for head in range(heads):
        part = slice(head * head_dim, (head + 1) * head_dim)
        ratio = weighted[:, part] / total[:, head * lanes : head * lanes + 1]
        attended_out[:, part] = ratio
        mixed_out[:, part] = ratio.astype(bf16)
    finish(output_copies)
    projected = nn(mixed_out[...], output_full[...])
    projected_out[...] = projected
    hat, _ = unit(projected)
    after = hidden[...].astype(f32) + hat * (1.0 + gain_mix[...])
    after_out[...] = after
    hat, _ = unit(after)
    normed_out[...] = (hat * (1.0 + gain_feed[...])).astype(bf16)
    finish(gate_copies)
    finish(up_copies)
    step_width = 512

    @pl.loop(0, gate_full.shape[1] // step_width)
    def _(step):
        part = pl.ds(pl.multiple_of(step * step_width, step_width), step_width)
        gate = nn(normed_out[...], gate_full[:, part])
        up = nn(normed_out[...], up_full[:, part])
        gate_out[:, part] = gate
        up_out[:, part] = up
        inner = 0.7978845608028654 * (gate + 0.044715 * gate * gate * gate)
        act_out[:, part] = (0.5 * gate * (1.0 + jnp.tanh(inner)) * up).astype(bf16)


def store_columns(keep, send, slot, base, rows, block):
    target = keep if slot < 2 else send
    for number in range(block.shape[1] // lanes):
        target[slot % 2, base + number * rows : base + (number + 1) * rows, :] = block[
            :, number * lanes : (number + 1) * lanes
        ].astype(bf16)


def feed_kernel(
    info, act, gate, up, normed, after, cotangent, gain_final,
    d0, d1, d2, d3,
    hidden_out, d_gate, d_up, gain_grad, keep, send,
    down_full, d_down, turned, sems,
):
    index = info[0]
    finish(place(index, (d0, d1, d2, d3), down_full, sems))
    down = nn(act[...], down_full[...])
    hat, inverse = unit(down)
    scale = 1.0 + gain_final[...]
    hidden_out[...] = (after[...] + hat * scale).astype(bf16)
    grad = cotangent[...].astype(f32)
    gain_grad[...] = jnp.sum(grad * hat, axis=0, keepdims=True)
    d_down[...] = unit_back(hat, inverse, grad * scale).astype(bf16)
    turned[...] = normed[...].astype(f32).T.astype(bf16)
    step_width = 512

    @pl.loop(0, down_full.shape[0] // step_width)
    def _(step):
        part = pl.ds(pl.multiple_of(step * step_width, step_width), step_width)
        d_act = nt(d_down[...], down_full[part, :])
        x = gate[:, part]
        curve = jnp.tanh(0.7978845608028654 * (x + 0.044715 * x * x * x))
        slope = 0.5 * (1.0 + curve) + 0.5 * x * (1.0 - curve * curve) * (
            0.7978845608028654 * (1.0 + 3.0 * 0.044715 * x * x)
        )
        d_gate[:, part] = (d_act * up[:, part] * slope).astype(bf16)
        d_up[:, part] = (d_act * (0.5 * x * (1.0 + curve))).astype(bf16)

    model = normed.shape[1]
    rows = model // 4
    wide = gate.shape[1]
    down_rows = wide // 4
    part_rows = (wide // lanes) * rows
    for slot, step in enumerate(order):
        target = keep if slot < 2 else send
        owner = index ^ step
        lhs = turned[pl.ds(pl.multiple_of(owner * rows, 16), rows), :]
        for base, source in ((0, d_gate), (part_rows, d_up)):

            @pl.loop(0, wide // step_width)
            def _(move):
                part = pl.ds(pl.multiple_of(move * step_width, step_width), step_width)
                block = nn(lhs, source[:, part]).astype(bf16)
                for number in range(step_width // lanes):
                    begin = base + (move * (step_width // lanes) + number) * rows
                    target[slot % 2, pl.ds(pl.multiple_of(begin, 16), rows), :] = block[
                        :, number * lanes : (number + 1) * lanes
                    ]

        left = act[:, pl.ds(pl.multiple_of(owner * down_rows, lanes), down_rows)]
        store_columns(keep, send, slot, 2 * part_rows, down_rows, tn(left, d_down[...]))


def feed_back_kernel(
    info, d_gate, d_up, after, projected, attended, total, cotangent, gain_mix, gain_feed,
    g0, g1, g2, g3, u0, u1, u2, u3, o0, o1, o2, o3,
    d_after_out, d_projected_out, d_mixed_out, rows_out, feed_grad, mix_grad,
    gate_full, up_full, output_full, total_grad, sems,
):
    index = info[0]
    gate_copies = place(index, (g0, g1, g2, g3), gate_full, sems.at[0])
    up_copies = place(index, (u0, u1, u2, u3), up_full, sems.at[1])
    output_copies = place(index, (o0, o1, o2, o3), output_full, sems.at[2])
    finish(gate_copies)
    total_grad[...] = nt(d_gate[...], gate_full[...])
    finish(up_copies)
    grad = total_grad[...] + nt(d_up[...], up_full[...])
    hat, inverse = unit(after[...])
    feed_grad[...] = jnp.sum(grad * hat, axis=0, keepdims=True)
    d_after = cotangent[...].astype(f32) + unit_back(hat, inverse, grad * (1.0 + gain_feed[...]))
    d_after_out[...] = d_after
    hat, inverse = unit(projected[...])
    mix_grad[...] = jnp.sum(d_after * hat, axis=0, keepdims=True)
    d_projected = unit_back(hat, inverse, d_after * (1.0 + gain_mix[...])).astype(bf16)
    d_projected_out[...] = d_projected
    finish(output_copies)
    d_mixed = nt(d_projected, output_full[...]).astype(bf16)
    d_mixed_out[...] = d_mixed
    heads = total.shape[1] // lanes
    head_dim = attended.shape[1] // heads
    tokens = attended.shape[0]
    lane = lax.broadcasted_iota(jnp.int32, (tokens, lanes), 1)
    table = jnp.zeros((tokens, lanes), f32)
    for head in range(heads):
        part = slice(head * head_dim, (head + 1) * head_dim)
        delta = jnp.sum(d_mixed[:, part].astype(f32) * attended[:, part], axis=1, keepdims=True)
        table = jnp.where(lane == head, delta, table)
        share = 1.0 / total[:, head * lanes : (head + 1) * lanes]
        table = jnp.where(lane == heads + head, share, table)
    rows_out[...] = table.T[: rows_out.shape[0], :]


def attend_back_kernel(first, count, info, queries, d_mixed, table, places, *refs):
    chunks = refs[:count]
    refs = refs[count:]
    if not first:
        query_in = refs[0]
        refs = refs[1:]
    query_grads = refs[0]
    chunk_grads = refs[1 : 1 + count]
    key_sum, value_sum = refs[1 + count :]
    tokens = queries.shape[0]
    head_dim = chunks[0].shape[1] // 2
    heads = queries.shape[1] // head_dim
    if first:
        query_grads[...] = jnp.zeros_like(query_grads)
    else:
        query_grads[...] = query_in[...]
    first_row = info[1]
    for number, (chunk, chunk_grad) in enumerate(zip(chunks, chunk_grads)):
        base = info[2 + number]
        chunk_grad[...] = jnp.zeros_like(chunk_grad)

        @pl.loop(0, chunk.shape[0] // tokens)
        def _(step):
            start = base + step * tokens

            @pl.when((start >= 0) & (start <= first_row))
            def _():
                local = pl.ds(pl.multiple_of(step * tokens, tokens), tokens)
                row = first_row + lax.broadcasted_iota(jnp.int32, (tokens, tokens), 1)
                col = start + lax.broadcasted_iota(jnp.int32, (tokens, tokens), 0)
                allowed = (col <= row) & (col >= row - places[...])
                keys = chunk[local, :head_dim]
                values = chunk[local, head_dim:]
                for head in range(heads):
                    part = slice(head * head_dim, (head + 1) * head_dim)
                    query = queries[:, part]
                    grad = d_mixed[:, part]
                    expo = jnp.where(allowed, jnp.exp(nt(keys, query)), 0.0)
                    probs = expo * table[heads + head : heads + head + 1, :]
                    back = nt(values, grad) - table[head : head + 1, :]
                    d_scores = (probs * back).astype(bf16)
                    d_value = nn(probs.astype(bf16), grad)
                    d_key = nn(d_scores, query)
                    if head == 0:
                        key_sum[...] = d_key
                        value_sum[...] = d_value
                    else:
                        key_sum[...] += d_key
                        value_sum[...] += d_value
                    query_grads[:, part] += tn(d_scores, keys)
                chunk_grad[local, :head_dim] = key_sum[...].astype(bf16)
                chunk_grad[local, head_dim:] = value_sum[...].astype(bf16)


def unspin(value, cosine, sine):
    half = value.shape[-1] // 2
    first, second = value[:, :half], value[:, half:]
    return jnp.concatenate(
        [first * cosine + second * sine, second * cosine - first * sine], axis=-1
    )


def query_back_kernel(
    info, query_grads, raw, cosine, sine, gain_query, normed, mixed, d_projected,
    q0, q1, q2, q3,
    d_normed_out, gain_grad, keep, send,
    query_full, d_raw, turned, sems,
):
    index = info[0]
    copies = place(index, (q0, q1, q2, q3), query_full, sems)
    head_dim = gain_query.shape[1]
    wide = raw.shape[1]
    scale = 1.0 + gain_query[...]
    gain_sum = jnp.zeros((1, head_dim), f32)
    for start in range(0, wide, head_dim):
        part = slice(start, start + head_dim)
        hat, inverse = unit(raw[:, part])
        grad = unspin(query_grads[:, part] * head_dim ** (-0.5), cosine[...], sine[...])
        gain_sum += jnp.sum(grad * hat, axis=0, keepdims=True)
        d_raw[:, part] = unit_back(hat, inverse, grad * scale).astype(bf16)
    gain_grad[...] = gain_sum
    turned[...] = normed[...].astype(f32).T.astype(bf16)
    rows = normed.shape[1] // 4
    mixed_rows = mixed.shape[1] // 4
    for slot, step in enumerate(order):
        owner = index ^ step
        lhs = turned[pl.ds(pl.multiple_of(owner * rows, 16), rows), :]
        store_columns(keep, send, slot, 0, rows, nn(lhs, d_raw[...]))
        left = mixed[:, pl.ds(pl.multiple_of(owner * mixed_rows, lanes), mixed_rows)]
        store_columns(
            keep, send, slot, (wide // lanes) * rows, mixed_rows, tn(left, d_projected[...])
        )
    finish(copies)
    d_normed_out[...] = nt(d_raw[...], query_full[...])


def key_back_kernel(
    count, info, cosine, sine, gain_key, gain_in, raw, normed, hidden, d_after, d_normed_query,
    k0, k1, k2, k3, v0, v1, v2, v3, *refs,
):
    parts = refs[:count]
    (
        input_grad, key_gain_grad, in_gain_grad, keep, send,
        key_full, value_full, d_both, turned, sems,
    ) = refs[count:]
    index = info[0]
    key_copies = place(index, (k0, k1, k2, k3), key_full, sems.at[0])
    value_copies = place(index, (v0, v1, v2, v3), value_full, sems.at[1])
    width = raw.shape[1]
    both = parts[0][...].astype(f32)
    for piece in parts[1:]:
        both = both + piece[...].astype(f32)
    hat, inverse = unit(raw[...])
    grad = unspin(both[:, :width], cosine[...], sine[...])
    key_gain_grad[...] = jnp.sum(grad * hat, axis=0, keepdims=True)
    d_both[:, :width] = unit_back(hat, inverse, grad * (1.0 + gain_key[...])).astype(bf16)
    d_both[:, width:] = both[:, width:].astype(bf16)
    turned[...] = normed[...].astype(f32).T.astype(bf16)
    rows = normed.shape[1] // 4
    for slot, step in enumerate(order):
        owner = index ^ step
        lhs = turned[pl.ds(pl.multiple_of(owner * rows, 16), rows), :]
        store_columns(keep, send, slot, 0, rows, nn(lhs, d_both[...]))
    finish(key_copies)
    finish(value_copies)
    d_normed = (
        d_normed_query[...]
        + nt(d_both[:, :width], key_full[...])
        + nt(d_both[:, width:], value_full[...])
    )
    hat, inverse = unit(hidden[...].astype(f32))
    in_gain_grad[...] = jnp.sum(d_normed * hat, axis=0, keepdims=True)
    input_grad[...] = d_after[...] + unit_back(hat, inverse, d_normed * (1.0 + gain_in[...]))


def unpack_kernel(widths, rows_of, pack, *outs):
    base = 0
    for out, width, rows in zip(outs, widths, rows_of):
        for number in range(width // lanes):
            out[:, number * lanes : (number + 1) * lanes] = pack[
                base : base + rows, :
            ].astype(f32)
            base += rows


def flip(value, axis, bit):
    size = lax.axis_size(axis)
    return lax.ppermute(value, axis, [(i, i ^ bit) for i in range(size)])


def gather_blocks(shard):
    far = flip(shard, "fsdp", 2)
    near = flip(shard, "fsdp", 1)
    return shard, near, far, flip(far, "fsdp", 1)


def add_low(*values):
    total = values[0].astype(f32)
    for value in values[1:]:
        total = total + value.astype(f32)
    return total.astype(bf16)


def take_half(value, which):
    half = value.shape[0] // 2
    return lax.dynamic_slice_in_dim(value, which * half, half, 0)


def reduce_fsdp(keep, send):
    near = flip(send, "fsdp", 1)
    far = flip(add_low(keep[1], near[1]), "fsdp", 2)
    return add_low(keep[0], near[0], far)


def reduce_ctx(value):
    me = lax.axis_index("ctx")
    size = lax.axis_size("ctx")
    bits = [1 << i for i in range(size.bit_length() - 1)]
    for bit in bits:
        mine = (me // bit) % 2
        sent = flip(take_half(value, 1 - mine), "ctx", bit)
        value = add_low(take_half(value, mine), sent)
    for bit in reversed(bits):
        mine = (me // bit) % 2
        other = flip(value, "ctx", bit)
        low = jnp.where(mine == 0, value, other)
        high = jnp.where(mine == 0, other, value)
        value = jnp.concatenate([low, high], axis=0)
    return value


def on_device(
    hidden_in, positions, query_weight, key_weight, value_weight, output_weight, gate_weight,
    up_weight, down_weight, input_gain, mixer_gain, feed_gain, final_gain, query_gain, key_gain,
    out_grad,
):
    tokens = hidden_in.shape[1]
    model = hidden_in.shape[2]
    rows = key_weight.shape[0]
    head_dim = key_weight.shape[1]
    wide = query_weight.shape[1]
    heads = wide // head_dim
    feed = gate_weight.shape[1]
    mixed_rows = output_weight.shape[0]
    down_rows = down_weight.shape[0]
    me = lax.axis_index("fsdp")
    ctx = lax.axis_index("ctx")
    groups = lax.axis_size("ctx")
    first_row = ctx * tokens

    gain_pack = jnp.concatenate(
        [input_gain, mixer_gain, feed_gain, final_gain, query_gain, key_gain]
    )[None]
    gain_pack = jnp.broadcast_to(gain_pack, (16, gain_pack.shape[1]))
    gain_blocks = gather_blocks(gain_pack)
    key_blocks = gather_blocks(key_weight)
    value_blocks = gather_blocks(value_weight)
    query_blocks = gather_blocks(query_weight)
    output_blocks = gather_blocks(output_weight)
    gate_blocks = gather_blocks(gate_weight)
    up_blocks = gather_blocks(up_weight)
    down_blocks = gather_blocks(down_weight)

    gain_rows = jnp.zeros((4, gain_pack.shape[1]), bf16)
    for step, block in enumerate(gain_blocks):
        gain_rows = lax.dynamic_update_slice_in_dim(gain_rows, block[:1], me ^ step, 0)
    gain_rows = gain_rows.astype(f32)
    gain_in, gain_mix, gain_feed, gain_final = [
        gain_rows[:, i * rows : (i + 1) * rows].reshape(1, -1) for i in range(4)
    ]
    head_piece = query_gain.shape[0]
    gain_query, gain_key = [
        gain_rows[:, 4 * rows + i * head_piece : 4 * rows + (i + 1) * head_piece].reshape(1, -1)
        for i in range(2)
    ]

    hidden = hidden_in[0]
    cotangent = out_grad[0]
    places = positions[0]
    place_col = places[:, None]
    place_row = places[None, :]
    half = head_dim // 2
    freqs = rope_base ** (-(jnp.arange(half, dtype=f32) * 2.0) / head_dim)
    angles = places.astype(f32)[:, None] * freqs[None, :]
    cosine, sine = jnp.cos(angles), jnp.sin(angles)

    def facts(*starts):
        return jnp.stack([me, first_row, *starts]).astype(jnp.int32)

    info = facts()
    sem = pltpu.SemaphoreType.DMA
    token_flops = 2 * tokens * model

    normed, key_raw, kv = call(
        kv_kernel,
        (info, hidden, gain_in, gain_key, cosine, sine, *key_blocks, *value_blocks),
        [SMEM] + [VMEM] * 5 + [ANY] * 8,
        [((tokens, model), bf16), ((tokens, head_dim), f32), ((tokens, 2 * head_dim), bf16)],
        [
            pltpu.VMEM((model, head_dim), bf16),
            pltpu.VMEM((model, head_dim), bf16),
            sem((2, 4)),
        ],
        flops=token_flops * 2 * head_dim,
        name="key_value",
    )
    query_raw, queries = call(
        query_kernel,
        (info, normed, gain_query, cosine, sine, *query_blocks),
        [SMEM] + [VMEM] * 4 + [ANY] * 4,
        [((tokens, wide), f32), ((tokens, wide), bf16)],
        [pltpu.VMEM((model, wide), bf16), sem((4,))],
        flops=token_flops * wide,
        name="query",
    )

    ring = groups == 8
    if ring:
        side = ctx % 2
        stage = ctx // 2
        sources = []
        for shift in range(groups // 2):
            if shift == 0:
                mine = kv
            else:
                mine = lax.ppermute(
                    kv, "ctx", [(i, i + 2 * shift) for i in range(groups - 2 * shift)]
                )
            other = flip(mine, "ctx", 1)
            base = (stage - shift) * 2
            sources.append(
                ((mine, other), ((base + side) * tokens, (base + 1 - side) * tokens))
            )
    else:
        sources = [((lax.all_gather(kv, "ctx", axis=0, tiled=True),), (jnp.int32(0),))]

    state = ()
    chunk_flops = 4 * tokens * tokens * wide
    for number, (arrays, starts) in enumerate(sources):
        first = number == 0
        count = len(arrays)

        def attend(*args, first=first, count=count):
            attend_kernel(first, count, *args)

        state = call(
            attend,
            (facts(*starts), queries, place_col, *arrays, *state),
            [SMEM] + [VMEM] * (2 + count + len(state)),
            [((tokens, wide), f32), ((tokens, heads * lanes), f32)],
            flops=chunk_flops * 2,
            name="attend",
        )
    weighted, total = state

    attended, mixed, projected, after, normed_feed, gate_value, up_value, activated = call(
        mix_kernel,
        (
            info, weighted, total, hidden, gain_mix, gain_feed,
            *output_blocks, *gate_blocks, *up_blocks,
        ),
        [SMEM] + [VMEM] * 5 + [ANY] * 12,
        [
            ((tokens, wide), f32),
            ((tokens, wide), bf16),
            ((tokens, model), f32),
            ((tokens, model), f32),
            ((tokens, model), bf16),
            ((tokens, feed), f32),
            ((tokens, feed), f32),
            ((tokens, feed), bf16),
        ],
        [
            pltpu.VMEM((wide, model), bf16),
            pltpu.VMEM((model, feed), bf16),
            pltpu.VMEM((model, feed), bf16),
            sem((3, 4)),
        ],
        flops=token_flops * (wide + 2 * feed),
        name="mix",
    )
    feed_rows = 2 * (feed // lanes) * rows + (model // lanes) * down_rows
    hidden_out, d_gate, d_up, grad_final, feed_keep, feed_send = call(
        feed_kernel,
        (
            info, activated, gate_value, up_value, normed_feed, after, cotangent, gain_final,
            *down_blocks,
        ),
        [SMEM] + [VMEM] * 7 + [ANY] * 4,
        [
            ((tokens, model), bf16),
            ((tokens, feed), bf16),
            ((tokens, feed), bf16),
            ((1, model), f32),
            ((2, feed_rows, lanes), bf16),
            ((2, feed_rows, lanes), bf16),
        ],
        [
            pltpu.VMEM((feed, model), bf16),
            pltpu.VMEM((tokens, model), bf16),
            pltpu.VMEM((model, tokens), bf16),
            sem((4,)),
        ],
        flops=token_flops * 5 * feed,
        name="feed",
    )
    feed_shard = reduce_fsdp(feed_keep, feed_send)

    d_after, d_projected, d_mixed, table, grad_feed_gain, grad_mix_gain = call(
        feed_back_kernel,
        (
            info, d_gate, d_up, after, projected, attended, total, cotangent, gain_mix, gain_feed,
            *gate_blocks, *up_blocks, *output_blocks,
        ),
        [SMEM] + [VMEM] * 9 + [ANY] * 12,
        [
            ((tokens, model), f32),
            ((tokens, model), bf16),
            ((tokens, wide), bf16),
            ((2 * heads, tokens), f32),
            ((1, model), f32),
            ((1, model), f32),
        ],
        [
            pltpu.VMEM((model, feed), bf16),
            pltpu.VMEM((model, feed), bf16),
            pltpu.VMEM((wide, model), bf16),
            pltpu.VMEM((tokens, model), f32),
            sem((3, 4)),
        ],
        flops=token_flops * (2 * feed + wide),
        name="feed_back",
    )

    query_grads = ()
    arrived = []
    for number, (arrays, starts) in enumerate(reversed(sources)):
        first = number == 0
        count = len(arrays)

        def attend_back(*args, first=first, count=count):
            attend_back_kernel(first, count, *args)

        results = call(
            attend_back,
            (facts(*starts), queries, d_mixed, table, place_row, *arrays, *query_grads),
            [SMEM] + [VMEM] * (4 + count + len(query_grads)),
            [((tokens, wide), f32)] + [(a.shape, bf16) for a in arrays],
            [pltpu.VMEM((tokens, head_dim), f32), pltpu.VMEM((tokens, head_dim), f32)],
            flops=chunk_flops * 5,
            name="attend_back",
        )
        query_grads = results[:1]
        if ring:
            mine, other = results[1:]
            shift = len(sources) - 1 - number
            crossed = flip(other, "ctx", 1)
            if shift == 0:
                arrived += [mine, crossed]
            else:
                arrived.append(
                    lax.ppermute(
                        add_low(mine, crossed),
                        "ctx",
                        [(i + 2 * shift, i) for i in range(groups - 2 * shift)],
                    )
                )
        else:
            arrived.append(
                lax.psum_scatter(results[1], "ctx", scatter_dimension=0, tiled=True)
            )

    query_rows = (wide // lanes) * rows
    output_rows = (model // lanes) * mixed_rows
    d_normed_query, grad_query_gain, query_keep, query_send = call(
        query_back_kernel,
        (
            info, query_grads[0], query_raw, cosine, sine, gain_query, normed, mixed, d_projected,
            *query_blocks,
        ),
        [SMEM] + [VMEM] * 8 + [ANY] * 4,
        [
            ((tokens, model), f32),
            ((1, head_dim), f32),
            ((2, query_rows + output_rows, lanes), bf16),
            ((2, query_rows + output_rows, lanes), bf16),
        ],
        [
            pltpu.VMEM((model, wide), bf16),
            pltpu.VMEM((tokens, wide), bf16),
            pltpu.VMEM((model, tokens), bf16),
            sem((4,)),
        ],
        flops=token_flops * 3 * wide,
        name="query_back",
    )
    query_shard = reduce_fsdp(query_keep, query_send)

    both_rows = (2 * head_dim // lanes) * rows
    arrived_count = len(arrived)

    def key_back(*args):
        key_back_kernel(arrived_count, *args)

    grad_input, grad_key_gain, grad_in_gain, both_keep, both_send = call(
        key_back,
        (
            info, cosine, sine, gain_key, gain_in, key_raw, normed, hidden, d_after,
            d_normed_query, *key_blocks, *value_blocks, *arrived,
        ),
        [SMEM] + [VMEM] * 9 + [ANY] * 8 + [VMEM] * arrived_count,
        [
            ((tokens, model), f32),
            ((1, head_dim), f32),
            ((1, model), f32),
            ((2, both_rows, lanes), bf16),
            ((2, both_rows, lanes), bf16),
        ],
        [
            pltpu.VMEM((model, head_dim), bf16),
            pltpu.VMEM((model, head_dim), bf16),
            pltpu.VMEM((tokens, 2 * head_dim), bf16),
            pltpu.VMEM((model, tokens), bf16),
            sem((2, 4)),
        ],
        flops=token_flops * 4 * head_dim,
        name="key_back",
    )
    both_shard = reduce_fsdp(both_keep, both_send)

    gain_sums = jnp.concatenate(
        [
            grad_in_gain, grad_mix_gain, grad_feed_gain, grad_final, grad_query_gain,
            grad_key_gain,
        ],
        axis=1,
    ).reshape(-1, lanes)
    for axis in ("fsdp", "ctx"):
        bit = 1
        while bit < lax.axis_size(axis):
            gain_sums = gain_sums + flip(gain_sums, axis, bit)
            bit *= 2
    gain_sums = gain_sums.reshape(-1)
    gain_shards = []
    start = 0
    for size in (model, model, model, model, head_dim, head_dim):
        gain_shards.append(
            lax.dynamic_slice_in_dim(gain_sums, start + me * (size // 4), size // 4, 0)
        )
        start += size

    def unpack(pack, shapes):
        def kernel(*args):
            unpack_kernel([s[1] for s in shapes], [s[0] for s in shapes], *args)

        return call(kernel, (pack,), [VMEM], [(s, f32) for s in shapes], name="unpack")

    grad_gate, grad_up, grad_down = unpack(
        reduce_ctx(feed_shard), [gate_weight.shape, up_weight.shape, down_weight.shape]
    )
    grad_query, grad_output = unpack(
        reduce_ctx(query_shard), [query_weight.shape, output_weight.shape]
    )
    grad_key, grad_value = unpack(
        reduce_ctx(both_shard), [key_weight.shape, value_weight.shape]
    )
    return (
        hidden_out[None],
        grad_input[None],
        grad_query,
        grad_key,
        grad_value,
        grad_output,
        grad_gate,
        grad_up,
        grad_down,
        *gain_shards,
    )


def solution(mesh):
    token = P("fsdp", "ctx", None)
    weight = P("fsdp", None)
    gain = P("fsdp")
    return jax.shard_map(
        on_device,
        mesh=mesh,
        in_specs=(token, P("fsdp", "ctx")) + (weight,) * 7 + (gain,) * 6 + (token,),
        out_specs=(token, token) + (weight,) * 7 + (gain,) * 6,
        check_vma=False,
    )
```

```python
import jax
import jax.numpy as jnp
from jax import lax
from jax.experimental import pallas as pl
from jax.experimental.pallas import tpu as pltpu
from jax.sharding import PartitionSpec as P

eps = 1e-06
rope_base = 1000000.0
lanes = 128
order = (0, 2, 1, 3)
vmem_bytes = 48 * 1024 * 1024
f32 = jnp.float32
bf16 = jnp.bfloat16

ANY = pl.BlockSpec(memory_space=pl.ANY)
SMEM = pl.BlockSpec(memory_space=pltpu.SMEM)
VMEM = pl.BlockSpec(memory_space=pltpu.VMEM)


def tie(*values):
    return lax.optimization_barrier(values)


def call(kernel, inputs, specs, outs, scratch=(), flops=0, aliases=None, name=None):
    return pl.pallas_call(
        kernel,
        out_shape=tuple(jax.ShapeDtypeStruct(s, d) for s, d in outs),
        in_specs=list(specs),
        out_specs=tuple(VMEM for _ in outs),
        scratch_shapes=list(scratch),
        input_output_aliases=aliases or {},
        compiler_params=pltpu.CompilerParams(vmem_limit_bytes=vmem_bytes),
        cost_estimate=pl.CostEstimate(flops=1, bytes_accessed=1, transcendentals=0),
        name=name,
    )(*inputs)


def nn(left, right):
    return lax.dot_general(left, right, (((1,), (0,)), ((), ())), preferred_element_type=f32)


def nt(left, right):
    return lax.dot_general(left, right, (((1,), (1,)), ((), ())), preferred_element_type=f32)


def tn(left, right):
    return lax.dot_general(left, right, (((0,), (0,)), ((), ())), preferred_element_type=f32)


def unit(value):
    inverse = lax.rsqrt(jnp.mean(value * value, axis=-1, keepdims=True) + eps)
    return value * inverse, inverse


def unit_back(hat, inverse, grad_hat):
    return inverse * (grad_hat - hat * jnp.mean(grad_hat * hat, axis=-1, keepdims=True))


def spin(value, cosine, sine):
    half = value.shape[-1] // 2
    first, second = value[:, :half], value[:, half:]
    return jnp.concatenate(
        [first * cosine - second * sine, second * cosine + first * sine], axis=-1
    )


def place(index, pairs, full, sems, columns=None):
    rows = pairs[0].shape[0] // 2
    copies = []
    for step in range(4):
        begin = pl.multiple_of((index ^ step) * rows, 16)
        source = pairs[step % 2].at[pl.ds((step // 2) * rows, rows)]
        if columns is not None:
            source = source.at[:, pl.ds(columns, full.shape[1])]
        copy = pltpu.make_async_copy(source, full.at[pl.ds(begin, rows)], sems.at[step])
        copy.start()
        copies.append(copy)
    return copies


def finish(copies):
    for copy in copies:
        copy.wait()


def kv_kernel(
    info, hidden, gain_in, gain_key, cosine, sine,
    b0, b1,
    normed_out, key_raw_out, kv_out,
    both_full, sems,
):
    index = info[0]
    copies = place(index, (b0, b1), both_full, sems)
    hat, _ = unit(hidden[...].astype(f32))
    normed = (hat * (1.0 + gain_in[...])).astype(bf16)
    normed_out[...] = normed
    width = key_raw_out.shape[1]
    finish(copies)
    raw = nn(normed, both_full[:, :width])
    key_raw_out[...] = raw
    hat, _ = unit(raw)
    kv_out[:, :width] = spin(hat * (1.0 + gain_key[...]), cosine[...], sine[...]).astype(bf16)
    kv_out[:, width:] = nn(normed, both_full[:, width:]).astype(bf16)


def query_kernel(
    info, normed, gain_query, cosine, sine, q0, q1,
    raw_out, query_out, query_full, sems,
):
    finish(place(info[0], (q0, q1), query_full, sems))
    head_dim = gain_query.shape[1]
    for start in range(0, query_full.shape[1], head_dim):
        part = slice(start, start + head_dim)
        raw = nn(normed[...], query_full[:, part])
        raw_out[:, part] = raw
        hat, _ = unit(raw)
        turned = spin(hat * (1.0 + gain_query[...]), cosine[...], sine[...])
        query_out[:, part] = (turned * head_dim ** (-0.5)).astype(bf16)


def attend_kernel(first, count, info, queries, places, *refs):
    chunks = refs[:count]
    refs = refs[count:]
    if not first:
        weighted_in, total_in = refs[:2]
        refs = refs[2:]
    weighted, total = refs
    tokens = queries.shape[0]
    head_dim = chunks[0].shape[1] // 2
    heads = queries.shape[1] // head_dim
    if first:
        weighted[...] = jnp.zeros_like(weighted)
        total[...] = jnp.zeros_like(total)
    else:
        weighted[...] = weighted_in[...]
        total[...] = total_in[...]
    first_row = info[1]
    for number, chunk in enumerate(chunks):
        base = info[2 + number]

        @pl.loop(0, chunk.shape[0] // tokens)
        def _(step):
            start = base + step * tokens

            @pl.when((start >= 0) & (start <= first_row))
            def _():
                local = pl.ds(pl.multiple_of(step * tokens, tokens), tokens)
                row = first_row + lax.broadcasted_iota(jnp.int32, (tokens, tokens), 0)
                col = start + lax.broadcasted_iota(jnp.int32, (tokens, tokens), 1)
                allowed = (col <= row) & (col >= row - places[...])
                keys = chunk[local, :head_dim]
                values = chunk[local, head_dim:]
                for head in range(heads):
                    part = slice(head * head_dim, (head + 1) * head_dim)
                    scores = nt(queries[:, part], keys)
                    expo = jnp.where(allowed, jnp.exp(scores), 0.0)
                    spot = slice(head * lanes, (head + 1) * lanes)
                    total[:, spot] += jnp.sum(expo, axis=1, keepdims=True)
                    weighted[:, part] += nn(expo.astype(bf16), values)


def mix_kernel(
    info, weighted, total, hidden, gain_mix, gain_feed,
    o0, o1, g0, g1,
    attended_out, mixed_out, projected_out, after_out, normed_out, gate_out, up_out, act_out,
    output_full, gate_full, up_full, sems,
):
    index = info[0]
    feed = gate_full.shape[1]
    output_copies = place(index, (o0, o1), output_full, sems.at[0])
    gate_copies = place(index, (g0, g1), gate_full, sems.at[1], 0)
    up_copies = place(index, (g0, g1), up_full, sems.at[2], feed)
    heads = total.shape[1] // lanes
    head_dim = weighted.shape[1] // heads
    for head in range(heads):
        part = slice(head * head_dim, (head + 1) * head_dim)
        ratio = weighted[:, part] / total[:, head * lanes : head * lanes + 1]
        attended_out[:, part] = ratio
        mixed_out[:, part] = ratio.astype(bf16)
    finish(output_copies)
    projected = nn(mixed_out[...], output_full[...])
    projected_out[...] = projected
    hat, _ = unit(projected)
    after = hidden[...].astype(f32) + hat * (1.0 + gain_mix[...])
    after_out[...] = after
    hat, _ = unit(after)
    normed_out[...] = (hat * (1.0 + gain_feed[...])).astype(bf16)
    finish(gate_copies)
    finish(up_copies)
    step_width = 512

    @pl.loop(0, gate_full.shape[1] // step_width)
    def _(step):
        part = pl.ds(pl.multiple_of(step * step_width, step_width), step_width)
        gate = nn(normed_out[...], gate_full[:, part])
        up = nn(normed_out[...], up_full[:, part])
        gate_out[:, part] = gate
        up_out[:, part] = up
        inner = 0.7978845608028654 * (gate + 0.044715 * gate * gate * gate)
        act_out[:, part] = (0.5 * gate * (1.0 + jnp.tanh(inner)) * up).astype(bf16)


def store_columns(keep, send, slot, base, rows, block):
    target = keep if slot < 2 else send
    for number in range(block.shape[1] // lanes):
        target[slot % 2, base + number * rows : base + (number + 1) * rows, :] = block[
            :, number * lanes : (number + 1) * lanes
        ].astype(bf16)


def feed_kernel(
    info, act, gate, up, normed, after, cotangent, gain_final,
    d0, d1,
    hidden_out, d_gate, d_up, gain_grad, keep, send,
    down_full, d_down, turned, sems,
):
    index = info[0]
    finish(place(index, (d0, d1), down_full, sems))
    down = nn(act[...], down_full[...])
    hat, inverse = unit(down)
    scale = 1.0 + gain_final[...]
    hidden_out[...] = (after[...] + hat * scale).astype(bf16)
    grad = cotangent[...].astype(f32)
    gain_grad[...] = jnp.sum(grad * hat, axis=0, keepdims=True)
    d_down[...] = unit_back(hat, inverse, grad * scale).astype(bf16)
    turned[...] = normed[...].astype(f32).T.astype(bf16)
    step_width = 512

    @pl.loop(0, down_full.shape[0] // step_width)
    def _(step):
        part = pl.ds(pl.multiple_of(step * step_width, step_width), step_width)
        d_act = nt(d_down[...], down_full[part, :])
        x = gate[:, part]
        curve = jnp.tanh(0.7978845608028654 * (x + 0.044715 * x * x * x))
        slope = 0.5 * (1.0 + curve) + 0.5 * x * (1.0 - curve * curve) * (
            0.7978845608028654 * (1.0 + 3.0 * 0.044715 * x * x)
        )
        d_gate[:, part] = (d_act * up[:, part] * slope).astype(bf16)
        d_up[:, part] = (d_act * (0.5 * x * (1.0 + curve))).astype(bf16)

    model = normed.shape[1]
    rows = model // 4
    wide = gate.shape[1]
    down_rows = wide // 4
    part_rows = (wide // lanes) * rows
    for slot, step in enumerate(order):
        target = keep if slot < 2 else send
        owner = index ^ step
        lhs = turned[pl.ds(pl.multiple_of(owner * rows, 16), rows), :]
        for base, source in ((0, d_gate), (part_rows, d_up)):

            @pl.loop(0, wide // step_width)
            def _(move):
                part = pl.ds(pl.multiple_of(move * step_width, step_width), step_width)
                block = nn(lhs, source[:, part]).astype(bf16)
                for number in range(step_width // lanes):
                    begin = base + (move * (step_width // lanes) + number) * rows
                    target[slot % 2, pl.ds(pl.multiple_of(begin, 16), rows), :] = block[
                        :, number * lanes : (number + 1) * lanes
                    ]

        left = act[:, pl.ds(pl.multiple_of(owner * down_rows, lanes), down_rows)]
        store_columns(keep, send, slot, 2 * part_rows, down_rows, tn(left, d_down[...]))


def feed_back_kernel(
    info, d_gate, d_up, after, projected, attended, total, cotangent, gain_mix, gain_feed,
    g0, g1, o0, o1,
    d_after_out, d_projected_out, d_mixed_out, rows_out, feed_grad, mix_grad,
    gate_full, up_full, output_full, total_grad, sems,
):
    index = info[0]
    gate_copies = place(index, (g0, g1), gate_full, sems.at[0], 0)
    up_copies = place(index, (g0, g1), up_full, sems.at[1], gate_full.shape[1])
    output_copies = place(index, (o0, o1), output_full, sems.at[2])
    finish(gate_copies)
    total_grad[...] = nt(d_gate[...], gate_full[...])
    finish(up_copies)
    grad = total_grad[...] + nt(d_up[...], up_full[...])
    hat, inverse = unit(after[...])
    feed_grad[...] = jnp.sum(grad * hat, axis=0, keepdims=True)
    d_after = cotangent[...].astype(f32) + unit_back(hat, inverse, grad * (1.0 + gain_feed[...]))
    d_after_out[...] = d_after
    hat, inverse = unit(projected[...])
    mix_grad[...] = jnp.sum(d_after * hat, axis=0, keepdims=True)
    d_projected = unit_back(hat, inverse, d_after * (1.0 + gain_mix[...])).astype(bf16)
    d_projected_out[...] = d_projected
    finish(output_copies)
    d_mixed = nt(d_projected, output_full[...]).astype(bf16)
    d_mixed_out[...] = d_mixed
    heads = total.shape[1] // lanes
    head_dim = attended.shape[1] // heads
    tokens = attended.shape[0]
    lane = lax.broadcasted_iota(jnp.int32, (tokens, lanes), 1)
    table = jnp.zeros((tokens, lanes), f32)
    for head in range(heads):
        part = slice(head * head_dim, (head + 1) * head_dim)
        delta = jnp.sum(d_mixed[:, part].astype(f32) * attended[:, part], axis=1, keepdims=True)
        table = jnp.where(lane == head, delta, table)
        share = 1.0 / total[:, head * lanes : (head + 1) * lanes]
        table = jnp.where(lane == heads + head, share, table)
    rows_out[...] = table.T[: rows_out.shape[0], :]


def attend_back_kernel(first, count, info, queries, d_mixed, table, places, *refs):
    chunks = refs[:count]
    refs = refs[count:]
    if not first:
        query_in = refs[0]
        refs = refs[1:]
    query_grads = refs[0]
    chunk_grads = refs[1 : 1 + count]
    key_sum, value_sum = refs[1 + count :]
    tokens = queries.shape[0]
    head_dim = chunks[0].shape[1] // 2
    heads = queries.shape[1] // head_dim
    if first:
        query_grads[...] = jnp.zeros_like(query_grads)
    else:
        query_grads[...] = query_in[...]
    first_row = info[1]
    for number, (chunk, chunk_grad) in enumerate(zip(chunks, chunk_grads)):
        base = info[2 + number]
        chunk_grad[...] = jnp.zeros_like(chunk_grad)

        @pl.loop(0, chunk.shape[0] // tokens)
        def _(step):
            start = base + step * tokens

            @pl.when((start >= 0) & (start <= first_row))
            def _():
                local = pl.ds(pl.multiple_of(step * tokens, tokens), tokens)
                row = first_row + lax.broadcasted_iota(jnp.int32, (tokens, tokens), 1)
                col = start + lax.broadcasted_iota(jnp.int32, (tokens, tokens), 0)
                allowed = (col <= row) & (col >= row - places[...])
                keys = chunk[local, :head_dim]
                values = chunk[local, head_dim:]
                for head in range(heads):
                    part = slice(head * head_dim, (head + 1) * head_dim)
                    query = queries[:, part]
                    grad = d_mixed[:, part]
                    expo = jnp.where(allowed, jnp.exp(nt(keys, query)), 0.0)
                    probs = expo * table[heads + head : heads + head + 1, :]
                    back = nt(values, grad) - table[head : head + 1, :]
                    d_scores = (probs * back).astype(bf16)
                    d_value = nn(probs.astype(bf16), grad)
                    d_key = nn(d_scores, query)
                    if head == 0:
                        key_sum[...] = d_key
                        value_sum[...] = d_value
                    else:
                        key_sum[...] += d_key
                        value_sum[...] += d_value
                    query_grads[:, part] += tn(d_scores, keys)
                chunk_grad[local, :head_dim] = key_sum[...].astype(bf16)
                chunk_grad[local, head_dim:] = value_sum[...].astype(bf16)


def unspin(value, cosine, sine):
    half = value.shape[-1] // 2
    first, second = value[:, :half], value[:, half:]
    return jnp.concatenate(
        [first * cosine + second * sine, second * cosine - first * sine], axis=-1
    )


def query_back_kernel(
    info, query_grads, raw, cosine, sine, gain_query, normed, mixed, d_projected,
    q0, q1,
    d_normed_out, gain_grad, keep, send,
    query_full, d_raw, turned, sems,
):
    index = info[0]
    copies = place(index, (q0, q1), query_full, sems)
    head_dim = gain_query.shape[1]
    wide = raw.shape[1]
    scale = 1.0 + gain_query[...]
    gain_sum = jnp.zeros((1, head_dim), f32)
    for start in range(0, wide, head_dim):
        part = slice(start, start + head_dim)
        hat, inverse = unit(raw[:, part])
        grad = unspin(query_grads[:, part] * head_dim ** (-0.5), cosine[...], sine[...])
        gain_sum += jnp.sum(grad * hat, axis=0, keepdims=True)
        d_raw[:, part] = unit_back(hat, inverse, grad * scale).astype(bf16)
    gain_grad[...] = gain_sum
    turned[...] = normed[...].astype(f32).T.astype(bf16)
    rows = normed.shape[1] // 4
    mixed_rows = mixed.shape[1] // 4
    for slot, step in enumerate(order):
        owner = index ^ step
        lhs = turned[pl.ds(pl.multiple_of(owner * rows, 16), rows), :]
        store_columns(keep, send, slot, 0, rows, nn(lhs, d_raw[...]))
        left = mixed[:, pl.ds(pl.multiple_of(owner * mixed_rows, lanes), mixed_rows)]
        store_columns(
            keep, send, slot, (wide // lanes) * rows, mixed_rows, tn(left, d_projected[...])
        )
    finish(copies)
    d_normed_out[...] = nt(d_raw[...], query_full[...])


def key_back_kernel(
    count, info, cosine, sine, gain_key, gain_in, raw, normed, hidden, d_after, d_normed_query,
    b0, b1, *refs,
):
    parts = refs[:count]
    (
        input_grad, key_gain_grad, in_gain_grad, keep, send,
        both_full, d_both, turned, sems,
    ) = refs[count:]
    index = info[0]
    copies = place(index, (b0, b1), both_full, sems)
    width = raw.shape[1]
    both = parts[0][...].astype(f32)
    for piece in parts[1:]:
        both = both + piece[...].astype(f32)
    hat, inverse = unit(raw[...])
    grad = unspin(both[:, :width], cosine[...], sine[...])
    key_gain_grad[...] = jnp.sum(grad * hat, axis=0, keepdims=True)
    d_both[:, :width] = unit_back(hat, inverse, grad * (1.0 + gain_key[...])).astype(bf16)
    d_both[:, width:] = both[:, width:].astype(bf16)
    turned[...] = normed[...].astype(f32).T.astype(bf16)
    rows = normed.shape[1] // 4
    for slot, step in enumerate(order):
        owner = index ^ step
        lhs = turned[pl.ds(pl.multiple_of(owner * rows, 16), rows), :]
        store_columns(keep, send, slot, 0, rows, nn(lhs, d_both[...]))
    finish(copies)
    d_normed = d_normed_query[...] + nt(d_both[...], both_full[...])
    hat, inverse = unit(hidden[...].astype(f32))
    in_gain_grad[...] = jnp.sum(d_normed * hat, axis=0, keepdims=True)
    input_grad[...] = d_after[...] + unit_back(hat, inverse, d_normed * (1.0 + gain_in[...]))


def unpack_kernel(widths, rows_of, pack, *outs):
    base = 0
    for out, width, rows in zip(outs, widths, rows_of):
        for number in range(width // lanes):
            out[:, number * lanes : (number + 1) * lanes] = pack[
                base : base + rows, :
            ].astype(f32)
            base += rows


def flip(value, axis, bit):
    size = lax.axis_size(axis)
    return lax.ppermute(value, axis, [(i, i ^ bit) for i in range(size)])


def pair_up(shard, far):
    both = jnp.concatenate([shard, far], axis=0)
    return both, flip(both, "fsdp", 1)


def add_low(*values):
    total = values[0].astype(f32)
    for value in values[1:]:
        total = total + value.astype(f32)
    return total.astype(bf16)


def take_half(value, which):
    half = value.shape[0] // 2
    return lax.dynamic_slice_in_dim(value, which * half, half, 0)


def send_far(keep, near):
    return add_low(keep[1], near[1])


def add_far(keep, near, far):
    return add_low(keep[0], near[0], far)


def ctx_bits():
    return [1 << i for i in range(lax.axis_size("ctx").bit_length() - 1)]


def scatter_ctx(value):
    me = lax.axis_index("ctx")
    for bit in ctx_bits():
        mine = (me // bit) % 2
        sent = flip(take_half(value, 1 - mine), "ctx", bit)
        value = add_low(take_half(value, mine), sent)
    return value


def gather_ctx(value):
    me = lax.axis_index("ctx")
    for bit in reversed(ctx_bits()):
        mine = (me // bit) % 2
        other = flip(value, "ctx", bit)
        low = jnp.where(mine == 0, value, other)
        high = jnp.where(mine == 0, other, value)
        value = jnp.concatenate([low, high], axis=0)
    return value


def send_back(pair, shift, groups):
    return lax.ppermute(
        add_low(*pair), "ctx", [(i + shift, i) for i in range(groups - shift)]
    )


def on_device(
    hidden_in, positions, query_weight, key_weight, value_weight, output_weight, gate_weight,
    up_weight, down_weight, input_gain, mixer_gain, feed_gain, final_gain, query_gain, key_gain,
    out_grad,
):
    tokens = hidden_in.shape[1]
    model = hidden_in.shape[2]
    rows = key_weight.shape[0]
    head_dim = key_weight.shape[1]
    wide = query_weight.shape[1]
    heads = wide // head_dim
    feed = gate_weight.shape[1]
    mixed_rows = output_weight.shape[0]
    down_rows = down_weight.shape[0]
    me = lax.axis_index("fsdp")
    ctx = lax.axis_index("ctx")
    groups = lax.axis_size("ctx")
    first_row = ctx * tokens

    both_shard = jnp.concatenate([key_weight, value_weight], axis=1)
    far_both = flip(both_shard, "fsdp", 2)
    gains = (input_gain, mixer_gain, feed_gain, final_gain, query_gain, key_gain)
    gains, both_shard = tie(gains, both_shard)
    gain_pack = jnp.concatenate(gains)[None]
    gain_pack = jnp.broadcast_to(gain_pack, (16, gain_pack.shape[1]))
    far_gain = flip(gain_pack, "fsdp", 2)
    far_query = flip(query_weight, "fsdp", 2)
    both_blocks = pair_up(both_shard, far_both)
    gain_blocks = pair_up(gain_pack, far_gain)
    feed_pair = jnp.concatenate([gate_weight, up_weight], axis=1)

    gain_rows = jnp.zeros((4, gain_pack.shape[1]), bf16)
    for step in range(4):
        row = 16 * (step // 2)
        gain_rows = lax.dynamic_update_slice_in_dim(
            gain_rows, gain_blocks[step % 2][row : row + 1], me ^ step, 0
        )
    gain_rows = gain_rows.astype(f32)
    gain_in, gain_mix, gain_feed, gain_final = [
        gain_rows[:, i * rows : (i + 1) * rows].reshape(1, -1) for i in range(4)
    ]
    head_piece = query_gain.shape[0]
    gain_query, gain_key = [
        gain_rows[:, 4 * rows + i * head_piece : 4 * rows + (i + 1) * head_piece].reshape(1, -1)
        for i in range(2)
    ]

    hidden = hidden_in[0]
    cotangent = out_grad[0]
    places = positions[0]
    place_col = places[:, None]
    place_row = places[None, :]
    half = head_dim // 2
    freqs = rope_base ** (-(jnp.arange(half, dtype=f32) * 2.0) / head_dim)
    angles = places.astype(f32)[:, None] * freqs[None, :]
    cosine, sine = jnp.cos(angles), jnp.sin(angles)

    def facts(*starts):
        return jnp.stack([me, first_row, *starts]).astype(jnp.int32)

    info = facts()
    sem = pltpu.SemaphoreType.DMA
    token_flops = 2 * tokens * model

    normed, key_raw, kv = call(
        kv_kernel,
        (info, hidden, gain_in, gain_key, cosine, sine, *both_blocks),
        [SMEM] + [VMEM] * 5 + [ANY] * 2,
        [((tokens, model), bf16), ((tokens, head_dim), f32), ((tokens, 2 * head_dim), bf16)],
        [pltpu.VMEM((model, 2 * head_dim), bf16), sem((4,))],
        flops=token_flops * 2 * head_dim,
        name="key_value",
    )
    far_query, kv = tie(far_query, kv)
    far_output = flip(output_weight, "fsdp", 2)

    ring = groups == 8
    if ring:
        side = ctx % 2
        stage = ctx // 2
        crossed = flip(kv, "ctx", 1)
        moved = [
            lax.ppermute(kv, "ctx", [(i, i + 2 * shift) for i in range(groups - 2 * shift)])
            for shift in range(1, groups // 2)
        ]
        crossed, moved[0], far_query = tie(crossed, moved[0], far_query)
    else:
        gathered = lax.all_gather(kv, "ctx", axis=0, tiled=True)
    query_blocks = pair_up(query_weight, far_query)
    query_raw, queries = call(
        query_kernel,
        (info, normed, gain_query, cosine, sine, *query_blocks),
        [SMEM] + [VMEM] * 4 + [ANY] * 2,
        [((tokens, wide), f32), ((tokens, wide), bf16)],
        [pltpu.VMEM((model, wide), bf16), sem((4,))],
        flops=token_flops * wide,
        name="query",
    )

    far_output, feed_pair = tie(far_output, feed_pair)
    far_feed = flip(feed_pair, "fsdp", 2)
    if ring:
        queries, moved[1] = tie(queries, moved[1])
    if ring:
        sources = []
        for shift in range(groups // 2):
            if shift == 0:
                mine, other = kv, crossed
            else:
                mine = moved[shift - 1]
                other = flip(mine, "ctx", 1)
            base = (stage - shift) * 2
            sources.append(
                ((mine, other), ((base + side) * tokens, (base + 1 - side) * tokens))
            )
    else:
        sources = [((gathered,), (jnp.int32(0),))]

    state = ()
    history = []
    chunk_flops = 4 * tokens * tokens * wide
    for number, (arrays, starts) in enumerate(sources):
        first = number == 0
        count = len(arrays)

        def attend(*args, first=first, count=count):
            attend_kernel(first, count, *args)

        state = call(
            attend,
            (facts(*starts), queries, place_col, *arrays, *state),
            [SMEM] + [VMEM] * (2 + count + len(state)),
            [((tokens, wide), f32), ((tokens, heads * lanes), f32)],
            flops=chunk_flops * 2,
            name="attend",
        )
        history.append(state[1])
    weighted, total = state
    far_output, total, far_feed, down_weight = tie(far_output, total, far_feed, down_weight)
    output_blocks = pair_up(output_weight, far_output)
    feed_blocks = pair_up(feed_pair, far_feed)
    far_down = flip(down_weight, "fsdp", 2)

    attended, mixed, projected, after, normed_feed, gate_value, up_value, activated = call(
        mix_kernel,
        (
            info, weighted, total, hidden, gain_mix, gain_feed,
            *output_blocks, *feed_blocks,
        ),
        [SMEM] + [VMEM] * 5 + [ANY] * 4,
        [
            ((tokens, wide), f32),
            ((tokens, wide), bf16),
            ((tokens, model), f32),
            ((tokens, model), f32),
            ((tokens, model), bf16),
            ((tokens, feed), f32),
            ((tokens, feed), f32),
            ((tokens, feed), bf16),
        ],
        [
            pltpu.VMEM((wide, model), bf16),
            pltpu.VMEM((model, feed), bf16),
            pltpu.VMEM((model, feed), bf16),
            sem((3, 4)),
        ],
        flops=token_flops * (wide + 2 * feed),
        name="mix",
    )
    far_down, mixed = tie(far_down, mixed)
    down_blocks = pair_up(down_weight, far_down)
    feed_rows = 2 * (feed // lanes) * rows + (model // lanes) * down_rows
    hidden_out, d_gate, d_up, grad_final, feed_keep, feed_send = call(
        feed_kernel,
        (
            info, activated, gate_value, up_value, normed_feed, after, cotangent, gain_final,
            *down_blocks,
        ),
        [SMEM] + [VMEM] * 7 + [ANY] * 2,
        [
            ((tokens, model), bf16),
            ((tokens, feed), bf16),
            ((tokens, feed), bf16),
            ((1, model), f32),
            ((2, feed_rows, lanes), bf16),
            ((2, feed_rows, lanes), bf16),
        ],
        [
            pltpu.VMEM((feed, model), bf16),
            pltpu.VMEM((tokens, model), bf16),
            pltpu.VMEM((model, tokens), bf16),
            sem((4,)),
        ],
        flops=token_flops * 5 * feed,
        name="feed",
    )
    feed_near = flip(feed_send, "fsdp", 1)

    d_after, d_projected, d_mixed, table, grad_feed_gain, grad_mix_gain = call(
        feed_back_kernel,
        (
            info, d_gate, d_up, after, projected, attended, total, cotangent, gain_mix, gain_feed,
            *feed_blocks, *output_blocks,
        ),
        [SMEM] + [VMEM] * 9 + [ANY] * 4,
        [
            ((tokens, model), f32),
            ((tokens, model), bf16),
            ((tokens, wide), bf16),
            ((2 * heads, tokens), f32),
            ((1, model), f32),
            ((1, model), f32),
        ],
        [
            pltpu.VMEM((model, feed), bf16),
            pltpu.VMEM((model, feed), bf16),
            pltpu.VMEM((wide, model), bf16),
            pltpu.VMEM((tokens, model), f32),
            sem((3, 4)),
        ],
        flops=token_flops * (2 * feed + wide),
        name="feed_back",
    )

    feed_near, d_mixed = tie(feed_near, d_mixed)
    gate_rows = (feed // lanes) * rows
    cuts = (0, gate_rows, 2 * gate_rows, feed_rows)
    feed_sums = [
        add_low(feed_keep[1, i:j], feed_near[1, i:j]) for i, j in zip(cuts[:-1], cuts[1:])
    ]
    d_mixed, *feed_sums = tie(d_mixed, *feed_sums)
    gate_far = flip(feed_sums[0], "fsdp", 2)

    query_grads = ()
    arrived = []
    waiting = None
    last = len(sources) - 1
    for number, (arrays, starts) in enumerate(reversed(sources)):
        first = number == 0
        count = len(arrays)

        def attend_back(*args, first=first, count=count):
            attend_back_kernel(first, count, *args)

        results = call(
            attend_back,
            (facts(*starts), queries, d_mixed, table, place_row, *arrays, *query_grads),
            [SMEM] + [VMEM] * (4 + count + len(query_grads)),
            [((tokens, wide), f32)] + [(a.shape, bf16) for a in arrays],
            [pltpu.VMEM((tokens, head_dim), f32), pltpu.VMEM((tokens, head_dim), f32)],
            flops=chunk_flops * 5,
            name="attend_back",
        )
        query_grads = results[:1]
        if not ring:
            arrived.append(
                lax.psum_scatter(results[1], "ctx", scatter_dimension=0, tiled=True)
            )
            continue
        shift = last - number
        own, other = results[1:]
        if waiting is not None:
            crossed, held = tie(waiting[1], query_grads[0])
            query_grads = (held,)
            arrived.append(send_back((waiting[0], crossed), 2 * (shift + 1), groups))
        waiting = (own, flip(other, "ctx", 1))
    if ring:
        arrived += list(waiting)
        arrived[0], held = tie(arrived[0], query_grads[0])
        query_grads = (held,)
    held, gate_far, feed_sums[1] = tie(query_grads[0], gate_far, feed_sums[1])
    query_grads = (held,)
    up_far = flip(feed_sums[1], "fsdp", 2)

    query_rows = (wide // lanes) * rows
    output_rows = (model // lanes) * mixed_rows
    d_normed_query, grad_query_gain, query_keep, query_send = call(
        query_back_kernel,
        (
            info, query_grads[0], query_raw, cosine, sine, gain_query, normed, mixed, d_projected,
            *query_blocks,
        ),
        [SMEM] + [VMEM] * 8 + [ANY] * 2,
        [
            ((tokens, model), f32),
            ((1, head_dim), f32),
            ((2, query_rows + output_rows, lanes), bf16),
            ((2, query_rows + output_rows, lanes), bf16),
        ],
        [
            pltpu.VMEM((model, wide), bf16),
            pltpu.VMEM((tokens, wide), bf16),
            pltpu.VMEM((model, tokens), bf16),
            sem((4,)),
        ],
        flops=token_flops * 3 * wide,
        name="query_back",
    )
    query_near = flip(query_send, "fsdp", 1)
    query_sum = add_low(query_keep[1], query_near[1])
    d_after, query_sum, up_far, feed_sums[2] = tie(d_after, query_sum, up_far, feed_sums[2])
    query_far = flip(query_sum, "fsdp", 2)

    both_rows = (2 * head_dim // lanes) * rows
    arrived_count = len(arrived)

    def key_back(*args):
        key_back_kernel(arrived_count, *args)

    grad_input, grad_key_gain, grad_in_gain, both_keep, both_send = call(
        key_back,
        (
            info, cosine, sine, gain_key, gain_in, key_raw, normed, hidden, d_after,
            d_normed_query, *both_blocks, *arrived,
        ),
        [SMEM] + [VMEM] * 9 + [ANY] * 2 + [VMEM] * arrived_count,
        [
            ((tokens, model), f32),
            ((1, head_dim), f32),
            ((1, model), f32),
            ((2, both_rows, lanes), bf16),
            ((2, both_rows, lanes), bf16),
        ],
        [
            pltpu.VMEM((model, 2 * head_dim), bf16),
            pltpu.VMEM((tokens, 2 * head_dim), bf16),
            pltpu.VMEM((model, tokens), bf16),
            sem((4,)),
        ],
        flops=token_flops * 4 * head_dim,
        name="key_back",
    )
    both_near = flip(both_send, "fsdp", 1)
    down_far = flip(feed_sums[2], "fsdp", 2)
    both_far = flip(add_low(both_keep[1], both_near[1]), "fsdp", 2)

    gain_sums = jnp.concatenate(
        [
            grad_in_gain, grad_mix_gain, grad_feed_gain, grad_final, grad_query_gain,
            grad_key_gain,
        ],
        axis=1,
    ).reshape(-1, lanes)
    for axis in ("fsdp", "ctx"):
        bit = 1
        while bit < lax.axis_size(axis):
            gain_sums = gain_sums + flip(gain_sums, axis, bit)
            bit *= 2
    gain_sums = gain_sums.reshape(-1)
    gain_shards = []
    start = 0
    for size in (model, model, model, model, head_dim, head_dim):
        gain_shards.append(
            lax.dynamic_slice_in_dim(gain_sums, start + me * (size // 4), size // 4, 0)
        )
        start += size

    def unpack(pack, shapes):
        def kernel(*args):
            unpack_kernel([s[1] for s in shapes], [s[0] for s in shapes], *args)

        return call(kernel, (pack,), [VMEM], [(s, f32) for s in shapes], name="unpack")

    def feed_part(number, far):
        part = slice(cuts[number], cuts[number + 1])
        return add_low(feed_keep[0, part], feed_near[0, part], far)

    gate_far, both_keep = tie(gate_far, both_keep)
    gate_part = scatter_ctx(feed_part(0, gate_far))
    query_far, gate_part = tie(query_far, gate_part)
    up_part = scatter_ctx(feed_part(1, up_far))
    down_far, up_part = tie(down_far, up_part)
    query_part = scatter_ctx(add_low(query_keep[0], query_near[0], query_far))
    both_far, query_part = tie(both_far, query_part)
    down_part = scatter_ctx(feed_part(2, down_far))
    both_part = scatter_ctx(add_low(both_keep[0], both_near[0], both_far))
    (grad_gate,) = unpack(gather_ctx(gate_part), [gate_weight.shape])
    (grad_up,) = unpack(gather_ctx(up_part), [up_weight.shape])
    grad_query, grad_output = unpack(
        gather_ctx(query_part), [query_weight.shape, output_weight.shape]
    )
    (grad_down,) = unpack(gather_ctx(down_part), [down_weight.shape])
    grad_key, grad_value = unpack(
        gather_ctx(both_part), [key_weight.shape, value_weight.shape]
    )
    return (
        hidden_out[None],
        grad_input[None],
        grad_query,
        grad_key,
        grad_value,
        grad_output,
        grad_gate,
        grad_up,
        grad_down,
        *gain_shards,
    )


def solution(mesh):
    token = P("fsdp", "ctx", None)
    weight = P("fsdp", None)
    gain = P("fsdp")
    return jax.shard_map(
        on_device,
        mesh=mesh,
        in_specs=(token, P("fsdp", "ctx")) + (weight,) * 7 + (gain,) * 6 + (token,),
        out_specs=(token, token) + (weight,) * 7 + (gain,) * 6,
        check_vma=False,
    )
```

```python
import jax
import jax.numpy as jnp
from jax import lax
from jax.experimental import pallas as pl
from jax.experimental.pallas import tpu as pltpu
from jax.sharding import PartitionSpec as P

eps = 1e-06
rope_base = 1000000.0
lanes = 128
order = (0, 2, 1, 3)
vmem_bytes = 16 * 1024 * 1024
gain_pad = 16
f32 = jnp.float32
bf16 = jnp.bfloat16

ANY = pl.BlockSpec(memory_space=pl.ANY)
SMEM = pl.BlockSpec(memory_space=pltpu.SMEM)
VMEM = pl.BlockSpec(memory_space=pltpu.VMEM)


def tie(*values):
    return lax.optimization_barrier(values)


def call(kernel, inputs, specs, outs, scratch=(), flops=0, limit=vmem_bytes, name=None):
    return pl.pallas_call(
        kernel,
        out_shape=tuple(jax.ShapeDtypeStruct(s, d) for s, d in outs),
        in_specs=list(specs),
        out_specs=tuple(VMEM for _ in outs),
        scratch_shapes=list(scratch),
        compiler_params=pltpu.CompilerParams(vmem_limit_bytes=limit),
        cost_estimate=pl.CostEstimate(flops=1, bytes_accessed=1, transcendentals=0),
        name=name,
    )(*inputs)


def nn(left, right):
    return lax.dot_general(left, right, (((1,), (0,)), ((), ())), preferred_element_type=f32)


def nt(left, right):
    return lax.dot_general(left, right, (((1,), (1,)), ((), ())), preferred_element_type=f32)


def tn(left, right):
    return lax.dot_general(left, right, (((0,), (0,)), ((), ())), preferred_element_type=f32)


def unit(value):
    inverse = lax.rsqrt(jnp.mean(value * value, axis=-1, keepdims=True) + eps)
    return value * inverse, inverse


def unit_back(hat, inverse, grad_hat):
    return inverse * (grad_hat - hat * jnp.mean(grad_hat * hat, axis=-1, keepdims=True))


def spin(value, cosine, sine):
    half = value.shape[-1] // 2
    first, second = value[:, :half], value[:, half:]
    return jnp.concatenate(
        [first * cosine - second * sine, second * cosine + first * sine], axis=-1
    )


def place(index, pairs, full, sems, columns=None):
    rows = full.shape[0] // 4
    pitch = pairs[0].shape[0] // 2
    copies = []
    for step in range(4):
        begin = pl.multiple_of((index ^ step) * rows, 16)
        source = pairs[step % 2].at[pl.ds((step // 2) * pitch, rows)]
        if columns is not None:
            source = source.at[:, pl.ds(columns, full.shape[1])]
        copy = pltpu.make_async_copy(source, full.at[pl.ds(begin, rows)], sems.at[step])
        copy.start()
        copies.append(copy)
    return copies


def finish(copies):
    for copy in copies:
        copy.wait()


def kv_kernel(
    info, hidden, cosine, sine,
    b0, b1,
    normed_out, key_raw_out, kv_out, gains_out,
    both_full, gain_parts, sems,
):
    index = info[0]
    copies = place(index, (b0, b1), both_full, sems.at[0])
    model = hidden.shape[1]
    rows = model // 4
    width = key_raw_out.shape[1]
    piece = width // 4
    gain_copies = []
    for step in range(4):
        begin = pl.multiple_of((index ^ step) * gain_pad, gain_pad)
        source = (b0, b1)[step % 2].at[pl.ds((step // 2) * (rows + gain_pad) + rows, gain_pad)]
        copy = pltpu.make_async_copy(
            source, gain_parts.at[pl.ds(begin, gain_pad)], sems.at[1, step]
        )
        copy.start()
        gain_copies.append(copy)
    hat, _ = unit(hidden[...].astype(f32))
    finish(gain_copies)
    span = 2 * lanes
    line = lax.broadcasted_iota(jnp.int32, (span, model), 0)
    column = lax.broadcasted_iota(jnp.int32, (span, model), 1)
    wide_gain = jnp.zeros((gain_pad, model), f32)
    head_gain = jnp.zeros((gain_pad, model), f32)
    for owner in range(4):
        values = gain_parts[owner * gain_pad : (owner + 1) * gain_pad, :span]
        spots = (column == line + owner * rows) & (line < rows)
        wide_gain += nn(values, spots.astype(f32).astype(bf16))
        spots = (column == line + owner * piece) & (line < piece)
        head_gain += nn(values, spots.astype(f32).astype(bf16))
    which = lax.broadcasted_iota(jnp.int32, (gain_pad, model), 0)
    gains = jnp.where(which < 4, wide_gain, head_gain)
    gains_out[...] = gains
    normed = (hat * (1.0 + gains[0:1, :])).astype(bf16)
    normed_out[...] = normed
    finish(copies)
    raw = nn(normed, both_full[:, :width])
    key_raw_out[...] = raw
    hat, _ = unit(raw)
    scale = 1.0 + gains[5:6, :width]
    kv_out[:, :width] = spin(hat * scale, cosine[...], sine[...]).astype(bf16)
    kv_out[:, width:] = nn(normed, both_full[:, width:]).astype(bf16)


def query_kernel(
    info, normed, gains, cosine, sine, q0, q1,
    raw_out, query_out, query_full, sems,
):
    finish(place(info[0], (q0, q1), query_full, sems))
    head_dim = 2 * cosine.shape[1]
    for start in range(0, query_full.shape[1], head_dim):
        part = slice(start, start + head_dim)
        raw = nn(normed[...], query_full[:, part])
        raw_out[:, part] = raw
        hat, _ = unit(raw)
        turned = spin(hat * (1.0 + gains[4:5, :head_dim]), cosine[...], sine[...])
        query_out[:, part] = (turned * head_dim ** (-0.5)).astype(bf16)


def attend_kernel(first, count, info, queries, places, *refs):
    chunks = refs[:count]
    refs = refs[count:]
    if not first:
        weighted_in, total_in = refs[:2]
        refs = refs[2:]
    weighted, total = refs
    tokens = queries.shape[0]
    head_dim = chunks[0].shape[1] // 2
    heads = queries.shape[1] // head_dim
    if first:
        weighted[...] = jnp.zeros_like(weighted)
        total[...] = jnp.zeros_like(total)
    else:
        weighted[...] = weighted_in[...]
        total[...] = total_in[...]
    first_row = info[1]
    for number, chunk in enumerate(chunks):
        base = info[2 + number]

        @pl.loop(0, chunk.shape[0] // tokens)
        def _(step):
            start = base + step * tokens

            @pl.when((start >= 0) & (start <= first_row))
            def _():
                local = pl.ds(pl.multiple_of(step * tokens, tokens), tokens)
                row = first_row + lax.broadcasted_iota(jnp.int32, (tokens, tokens), 0)
                col = start + lax.broadcasted_iota(jnp.int32, (tokens, tokens), 1)
                allowed = (col <= row) & (col >= row - places[...])
                keys = chunk[local, :head_dim]
                values = chunk[local, head_dim:]
                for head in range(heads):
                    part = slice(head * head_dim, (head + 1) * head_dim)
                    scores = nt(queries[:, part], keys)
                    expo = jnp.where(allowed, jnp.exp(scores), 0.0)
                    spot = slice(head * lanes, (head + 1) * lanes)
                    total[:, spot] += jnp.sum(expo, axis=1, keepdims=True)
                    weighted[:, part] += nn(expo.astype(bf16), values)


def mix_kernel(
    info, weighted, total, hidden, gains,
    o0, o1, g0, g1,
    attended_out, mixed_out, projected_out, after_out, normed_out, gate_out, up_out, act_out,
    output_full, gate_full, up_full, sems,
):
    index = info[0]
    feed = gate_full.shape[1]
    output_copies = place(index, (o0, o1), output_full, sems.at[0])
    gate_copies = place(index, (g0, g1), gate_full, sems.at[1], 0)
    up_copies = place(index, (g0, g1), up_full, sems.at[2], feed)
    heads = total.shape[1] // lanes
    head_dim = weighted.shape[1] // heads
    for head in range(heads):
        part = slice(head * head_dim, (head + 1) * head_dim)
        ratio = weighted[:, part] / total[:, head * lanes : head * lanes + 1]
        attended_out[:, part] = ratio
        mixed_out[:, part] = ratio.astype(bf16)
    finish(output_copies)
    projected = nn(mixed_out[...], output_full[...])
    projected_out[...] = projected
    hat, _ = unit(projected)
    after = hidden[...].astype(f32) + hat * (1.0 + gains[1:2, :])
    after_out[...] = after
    hat, _ = unit(after)
    normed_out[...] = (hat * (1.0 + gains[2:3, :])).astype(bf16)
    finish(gate_copies)
    finish(up_copies)
    step_width = 512

    @pl.loop(0, gate_full.shape[1] // step_width)
    def _(step):
        part = pl.ds(pl.multiple_of(step * step_width, step_width), step_width)
        gate = nn(normed_out[...], gate_full[:, part])
        up = nn(normed_out[...], up_full[:, part])
        gate_out[:, part] = gate
        up_out[:, part] = up
        inner = 0.7978845608028654 * (gate + 0.044715 * gate * gate * gate)
        act_out[:, part] = (0.5 * gate * (1.0 + jnp.tanh(inner)) * up).astype(bf16)


def store_columns(keep, send, slot, base, rows, block):
    target = keep if slot < 2 else send
    for number in range(block.shape[1] // lanes):
        target[slot % 2, base + number * rows : base + (number + 1) * rows, :] = block[
            :, number * lanes : (number + 1) * lanes
        ].astype(bf16)


def feed_kernel(
    info, act, gate, up, normed, after, cotangent, gains,
    d0, d1,
    hidden_out, d_gate, d_up, gain_grad, keep, send,
    down_full, d_down, turned, sems,
):
    index = info[0]
    finish(place(index, (d0, d1), down_full, sems))
    down = nn(act[...], down_full[...])
    hat, inverse = unit(down)
    scale = 1.0 + gains[3:4, :]
    hidden_out[...] = (after[...] + hat * scale).astype(bf16)
    grad = cotangent[...].astype(f32)
    gain_grad[...] = jnp.sum(grad * hat, axis=0, keepdims=True)
    d_down[...] = unit_back(hat, inverse, grad * scale).astype(bf16)
    turned[...] = normed[...].astype(f32).T.astype(bf16)
    step_width = 512

    @pl.loop(0, down_full.shape[0] // step_width)
    def _(step):
        part = pl.ds(pl.multiple_of(step * step_width, step_width), step_width)
        d_act = nt(d_down[...], down_full[part, :])
        x = gate[:, part]
        curve = jnp.tanh(0.7978845608028654 * (x + 0.044715 * x * x * x))
        slope = 0.5 * (1.0 + curve) + 0.5 * x * (1.0 - curve * curve) * (
            0.7978845608028654 * (1.0 + 3.0 * 0.044715 * x * x)
        )
        d_gate[:, part] = (d_act * up[:, part] * slope).astype(bf16)
        d_up[:, part] = (d_act * (0.5 * x * (1.0 + curve))).astype(bf16)

    model = normed.shape[1]
    rows = model // 4
    wide = gate.shape[1]
    down_rows = wide // 4
    part_rows = (wide // lanes) * rows
    for slot, step in enumerate(order):
        target = keep if slot < 2 else send
        owner = index ^ step
        lhs = turned[pl.ds(pl.multiple_of(owner * rows, 16), rows), :]
        for base, source in ((0, d_gate), (part_rows, d_up)):

            @pl.loop(0, wide // step_width)
            def _(move):
                part = pl.ds(pl.multiple_of(move * step_width, step_width), step_width)
                block = nn(lhs, source[:, part]).astype(bf16)
                for number in range(step_width // lanes):
                    begin = base + (move * (step_width // lanes) + number) * rows
                    target[slot % 2, pl.ds(pl.multiple_of(begin, 16), rows), :] = block[
                        :, number * lanes : (number + 1) * lanes
                    ]

        left = act[:, pl.ds(pl.multiple_of(owner * down_rows, lanes), down_rows)]
        store_columns(keep, send, slot, 2 * part_rows, down_rows, tn(left, d_down[...]))


def feed_back_kernel(
    info, d_gate, d_up, after, projected, attended, total, cotangent, gains,
    g0, g1, o0, o1,
    d_after_out, d_projected_out, d_mixed_out, rows_out, feed_grad, mix_grad,
    gate_full, up_full, output_full, total_grad, sems,
):
    index = info[0]
    gate_copies = place(index, (g0, g1), gate_full, sems.at[0], 0)
    up_copies = place(index, (g0, g1), up_full, sems.at[1], gate_full.shape[1])
    output_copies = place(index, (o0, o1), output_full, sems.at[2])
    finish(gate_copies)
    total_grad[...] = nt(d_gate[...], gate_full[...])
    finish(up_copies)
    grad = total_grad[...] + nt(d_up[...], up_full[...])
    hat, inverse = unit(after[...])
    feed_grad[...] = jnp.sum(grad * hat, axis=0, keepdims=True)
    d_after = cotangent[...].astype(f32) + unit_back(hat, inverse, grad * (1.0 + gains[2:3, :]))
    d_after_out[...] = d_after
    hat, inverse = unit(projected[...])
    mix_grad[...] = jnp.sum(d_after * hat, axis=0, keepdims=True)
    d_projected = unit_back(hat, inverse, d_after * (1.0 + gains[1:2, :])).astype(bf16)
    d_projected_out[...] = d_projected
    finish(output_copies)
    d_mixed = nt(d_projected, output_full[...]).astype(bf16)
    d_mixed_out[...] = d_mixed
    heads = total.shape[1] // lanes
    head_dim = attended.shape[1] // heads
    tokens = attended.shape[0]
    lane = lax.broadcasted_iota(jnp.int32, (tokens, lanes), 1)
    table = jnp.zeros((tokens, lanes), f32)
    for head in range(heads):
        part = slice(head * head_dim, (head + 1) * head_dim)
        delta = jnp.sum(d_mixed[:, part].astype(f32) * attended[:, part], axis=1, keepdims=True)
        table = jnp.where(lane == head, delta, table)
        share = 1.0 / total[:, head * lanes : (head + 1) * lanes]
        table = jnp.where(lane == heads + head, share, table)
    rows_out[...] = table.T[: rows_out.shape[0], :]


def attend_back_kernel(first, count, info, queries, d_mixed, table, places, *refs):
    chunks = refs[:count]
    refs = refs[count:]
    if not first:
        query_in = refs[0]
        refs = refs[1:]
    query_grads = refs[0]
    chunk_grads = refs[1 : 1 + count]
    key_sum, value_sum = refs[1 + count :]
    tokens = queries.shape[0]
    head_dim = chunks[0].shape[1] // 2
    heads = queries.shape[1] // head_dim
    if first:
        query_grads[...] = jnp.zeros_like(query_grads)
    else:
        query_grads[...] = query_in[...]
    first_row = info[1]
    for number, (chunk, chunk_grad) in enumerate(zip(chunks, chunk_grads)):
        base = info[2 + number]
        chunk_grad[...] = jnp.zeros_like(chunk_grad)

        @pl.loop(0, chunk.shape[0] // tokens)
        def _(step):
            start = base + step * tokens

            @pl.when((start >= 0) & (start <= first_row))
            def _():
                local = pl.ds(pl.multiple_of(step * tokens, tokens), tokens)
                row = first_row + lax.broadcasted_iota(jnp.int32, (tokens, tokens), 1)
                col = start + lax.broadcasted_iota(jnp.int32, (tokens, tokens), 0)
                allowed = (col <= row) & (col >= row - places[...])
                keys = chunk[local, :head_dim]
                values = chunk[local, head_dim:]
                for head in range(heads):
                    part = slice(head * head_dim, (head + 1) * head_dim)
                    query = queries[:, part]
                    grad = d_mixed[:, part]
                    expo = jnp.where(allowed, jnp.exp(nt(keys, query)), 0.0)
                    probs = expo * table[heads + head : heads + head + 1, :]
                    back = nt(values, grad) - table[head : head + 1, :]
                    d_scores = (probs * back).astype(bf16)
                    d_value = nn(probs.astype(bf16), grad)
                    d_key = nn(d_scores, query)
                    if head == 0:
                        key_sum[...] = d_key
                        value_sum[...] = d_value
                    else:
                        key_sum[...] += d_key
                        value_sum[...] += d_value
                    query_grads[:, part] += tn(d_scores, keys)
                chunk_grad[local, :head_dim] = key_sum[...].astype(bf16)
                chunk_grad[local, head_dim:] = value_sum[...].astype(bf16)


def unspin(value, cosine, sine):
    half = value.shape[-1] // 2
    first, second = value[:, :half], value[:, half:]
    return jnp.concatenate(
        [first * cosine + second * sine, second * cosine - first * sine], axis=-1
    )


def query_back_kernel(
    info, query_grads, raw, cosine, sine, gains, normed, mixed, d_projected,
    q0, q1,
    d_normed_out, gain_grad, keep, send,
    query_full, d_raw, turned, sems,
):
    index = info[0]
    copies = place(index, (q0, q1), query_full, sems)
    head_dim = 2 * cosine.shape[1]
    wide = raw.shape[1]
    scale = 1.0 + gains[4:5, :head_dim]
    gain_sum = jnp.zeros((1, head_dim), f32)
    for start in range(0, wide, head_dim):
        part = slice(start, start + head_dim)
        hat, inverse = unit(raw[:, part])
        grad = unspin(query_grads[:, part] * head_dim ** (-0.5), cosine[...], sine[...])
        gain_sum += jnp.sum(grad * hat, axis=0, keepdims=True)
        d_raw[:, part] = unit_back(hat, inverse, grad * scale).astype(bf16)
    gain_grad[...] = gain_sum
    turned[...] = normed[...].astype(f32).T.astype(bf16)
    rows = normed.shape[1] // 4
    mixed_rows = mixed.shape[1] // 4
    for slot, step in enumerate(order):
        owner = index ^ step
        lhs = turned[pl.ds(pl.multiple_of(owner * rows, 16), rows), :]
        store_columns(keep, send, slot, 0, rows, nn(lhs, d_raw[...]))
        left = mixed[:, pl.ds(pl.multiple_of(owner * mixed_rows, lanes), mixed_rows)]
        store_columns(
            keep, send, slot, (wide // lanes) * rows, mixed_rows, tn(left, d_projected[...])
        )
    finish(copies)
    d_normed_out[...] = nt(d_raw[...], query_full[...])


def key_back_kernel(
    count, info, cosine, sine, gains, raw, normed, hidden, d_after, d_normed_query,
    mix_grad, feed_grad, final_grad, query_grad, b0, b1, *refs,
):
    parts = refs[:count]
    (
        input_grad, keep, send,
        both_full, d_both, turned, gain_grads, sems,
    ) = refs[count:]
    index = info[0]
    copies = place(index, (b0, b1), both_full, sems)
    width = raw.shape[1]
    both = parts[0][...].astype(f32)
    for piece in parts[1:]:
        both = both + piece[...].astype(f32)
    hat, inverse = unit(raw[...])
    grad = unspin(both[:, :width], cosine[...], sine[...])
    gain_grads[...] = jnp.zeros_like(gain_grads)
    gain_grads[5:6, :width] = jnp.sum(grad * hat, axis=0, keepdims=True)
    d_both[:, :width] = unit_back(hat, inverse, grad * (1.0 + gains[5:6, :width])).astype(bf16)
    d_both[:, width:] = both[:, width:].astype(bf16)
    turned[...] = normed[...].astype(f32).T.astype(bf16)
    rows = normed.shape[1] // 4
    for slot, step in enumerate(order):
        owner = index ^ step
        lhs = turned[pl.ds(pl.multiple_of(owner * rows, 16), rows), :]
        store_columns(keep, send, slot, 0, rows, nn(lhs, d_both[...]))
    finish(copies)
    d_normed = d_normed_query[...] + nt(d_both[...], both_full[...])
    hat, inverse = unit(hidden[...].astype(f32))
    gain_grads[0:1, :] = jnp.sum(d_normed * hat, axis=0, keepdims=True)
    gain_grads[1:2, :] = mix_grad[...]
    gain_grads[2:3, :] = feed_grad[...]
    gain_grads[3:4, :] = final_grad[...]
    gain_grads[4:5, :width] = query_grad[...]
    input_grad[...] = d_after[...] + unit_back(hat, inverse, d_normed * (1.0 + gains[0:1, :]))
    model = normed.shape[1]
    piece = width // 4
    span = 2 * lanes
    line = lax.broadcasted_iota(jnp.int32, (model, span), 0)
    column = lax.broadcasted_iota(jnp.int32, (model, span), 1)
    values = gain_grads[...].astype(bf16)
    base = (2 * width // lanes) * rows
    for slot, step in enumerate(order):
        target = keep if slot < 2 else send
        owner = index ^ step
        spots = (line == column + owner * rows) & (column < rows)
        wide_part = nn(values, spots.astype(f32).astype(bf16)).astype(bf16)
        spots = (line == column + owner * piece) & (column < piece)
        head_part = nn(values, spots.astype(f32).astype(bf16)).astype(bf16)
        begin = base
        for part in (wide_part[:, :lanes], wide_part[:, lanes:], head_part[:, :lanes]):
            target[slot % 2, begin : begin + gain_pad, :] = part
            begin += gain_pad
        target[slot % 2, begin:, :] = jnp.zeros((target.shape[1] - begin, lanes), bf16)


def unpack_kernel(widths, rows_of, pack, *outs):
    base = 0
    for out, width, rows in zip(outs, widths, rows_of):
        for number in range(width // lanes):
            out[:, number * lanes : (number + 1) * lanes] = pack[
                base : base + rows, :
            ].astype(f32)
            base += rows


def flip(value, axis, bit):
    size = lax.axis_size(axis)
    return lax.ppermute(value, axis, [(i, i ^ bit) for i in range(size)])


def pair_up(shard, far):
    both = jnp.concatenate([shard, far], axis=0)
    return both, flip(both, "fsdp", 1)


def add_low(*values):
    total = values[0].astype(f32)
    for value in values[1:]:
        total = total + value.astype(f32)
    return total.astype(bf16)


def take_half(value, which):
    half = value.shape[0] // 2
    return lax.dynamic_slice_in_dim(value, which * half, half, 0)


def send_far(keep, near):
    return add_low(keep[1], near[1])


def add_far(keep, near, far):
    return add_low(keep[0], near[0], far)


def ctx_bits():
    return [1 << i for i in range(lax.axis_size("ctx").bit_length() - 1)]


def scatter_ctx(value, bits=None):
    me = lax.axis_index("ctx")
    for bit in ctx_bits() if bits is None else bits:
        mine = (me // bit) % 2
        sent = flip(take_half(value, 1 - mine), "ctx", bit)
        value = add_low(take_half(value, mine), sent)
    return value


def gather_ctx(value):
    me = lax.axis_index("ctx")
    for bit in reversed(ctx_bits()):
        mine = (me // bit) % 2
        other = flip(value, "ctx", bit)
        low = jnp.where(mine == 0, value, other)
        high = jnp.where(mine == 0, other, value)
        value = jnp.concatenate([low, high], axis=0)
    return value


def send_on(value, shift, groups):
    return lax.ppermute(value, "ctx", [(i, i + shift) for i in range(groups - shift)])


def send_back(value, shift, groups):
    return lax.ppermute(value, "ctx", [(i + shift, i) for i in range(groups - shift)])


def on_device(
    hidden_in, positions, query_weight, key_weight, value_weight, output_weight, gate_weight,
    up_weight, down_weight, input_gain, mixer_gain, feed_gain, final_gain, query_gain, key_gain,
    out_grad,
):
    tokens = hidden_in.shape[1]
    model = hidden_in.shape[2]
    rows = key_weight.shape[0]
    head_dim = key_weight.shape[1]
    wide = query_weight.shape[1]
    heads = wide // head_dim
    feed = gate_weight.shape[1]
    mixed_rows = output_weight.shape[0]
    down_rows = down_weight.shape[0]
    me = lax.axis_index("fsdp")
    ctx = lax.axis_index("ctx")
    groups = lax.axis_size("ctx")
    first_row = ctx * tokens

    gains = jnp.zeros((gain_pad, 2 * head_dim), bf16)
    shards = (input_gain, mixer_gain, feed_gain, final_gain, query_gain, key_gain)
    for number, gain in enumerate(shards):
        gains = gains + jnp.pad(
            gain[None], ((number, gain_pad - 1 - number), (0, 2 * head_dim - gain.shape[0]))
        )
    both_shard = jnp.concatenate(
        [jnp.concatenate([key_weight, value_weight], axis=1), gains], axis=0
    )
    far_both = flip(both_shard, "fsdp", 2)
    far_query = flip(query_weight, "fsdp", 2)
    both_blocks = pair_up(both_shard, far_both)
    feed_pair = jnp.concatenate([gate_weight, up_weight], axis=1)

    hidden = hidden_in[0]
    cotangent = out_grad[0]
    places = positions[0]
    place_col = places[:, None]
    place_row = places[None, :]
    half = head_dim // 2
    freqs = rope_base ** (-(jnp.arange(half, dtype=f32) * 2.0) / head_dim)
    angles = places.astype(f32)[:, None] * freqs[None, :]
    cosine, sine = jnp.cos(angles), jnp.sin(angles)

    def facts(*starts):
        return jnp.stack([me, first_row, *starts]).astype(jnp.int32)

    info = facts()
    sem = pltpu.SemaphoreType.DMA
    token_flops = 2 * tokens * model

    normed, key_raw, kv, gains = call(
        kv_kernel,
        (info, hidden, cosine, sine, *both_blocks),
        [SMEM] + [VMEM] * 3 + [ANY] * 2,
        [
            ((tokens, model), bf16),
            ((tokens, head_dim), f32),
            ((tokens, 2 * head_dim), bf16),
            ((gain_pad, model), f32),
        ],
        [
            pltpu.VMEM((model, 2 * head_dim), bf16),
            pltpu.VMEM((4 * gain_pad, 2 * head_dim), bf16),
            sem((2, 4)),
        ],
        flops=token_flops * 2 * head_dim,
        name="key_value",
    )
    far_query, kv = tie(far_query, kv)
    far_output = flip(output_weight, "fsdp", 2)

    ring = groups == 8
    if ring:
        side = ctx % 2
        stage = ctx // 2
        moved = [kv, send_on(kv, 2, groups)]
        others = [flip(kv, "ctx", 1)]
        moved[1], far_query = tie(moved[1], far_query)
        moved.append(send_on(moved[1], 2, groups))
        others.append(flip(moved[1], "ctx", 1))
    else:
        gathered = lax.all_gather(kv, "ctx", axis=0, tiled=True)
    query_blocks = pair_up(query_weight, far_query)
    query_raw, queries = call(
        query_kernel,
        (info, normed, gains, cosine, sine, *query_blocks),
        [SMEM] + [VMEM] * 4 + [ANY] * 2,
        [((tokens, wide), f32), ((tokens, wide), bf16)],
        [pltpu.VMEM((model, wide), bf16), sem((4,))],
        flops=token_flops * wide,
        name="query",
    )

    far_output, feed_pair = tie(far_output, feed_pair)
    far_feed = flip(feed_pair, "fsdp", 2)
    if ring:
        queries, moved[2] = tie(queries, moved[2])
        moved.append(send_on(moved[2], 2, groups))
        others.append(flip(moved[2], "ctx", 1))

    state = ()
    history = []
    chunk_flops = 4 * tokens * tokens * wide
    sources = []
    for number in range(groups // 2 if ring else 1):
        if ring:
            if number == 1:
                moved[3], total = tie(moved[3], state[1])
                state = (state[0], total)
                others.append(flip(moved[3], "ctx", 1))
            arrays = (moved[number], others[number])
            base = (stage - number) * 2
            starts = ((base + side) * tokens, (base + 1 - side) * tokens)
        else:
            arrays, starts = (gathered,), (jnp.int32(0),)
        sources.append((arrays, starts))
        first = number == 0
        count = len(arrays)

        def attend(*args, first=first, count=count):
            attend_kernel(first, count, *args)

        state = call(
            attend,
            (facts(*starts), queries, place_col, *arrays, *state),
            [SMEM] + [VMEM] * (2 + count + len(state)),
            [((tokens, wide), f32), ((tokens, heads * lanes), f32)],
            flops=chunk_flops * 2,
            limit=vmem_bytes if ring else 3 * vmem_bytes,
            name="attend",
        )
        history.append(state[1])
    weighted, total = state
    far_output, total, far_feed, down_weight = tie(far_output, total, far_feed, down_weight)
    output_blocks = pair_up(output_weight, far_output)
    feed_blocks = pair_up(feed_pair, far_feed)
    far_down = flip(down_weight, "fsdp", 2)

    attended, mixed, projected, after, normed_feed, gate_value, up_value, activated = call(
        mix_kernel,
        (
            info, weighted, total, hidden, gains,
            *output_blocks, *feed_blocks,
        ),
        [SMEM] + [VMEM] * 4 + [ANY] * 4,
        [
            ((tokens, wide), f32),
            ((tokens, wide), bf16),
            ((tokens, model), f32),
            ((tokens, model), f32),
            ((tokens, model), bf16),
            ((tokens, feed), f32),
            ((tokens, feed), f32),
            ((tokens, feed), bf16),
        ],
        [
            pltpu.VMEM((wide, model), bf16),
            pltpu.VMEM((model, feed), bf16),
            pltpu.VMEM((model, feed), bf16),
            sem((3, 4)),
        ],
        flops=token_flops * (wide + 2 * feed),
        name="mix",
    )
    far_down, mixed = tie(far_down, mixed)
    down_blocks = pair_up(down_weight, far_down)
    feed_rows = 2 * (feed // lanes) * rows + (model // lanes) * down_rows
    hidden_out, d_gate, d_up, grad_final, feed_keep, feed_send = call(
        feed_kernel,
        (
            info, activated, gate_value, up_value, normed_feed, after, cotangent, gains,
            *down_blocks,
        ),
        [SMEM] + [VMEM] * 7 + [ANY] * 2,
        [
            ((tokens, model), bf16),
            ((tokens, feed), bf16),
            ((tokens, feed), bf16),
            ((1, model), f32),
            ((2, feed_rows, lanes), bf16),
            ((2, feed_rows, lanes), bf16),
        ],
        [
            pltpu.VMEM((feed, model), bf16),
            pltpu.VMEM((tokens, model), bf16),
            pltpu.VMEM((model, tokens), bf16),
            sem((4,)),
        ],
        flops=token_flops * 5 * feed,
        name="feed",
    )
    feed_near = flip(feed_send, "fsdp", 1)

    d_after, d_projected, d_mixed, table, grad_feed_gain, grad_mix_gain = call(
        feed_back_kernel,
        (
            info, d_gate, d_up, after, projected, attended, total, cotangent, gains,
            *feed_blocks, *output_blocks,
        ),
        [SMEM] + [VMEM] * 8 + [ANY] * 4,
        [
            ((tokens, model), f32),
            ((tokens, model), bf16),
            ((tokens, wide), bf16),
            ((2 * heads, tokens), f32),
            ((1, model), f32),
            ((1, model), f32),
        ],
        [
            pltpu.VMEM((model, feed), bf16),
            pltpu.VMEM((model, feed), bf16),
            pltpu.VMEM((wide, model), bf16),
            pltpu.VMEM((tokens, model), f32),
            sem((3, 4)),
        ],
        flops=token_flops * (2 * feed + wide),
        name="feed_back",
    )

    feed_near, d_mixed = tie(feed_near, d_mixed)
    gate_rows = (feed // lanes) * rows
    cuts = (0, gate_rows, feed_rows)
    feed_sums = [
        add_low(feed_keep[1, i:j], feed_near[1, i:j]) for i, j in zip(cuts[:-1], cuts[1:])
    ]
    d_mixed, *feed_sums = tie(d_mixed, *feed_sums)
    gate_far = flip(feed_sums[0], "fsdp", 2)

    query_grads = ()
    arrived = []
    waiting = None
    last = len(sources) - 1
    for number, (arrays, starts) in enumerate(reversed(sources)):
        first = number == 0
        count = len(arrays)

        def attend_back(*args, first=first, count=count):
            attend_back_kernel(first, count, *args)

        results = call(
            attend_back,
            (facts(*starts), queries, d_mixed, table, place_row, *arrays, *query_grads),
            [SMEM] + [VMEM] * (4 + count + len(query_grads)),
            [((tokens, wide), f32)] + [(a.shape, bf16) for a in arrays],
            [pltpu.VMEM((tokens, head_dim), f32), pltpu.VMEM((tokens, head_dim), f32)],
            flops=chunk_flops * 5,
            limit=vmem_bytes if ring else 3 * vmem_bytes,
            name="attend_back",
        )
        query_grads = results[:1]
        if not ring:
            arrived.append(
                lax.psum_scatter(results[1], "ctx", scatter_dimension=0, tiled=True)
            )
            continue
        shift = last - number
        own, other = results[1:]
        if waiting is not None:
            crossed, held, *arrived = tie(waiting[1], query_grads[0], *arrived)
            query_grads = (held,)
            arrived = [send_back(add_low(waiting[0], crossed, *arrived), 2, groups)]
        waiting = (own, flip(other, "ctx", 1))
    if ring:
        arrived += list(waiting)
    held, gate_far, feed_sums[1] = tie(query_grads[0], gate_far, feed_sums[1])
    query_grads = (held,)
    rest_far = flip(feed_sums[1], "fsdp", 2)

    query_rows = (wide // lanes) * rows
    output_rows = (model // lanes) * mixed_rows
    d_normed_query, grad_query_gain, query_keep, query_send = call(
        query_back_kernel,
        (
            info, query_grads[0], query_raw, cosine, sine, gains, normed, mixed, d_projected,
            *query_blocks,
        ),
        [SMEM] + [VMEM] * 8 + [ANY] * 2,
        [
            ((tokens, model), f32),
            ((1, head_dim), f32),
            ((2, query_rows + output_rows, lanes), bf16),
            ((2, query_rows + output_rows, lanes), bf16),
        ],
        [
            pltpu.VMEM((model, wide), bf16),
            pltpu.VMEM((tokens, wide), bf16),
            pltpu.VMEM((model, tokens), bf16),
            sem((4,)),
        ],
        flops=token_flops * 3 * wide,
        name="query_back",
    )
    d_normed_query, gate_far = tie(d_normed_query, gate_far)
    query_near = flip(query_send, "fsdp", 1)
    query_sum = add_low(query_keep[1], query_near[1])

    def feed_part(number, far):
        part = slice(cuts[number], cuts[number + 1])
        return add_low(feed_keep[0, part], feed_near[0, part], far)

    bits = ctx_bits()
    gate_part = scatter_ctx(feed_part(0, gate_far), bits[:1])
    d_after, query_sum, gate_part = tie(d_after, query_sum, gate_part)

    both_rows = (2 * head_dim // lanes) * rows + lanes
    arrived_count = len(arrived)

    def key_back(*args):
        key_back_kernel(arrived_count, *args)

    grad_input, both_keep, both_send = call(
        key_back,
        (
            info, cosine, sine, gains, key_raw, normed, hidden, d_after,
            d_normed_query, grad_mix_gain, grad_feed_gain, grad_final, grad_query_gain,
            *both_blocks, *arrived,
        ),
        [SMEM] + [VMEM] * 12 + [ANY] * 2 + [VMEM] * arrived_count,
        [
            ((tokens, model), f32),
            ((2, both_rows, lanes), bf16),
            ((2, both_rows, lanes), bf16),
        ],
        [
            pltpu.VMEM((model, 2 * head_dim), bf16),
            pltpu.VMEM((tokens, 2 * head_dim), bf16),
            pltpu.VMEM((model, tokens), bf16),
            pltpu.VMEM((gain_pad, model), f32),
            sem((4,)),
        ],
        flops=token_flops * 4 * head_dim,
        name="key_back",
    )
    both_send, query_sum, rest_far, gate_part = tie(both_send, query_sum, rest_far, gate_part)
    query_far = flip(query_sum, "fsdp", 2)
    both_near = flip(both_send, "fsdp", 1)
    both_far = flip(add_low(both_keep[1], both_near[1]), "fsdp", 2)

    def unpack(pack, shapes):
        def kernel(*args):
            unpack_kernel([s[1] for s in shapes], [s[0] for s in shapes], *args)

        return call(kernel, (pack,), [VMEM], [(s, f32) for s in shapes], name="unpack")

    gate_part = scatter_ctx(gate_part, bits[1:])
    query_part = scatter_ctx(add_low(query_keep[0], query_near[0], query_far))
    rest = feed_part(1, rest_far)
    up_part = scatter_ctx(rest[:gate_rows])
    down_part = scatter_ctx(rest[gate_rows:])
    both_part = scatter_ctx(add_low(both_keep[0], both_near[0], both_far))
    (grad_gate,) = unpack(gather_ctx(gate_part), [gate_weight.shape])
    (grad_up,) = unpack(gather_ctx(up_part), [up_weight.shape])
    grad_query, grad_output = unpack(
        gather_ctx(query_part), [query_weight.shape, output_weight.shape]
    )
    (grad_down,) = unpack(gather_ctx(down_part), [down_weight.shape])
    grad_key, grad_value, wide_gains, head_gains = unpack(
        gather_ctx(both_part),
        [key_weight.shape, value_weight.shape, (gain_pad, 2 * lanes), (gain_pad, lanes)],
    )
    gain_shards = [wide_gains[i, :rows] for i in range(4)]
    gain_shards += [head_gains[i, : query_gain.shape[0]] for i in (4, 5)]
    return (
        hidden_out[None],
        grad_input[None],
        grad_query,
        grad_key,
        grad_value,
        grad_output,
        grad_gate,
        grad_up,
        grad_down,
        *gain_shards,
    )


def solution(mesh):
    token = P("fsdp", "ctx", None)
    weight = P("fsdp", None)
    gain = P("fsdp")
    return jax.shard_map(
        on_device,
        mesh=mesh,
        in_specs=(token, P("fsdp", "ctx")) + (weight,) * 7 + (gain,) * 6 + (token,),
        out_specs=(token, token) + (weight,) * 7 + (gain,) * 6,
        check_vma=False,
    )
```

```python
import jax
import jax.numpy as jnp
from jax import lax
from jax.experimental import pallas as pl
from jax.experimental.pallas import tpu as pltpu
from jax.sharding import PartitionSpec as P

eps = 1e-06
rope_base = 1000000.0
lanes = 128
order = (0, 2, 1, 3)
vmem_bytes = 16 * 1024 * 1024
gain_pad = 16
f32 = jnp.float32
bf16 = jnp.bfloat16

ANY = pl.BlockSpec(memory_space=pl.ANY)
SMEM = pl.BlockSpec(memory_space=pltpu.SMEM)
VMEM = pl.BlockSpec(memory_space=pltpu.VMEM)


def tie(*values):
    return lax.optimization_barrier(values)


def call(kernel, inputs, specs, outs, scratch=(), flops=0, limit=vmem_bytes, name=None):
    return pl.pallas_call(
        kernel,
        out_shape=tuple(jax.ShapeDtypeStruct(s, d) for s, d in outs),
        in_specs=list(specs),
        out_specs=tuple(VMEM for _ in outs),
        scratch_shapes=list(scratch),
        compiler_params=pltpu.CompilerParams(vmem_limit_bytes=limit),
        cost_estimate=pl.CostEstimate(flops=1, bytes_accessed=1, transcendentals=0),
        name=name,
    )(*inputs)


def nn(left, right):
    return lax.dot_general(left, right, (((1,), (0,)), ((), ())), preferred_element_type=f32)


def nt(left, right):
    return lax.dot_general(left, right, (((1,), (1,)), ((), ())), preferred_element_type=f32)


def tn(left, right):
    return lax.dot_general(left, right, (((0,), (0,)), ((), ())), preferred_element_type=f32)


def unit(value):
    inverse = lax.rsqrt(jnp.mean(value * value, axis=-1, keepdims=True) + eps)
    return value * inverse, inverse


def unit_back(hat, inverse, grad_hat):
    return inverse * (grad_hat - hat * jnp.mean(grad_hat * hat, axis=-1, keepdims=True))


def spin(value, cosine, sine):
    half = value.shape[-1] // 2
    first, second = value[:, :half], value[:, half:]
    return jnp.concatenate(
        [first * cosine - second * sine, second * cosine + first * sine], axis=-1
    )


def place(index, pairs, full, sems, columns=None):
    rows = full.shape[0] // 4
    pitch = pairs[0].shape[0] // 2
    copies = []
    for step in range(4):
        begin = pl.multiple_of((index ^ step) * rows, 16)
        source = pairs[step % 2].at[pl.ds((step // 2) * pitch, rows)]
        if columns is not None:
            source = source.at[:, pl.ds(columns, full.shape[1])]
        copy = pltpu.make_async_copy(source, full.at[pl.ds(begin, rows)], sems.at[step])
        copy.start()
        copies.append(copy)
    return copies


def finish(copies):
    for copy in copies:
        copy.wait()


def kv_kernel(
    info, hidden, cosine, sine,
    b0, b1,
    normed_out, key_raw_out, kv_out, gains_out,
    both_full, gain_parts, sems,
):
    index = info[0]
    copies = place(index, (b0, b1), both_full, sems.at[0])
    model = hidden.shape[1]
    rows = model // 4
    width = key_raw_out.shape[1]
    piece = width // 4
    gain_copies = []
    for step in range(4):
        begin = pl.multiple_of((index ^ step) * gain_pad, gain_pad)
        source = (b0, b1)[step % 2].at[pl.ds((step // 2) * (rows + gain_pad) + rows, gain_pad)]
        copy = pltpu.make_async_copy(
            source, gain_parts.at[pl.ds(begin, gain_pad)], sems.at[1, step]
        )
        copy.start()
        gain_copies.append(copy)
    hat, _ = unit(hidden[...].astype(f32))
    finish(gain_copies)
    span = 2 * lanes
    line = lax.broadcasted_iota(jnp.int32, (span, model), 0)
    column = lax.broadcasted_iota(jnp.int32, (span, model), 1)
    wide_gain = jnp.zeros((gain_pad, model), f32)
    head_gain = jnp.zeros((gain_pad, model), f32)
    for owner in range(4):
        values = gain_parts[owner * gain_pad : (owner + 1) * gain_pad, :span]
        spots = (column == line + owner * rows) & (line < rows)
        wide_gain += nn(values, spots.astype(f32).astype(bf16))
        spots = (column == line + owner * piece) & (line < piece)
        head_gain += nn(values, spots.astype(f32).astype(bf16))
    which = lax.broadcasted_iota(jnp.int32, (gain_pad, model), 0)
    gains = jnp.where(which < 4, wide_gain, head_gain)
    gains_out[...] = gains
    normed = (hat * (1.0 + gains[0:1, :])).astype(bf16)
    normed_out[...] = normed
    finish(copies)
    raw = nn(normed, both_full[:, :width])
    key_raw_out[...] = raw
    hat, _ = unit(raw)
    scale = 1.0 + gains[5:6, :width]
    kv_out[:, :width] = spin(hat * scale, cosine[...], sine[...]).astype(bf16)
    kv_out[:, width:] = nn(normed, both_full[:, width:]).astype(bf16)


def query_kernel(
    info, normed, gains, cosine, sine, q0, q1,
    raw_out, query_out, query_full, sems,
):
    finish(place(info[0], (q0, q1), query_full, sems))
    head_dim = 2 * cosine.shape[1]
    for start in range(0, query_full.shape[1], head_dim):
        part = slice(start, start + head_dim)
        raw = nn(normed[...], query_full[:, part])
        raw_out[:, part] = raw
        hat, _ = unit(raw)
        turned = spin(hat * (1.0 + gains[4:5, :head_dim]), cosine[...], sine[...])
        query_out[:, part] = (turned * head_dim ** (-0.5)).astype(bf16)


def attend_kernel(first, count, info, queries, places, *refs):
    chunks = refs[:count]
    refs = refs[count:]
    if not first:
        weighted_in, total_in = refs[:2]
        refs = refs[2:]
    weighted, total = refs
    tokens = queries.shape[0]
    head_dim = chunks[0].shape[1] // 2
    heads = queries.shape[1] // head_dim
    if first:
        weighted[...] = jnp.zeros_like(weighted)
        total[...] = jnp.zeros_like(total)
    else:
        weighted[...] = weighted_in[...]
        total[...] = total_in[...]
    first_row = info[1]
    for number, chunk in enumerate(chunks):
        base = info[2 + number]

        @pl.loop(0, chunk.shape[0] // tokens)
        def _(step):
            start = base + step * tokens

            @pl.when((start >= 0) & (start <= first_row))
            def _():
                local = pl.ds(pl.multiple_of(step * tokens, tokens), tokens)
                row = first_row + lax.broadcasted_iota(jnp.int32, (tokens, tokens), 0)
                col = start + lax.broadcasted_iota(jnp.int32, (tokens, tokens), 1)
                allowed = (col <= row) & (col >= row - places[...])
                keys = chunk[local, :head_dim]
                values = chunk[local, head_dim:]
                for head in range(heads):
                    part = slice(head * head_dim, (head + 1) * head_dim)
                    scores = nt(queries[:, part], keys)
                    expo = jnp.where(allowed, jnp.exp(scores), 0.0)
                    spot = slice(head * lanes, (head + 1) * lanes)
                    total[:, spot] += jnp.sum(expo, axis=1, keepdims=True)
                    weighted[:, part] += nn(expo.astype(bf16), values)


def mix_kernel(
    info, weighted, total, hidden, gains,
    o0, o1, g0, g1,
    attended_out, mixed_out, projected_out, after_out, normed_out, gate_out, up_out, act_out,
    output_full, gate_full, up_full, sems,
):
    index = info[0]
    feed = gate_full.shape[1]
    output_copies = place(index, (o0, o1), output_full, sems.at[0])
    gate_copies = place(index, (g0, g1), gate_full, sems.at[1], 0)
    up_copies = place(index, (g0, g1), up_full, sems.at[2], feed)
    heads = total.shape[1] // lanes
    head_dim = weighted.shape[1] // heads
    for head in range(heads):
        part = slice(head * head_dim, (head + 1) * head_dim)
        ratio = weighted[:, part] / total[:, head * lanes : head * lanes + 1]
        attended_out[:, part] = ratio
        mixed_out[:, part] = ratio.astype(bf16)
    finish(output_copies)
    projected = nn(mixed_out[...], output_full[...])
    projected_out[...] = projected
    hat, _ = unit(projected)
    after = hidden[...].astype(f32) + hat * (1.0 + gains[1:2, :])
    after_out[...] = after
    hat, _ = unit(after)
    normed_out[...] = (hat * (1.0 + gains[2:3, :])).astype(bf16)
    finish(gate_copies)
    finish(up_copies)
    step_width = 512

    @pl.loop(0, gate_full.shape[1] // step_width)
    def _(step):
        part = pl.ds(pl.multiple_of(step * step_width, step_width), step_width)
        gate = nn(normed_out[...], gate_full[:, part])
        up = nn(normed_out[...], up_full[:, part])
        gate_out[:, part] = gate
        up_out[:, part] = up
        inner = 0.7978845608028654 * (gate + 0.044715 * gate * gate * gate)
        act_out[:, part] = (0.5 * gate * (1.0 + jnp.tanh(inner)) * up).astype(bf16)


def store_columns(keep, send, slot, base, rows, block):
    target = keep if slot < 2 else send
    for number in range(block.shape[1] // lanes):
        target[slot % 2, base + number * rows : base + (number + 1) * rows, :] = block[
            :, number * lanes : (number + 1) * lanes
        ].astype(bf16)


def feed_kernel(
    info, act, gate, up, normed, after, cotangent, gains,
    d0, d1,
    hidden_out, d_gate, d_up, gain_grad, keep, send,
    down_full, d_down, turned, sems,
):
    index = info[0]
    finish(place(index, (d0, d1), down_full, sems))
    down = nn(act[...], down_full[...])
    hat, inverse = unit(down)
    scale = 1.0 + gains[3:4, :]
    hidden_out[...] = (after[...] + hat * scale).astype(bf16)
    grad = cotangent[...].astype(f32)
    gain_grad[...] = jnp.sum(grad * hat, axis=0, keepdims=True)
    d_down[...] = unit_back(hat, inverse, grad * scale).astype(bf16)
    turned[...] = normed[...].astype(f32).T.astype(bf16)
    step_width = 512

    @pl.loop(0, down_full.shape[0] // step_width)
    def _(step):
        part = pl.ds(pl.multiple_of(step * step_width, step_width), step_width)
        d_act = nt(d_down[...], down_full[part, :])
        x = gate[:, part]
        curve = jnp.tanh(0.7978845608028654 * (x + 0.044715 * x * x * x))
        slope = 0.5 * (1.0 + curve) + 0.5 * x * (1.0 - curve * curve) * (
            0.7978845608028654 * (1.0 + 3.0 * 0.044715 * x * x)
        )
        d_gate[:, part] = (d_act * up[:, part] * slope).astype(bf16)
        d_up[:, part] = (d_act * (0.5 * x * (1.0 + curve))).astype(bf16)

    model = normed.shape[1]
    rows = model // 4
    wide = gate.shape[1]
    down_rows = wide // 4
    part_rows = (wide // lanes) * rows
    for slot, step in enumerate(order):
        target = keep if slot < 2 else send
        owner = index ^ step
        lhs = turned[pl.ds(pl.multiple_of(owner * rows, 16), rows), :]
        for base, source in ((0, d_gate), (part_rows, d_up)):

            @pl.loop(0, wide // step_width)
            def _(move):
                part = pl.ds(pl.multiple_of(move * step_width, step_width), step_width)
                block = nn(lhs, source[:, part]).astype(bf16)
                for number in range(step_width // lanes):
                    begin = base + (move * (step_width // lanes) + number) * rows
                    target[slot % 2, pl.ds(pl.multiple_of(begin, 16), rows), :] = block[
                        :, number * lanes : (number + 1) * lanes
                    ]

        left = act[:, pl.ds(pl.multiple_of(owner * down_rows, lanes), down_rows)]
        store_columns(keep, send, slot, 2 * part_rows, down_rows, tn(left, d_down[...]))


def feed_back_kernel(
    info, d_gate, d_up, after, projected, attended, total, cotangent, gains,
    g0, g1, o0, o1,
    d_after_out, d_projected_out, d_mixed_out, rows_out, feed_grad, mix_grad,
    gate_full, up_full, output_full, total_grad, sems,
):
    index = info[0]
    gate_copies = place(index, (g0, g1), gate_full, sems.at[0], 0)
    up_copies = place(index, (g0, g1), up_full, sems.at[1], gate_full.shape[1])
    output_copies = place(index, (o0, o1), output_full, sems.at[2])
    finish(gate_copies)
    total_grad[...] = nt(d_gate[...], gate_full[...])
    finish(up_copies)
    grad = total_grad[...] + nt(d_up[...], up_full[...])
    hat, inverse = unit(after[...])
    feed_grad[...] = jnp.sum(grad * hat, axis=0, keepdims=True)
    d_after = cotangent[...].astype(f32) + unit_back(hat, inverse, grad * (1.0 + gains[2:3, :]))
    d_after_out[...] = d_after
    hat, inverse = unit(projected[...])
    mix_grad[...] = jnp.sum(d_after * hat, axis=0, keepdims=True)
    d_projected = unit_back(hat, inverse, d_after * (1.0 + gains[1:2, :])).astype(bf16)
    d_projected_out[...] = d_projected
    finish(output_copies)
    d_mixed = nt(d_projected, output_full[...]).astype(bf16)
    d_mixed_out[...] = d_mixed
    heads = total.shape[1] // lanes
    head_dim = attended.shape[1] // heads
    tokens = attended.shape[0]
    lane = lax.broadcasted_iota(jnp.int32, (tokens, lanes), 1)
    table = jnp.zeros((tokens, lanes), f32)
    for head in range(heads):
        part = slice(head * head_dim, (head + 1) * head_dim)
        delta = jnp.sum(d_mixed[:, part].astype(f32) * attended[:, part], axis=1, keepdims=True)
        table = jnp.where(lane == head, delta, table)
        share = 1.0 / total[:, head * lanes : (head + 1) * lanes]
        table = jnp.where(lane == heads + head, share, table)
    rows_out[...] = table.T[: rows_out.shape[0], :]


def attend_back_kernel(first, count, info, queries, d_mixed, table, places, *refs):
    chunks = refs[:count]
    refs = refs[count:]
    if not first:
        query_in = refs[0]
        refs = refs[1:]
    query_grads = refs[0]
    chunk_grads = refs[1 : 1 + count]
    key_sum, value_sum = refs[1 + count :]
    tokens = queries.shape[0]
    head_dim = chunks[0].shape[1] // 2
    heads = queries.shape[1] // head_dim
    if first:
        query_grads[...] = jnp.zeros_like(query_grads)
    else:
        query_grads[...] = query_in[...]
    first_row = info[1]
    for number, (chunk, chunk_grad) in enumerate(zip(chunks, chunk_grads)):
        base = info[2 + number]
        chunk_grad[...] = jnp.zeros_like(chunk_grad)

        @pl.loop(0, chunk.shape[0] // tokens)
        def _(step):
            start = base + step * tokens

            @pl.when((start >= 0) & (start <= first_row))
            def _():
                local = pl.ds(pl.multiple_of(step * tokens, tokens), tokens)
                row = first_row + lax.broadcasted_iota(jnp.int32, (tokens, tokens), 1)
                col = start + lax.broadcasted_iota(jnp.int32, (tokens, tokens), 0)
                allowed = (col <= row) & (col >= row - places[...])
                keys = chunk[local, :head_dim]
                values = chunk[local, head_dim:]
                for head in range(heads):
                    part = slice(head * head_dim, (head + 1) * head_dim)
                    query = queries[:, part]
                    grad = d_mixed[:, part]
                    expo = jnp.where(allowed, jnp.exp(nt(keys, query)), 0.0)
                    probs = expo * table[heads + head : heads + head + 1, :]
                    back = nt(values, grad) - table[head : head + 1, :]
                    d_scores = (probs * back).astype(bf16)
                    d_value = nn(probs.astype(bf16), grad)
                    d_key = nn(d_scores, query)
                    if head == 0:
                        key_sum[...] = d_key
                        value_sum[...] = d_value
                    else:
                        key_sum[...] += d_key
                        value_sum[...] += d_value
                    query_grads[:, part] += tn(d_scores, keys)
                chunk_grad[local, :head_dim] = key_sum[...].astype(bf16)
                chunk_grad[local, head_dim:] = value_sum[...].astype(bf16)


def unspin(value, cosine, sine):
    half = value.shape[-1] // 2
    first, second = value[:, :half], value[:, half:]
    return jnp.concatenate(
        [first * cosine + second * sine, second * cosine - first * sine], axis=-1
    )


def query_back_kernel(
    info, query_grads, raw, cosine, sine, gains, normed, mixed, d_projected,
    q0, q1,
    d_normed_out, gain_grad, keep, send,
    query_full, d_raw, turned, sems,
):
    index = info[0]
    copies = place(index, (q0, q1), query_full, sems)
    head_dim = 2 * cosine.shape[1]
    wide = raw.shape[1]
    scale = 1.0 + gains[4:5, :head_dim]
    gain_sum = jnp.zeros((1, head_dim), f32)
    for start in range(0, wide, head_dim):
        part = slice(start, start + head_dim)
        hat, inverse = unit(raw[:, part])
        grad = unspin(query_grads[:, part] * head_dim ** (-0.5), cosine[...], sine[...])
        gain_sum += jnp.sum(grad * hat, axis=0, keepdims=True)
        d_raw[:, part] = unit_back(hat, inverse, grad * scale).astype(bf16)
    gain_grad[...] = gain_sum
    turned[...] = normed[...].astype(f32).T.astype(bf16)
    rows = normed.shape[1] // 4
    mixed_rows = mixed.shape[1] // 4
    for slot, step in enumerate(order):
        owner = index ^ step
        lhs = turned[pl.ds(pl.multiple_of(owner * rows, 16), rows), :]
        store_columns(keep, send, slot, 0, rows, nn(lhs, d_raw[...]))
        left = mixed[:, pl.ds(pl.multiple_of(owner * mixed_rows, lanes), mixed_rows)]
        store_columns(
            keep, send, slot, (wide // lanes) * rows, mixed_rows, tn(left, d_projected[...])
        )
    finish(copies)
    d_normed_out[...] = nt(d_raw[...], query_full[...])


def key_back_kernel(
    count, info, cosine, sine, gains, raw, normed, hidden, d_after, d_normed_query,
    mix_grad, feed_grad, final_grad, query_grad, b0, b1, *refs,
):
    parts = refs[:count]
    (
        input_grad, keep, send,
        both_full, d_both, turned, gain_grads, sems,
    ) = refs[count:]
    index = info[0]
    copies = place(index, (b0, b1), both_full, sems)
    width = raw.shape[1]
    both = parts[0][...].astype(f32)
    for piece in parts[1:]:
        both = both + piece[...].astype(f32)
    hat, inverse = unit(raw[...])
    grad = unspin(both[:, :width], cosine[...], sine[...])
    gain_grads[...] = jnp.zeros_like(gain_grads)
    gain_grads[5:6, :width] = jnp.sum(grad * hat, axis=0, keepdims=True)
    d_both[:, :width] = unit_back(hat, inverse, grad * (1.0 + gains[5:6, :width])).astype(bf16)
    d_both[:, width:] = both[:, width:].astype(bf16)
    turned[...] = normed[...].astype(f32).T.astype(bf16)
    rows = normed.shape[1] // 4
    for slot, step in enumerate(order):
        owner = index ^ step
        lhs = turned[pl.ds(pl.multiple_of(owner * rows, 16), rows), :]
        store_columns(keep, send, slot, 0, rows, nn(lhs, d_both[...]))
    finish(copies)
    d_normed = d_normed_query[...] + nt(d_both[...], both_full[...])
    hat, inverse = unit(hidden[...].astype(f32))
    gain_grads[0:1, :] = jnp.sum(d_normed * hat, axis=0, keepdims=True)
    gain_grads[1:2, :] = mix_grad[...]
    gain_grads[2:3, :] = feed_grad[...]
    gain_grads[3:4, :] = final_grad[...]
    gain_grads[4:5, :width] = query_grad[...]
    input_grad[...] = d_after[...] + unit_back(hat, inverse, d_normed * (1.0 + gains[0:1, :]))
    model = normed.shape[1]
    piece = width // 4
    span = 2 * lanes
    line = lax.broadcasted_iota(jnp.int32, (model, span), 0)
    column = lax.broadcasted_iota(jnp.int32, (model, span), 1)
    values = gain_grads[...].astype(bf16)
    base = (2 * width // lanes) * rows
    for slot, step in enumerate(order):
        target = keep if slot < 2 else send
        owner = index ^ step
        spots = (line == column + owner * rows) & (column < rows)
        wide_part = nn(values, spots.astype(f32).astype(bf16)).astype(bf16)
        spots = (line == column + owner * piece) & (column < piece)
        head_part = nn(values, spots.astype(f32).astype(bf16)).astype(bf16)
        begin = base
        for part in (wide_part[:, :lanes], wide_part[:, lanes:], head_part[:, :lanes]):
            target[slot % 2, begin : begin + gain_pad, :] = part
            begin += gain_pad
        target[slot % 2, begin:, :] = jnp.zeros((target.shape[1] - begin, lanes), bf16)


def unpack_kernel(shapes, count, *refs):
    packs, outs = refs[:count], refs[count:]
    number, base = 0, 0
    for out, (rows, width) in zip(outs, shapes):
        for start in range(0, width, lanes):
            if base == packs[number].shape[0]:
                number, base = number + 1, 0
            out[:, start : start + lanes] = packs[number][base : base + rows, :].astype(f32)
            base += rows


def flip(value, axis, bit):
    size = lax.axis_size(axis)
    return lax.ppermute(value, axis, [(i, i ^ bit) for i in range(size)])


def pair_up(shard, far):
    both = jnp.concatenate([shard, far], axis=0)
    return both, flip(both, "fsdp", 1)


def add_low(*values):
    total = values[0].astype(f32)
    for value in values[1:]:
        total = total + value.astype(f32)
    return total.astype(bf16)


def take_half(value, which):
    half = value.shape[0] // 2
    return lax.dynamic_slice_in_dim(value, which * half, half, 0)


def send_far(keep, near):
    return add_low(keep[1], near[1])


def add_far(keep, near, far):
    return add_low(keep[0], near[0], far)


def ctx_bits():
    return [1 << i for i in range(lax.axis_size("ctx").bit_length() - 1)]


def scatter_step(value, bit):
    mine = (lax.axis_index("ctx") // bit) % 2
    sent = flip(take_half(value, 1 - mine), "ctx", bit)
    return add_low(take_half(value, mine), sent)


def gather_step(value, bit):
    mine = (lax.axis_index("ctx") // bit) % 2
    other = flip(value, "ctx", bit)
    low = jnp.where(mine == 0, value, other)
    high = jnp.where(mine == 0, other, value)
    return jnp.concatenate([low, high], axis=0)


def send_on(value, shift, groups):
    return lax.ppermute(value, "ctx", [(i, i + shift) for i in range(groups - shift)])


def send_back(value, shift, groups):
    return lax.ppermute(value, "ctx", [(i + shift, i) for i in range(groups - shift)])


def on_device(
    hidden_in, positions, query_weight, key_weight, value_weight, output_weight, gate_weight,
    up_weight, down_weight, input_gain, mixer_gain, feed_gain, final_gain, query_gain, key_gain,
    out_grad,
):
    tokens = hidden_in.shape[1]
    model = hidden_in.shape[2]
    rows = key_weight.shape[0]
    head_dim = key_weight.shape[1]
    wide = query_weight.shape[1]
    heads = wide // head_dim
    feed = gate_weight.shape[1]
    mixed_rows = output_weight.shape[0]
    down_rows = down_weight.shape[0]
    me = lax.axis_index("fsdp")
    ctx = lax.axis_index("ctx")
    groups = lax.axis_size("ctx")
    first_row = ctx * tokens

    gains = jnp.zeros((gain_pad, 2 * head_dim), bf16)
    shards = (input_gain, mixer_gain, feed_gain, final_gain, query_gain, key_gain)
    for number, gain in enumerate(shards):
        gains = gains + jnp.pad(
            gain[None], ((number, gain_pad - 1 - number), (0, 2 * head_dim - gain.shape[0]))
        )
    both_shard = jnp.concatenate(
        [jnp.concatenate([key_weight, value_weight], axis=1), gains], axis=0
    )
    far_both = flip(both_shard, "fsdp", 2)
    far_query = flip(query_weight, "fsdp", 2)
    both_blocks = pair_up(both_shard, far_both)
    feed_pair = jnp.concatenate([gate_weight, up_weight], axis=1)

    hidden = hidden_in[0]
    cotangent = out_grad[0]
    places = positions[0]
    place_col = places[:, None]
    place_row = places[None, :]
    half = head_dim // 2
    freqs = rope_base ** (-(jnp.arange(half, dtype=f32) * 2.0) / head_dim)
    angles = places.astype(f32)[:, None] * freqs[None, :]
    cosine, sine = jnp.cos(angles), jnp.sin(angles)

    def facts(*starts):
        return jnp.stack([me, first_row, *starts]).astype(jnp.int32)

    info = facts()
    sem = pltpu.SemaphoreType.DMA
    token_flops = 2 * tokens * model

    normed, key_raw, kv, gains = call(
        kv_kernel,
        (info, hidden, cosine, sine, *both_blocks),
        [SMEM] + [VMEM] * 3 + [ANY] * 2,
        [
            ((tokens, model), bf16),
            ((tokens, head_dim), f32),
            ((tokens, 2 * head_dim), bf16),
            ((gain_pad, model), f32),
        ],
        [
            pltpu.VMEM((model, 2 * head_dim), bf16),
            pltpu.VMEM((4 * gain_pad, 2 * head_dim), bf16),
            sem((2, 4)),
        ],
        flops=token_flops * 2 * head_dim,
        name="key_value",
    )
    far_query, kv = tie(far_query, kv)
    far_output = flip(output_weight, "fsdp", 2)

    ring = groups == 8
    if ring:
        side = ctx % 2
        stage = ctx // 2
        moved = [kv, send_on(kv, 2, groups)]
        others = [flip(kv, "ctx", 1)]
        moved[1], far_query = tie(moved[1], far_query)
        moved.append(send_on(moved[1], 2, groups))
        others.append(flip(moved[1], "ctx", 1))
    else:
        gathered = lax.all_gather(kv, "ctx", axis=0, tiled=True)
    query_blocks = pair_up(query_weight, far_query)
    query_raw, queries = call(
        query_kernel,
        (info, normed, gains, cosine, sine, *query_blocks),
        [SMEM] + [VMEM] * 4 + [ANY] * 2,
        [((tokens, wide), f32), ((tokens, wide), bf16)],
        [pltpu.VMEM((model, wide), bf16), sem((4,))],
        flops=token_flops * wide,
        name="query",
    )

    far_output, feed_pair, queries = tie(far_output, feed_pair, queries)
    far_feed = flip(feed_pair, "fsdp", 2)
    output_blocks = pair_up(output_weight, far_output)
    if ring:
        queries, moved[2], others[1] = tie(queries, moved[2], others[1])
        moved.append(send_on(moved[2], 2, groups))
        others.append(flip(moved[2], "ctx", 1))

    state = ()
    chunk_flops = 4 * tokens * tokens * wide
    sources = []
    for number in range(groups // 2 if ring else 1):
        if ring:
            if number == 1:
                moved[3], others[2], total = tie(moved[3], others[2], state[1])
                state = (state[0], total)
                others.append(flip(moved[3], "ctx", 1))
            if number == 2:
                total, output_blocks = tie(state[1], output_blocks)
                state = (state[0], total)
            if number == groups // 2 - 1:
                far_feed, down_weight, total = tie(far_feed, down_weight, state[1])
                state = (state[0], total)
            arrays = (moved[number], others[number])
            base = (stage - number) * 2
            starts = ((base + side) * tokens, (base + 1 - side) * tokens)
        else:
            arrays, starts = (gathered,), (jnp.int32(0),)
        sources.append((arrays, starts))
        first = number == 0
        count = len(arrays)

        def attend(*args, first=first, count=count):
            attend_kernel(first, count, *args)

        state = call(
            attend,
            (facts(*starts), queries, place_col, *arrays, *state),
            [SMEM] + [VMEM] * (2 + count + len(state)),
            [((tokens, wide), f32), ((tokens, heads * lanes), f32)],
            flops=chunk_flops * 2,
            limit=vmem_bytes if ring else 3 * vmem_bytes,
            name="attend",
        )
    weighted, total = state
    if not ring:
        total, far_feed, down_weight = tie(total, far_feed, down_weight)
    feed_blocks = pair_up(feed_pair, far_feed)
    far_down = flip(down_weight, "fsdp", 2)

    attended, mixed, projected, after, normed_feed, gate_value, up_value, activated = call(
        mix_kernel,
        (
            info, weighted, total, hidden, gains,
            *output_blocks, *feed_blocks,
        ),
        [SMEM] + [VMEM] * 4 + [ANY] * 4,
        [
            ((tokens, wide), f32),
            ((tokens, wide), bf16),
            ((tokens, model), f32),
            ((tokens, model), f32),
            ((tokens, model), bf16),
            ((tokens, feed), f32),
            ((tokens, feed), f32),
            ((tokens, feed), bf16),
        ],
        [
            pltpu.VMEM((wide, model), bf16),
            pltpu.VMEM((model, feed), bf16),
            pltpu.VMEM((model, feed), bf16),
            sem((3, 4)),
        ],
        flops=token_flops * (wide + 2 * feed),
        name="mix",
    )
    far_down, mixed = tie(far_down, mixed)
    down_blocks = pair_up(down_weight, far_down)
    feed_rows = 2 * (feed // lanes) * rows + (model // lanes) * down_rows
    hidden_out, d_gate, d_up, grad_final, feed_keep, feed_send = call(
        feed_kernel,
        (
            info, activated, gate_value, up_value, normed_feed, after, cotangent, gains,
            *down_blocks,
        ),
        [SMEM] + [VMEM] * 7 + [ANY] * 2,
        [
            ((tokens, model), bf16),
            ((tokens, feed), bf16),
            ((tokens, feed), bf16),
            ((1, model), f32),
            ((2, feed_rows, lanes), bf16),
            ((2, feed_rows, lanes), bf16),
        ],
        [
            pltpu.VMEM((feed, model), bf16),
            pltpu.VMEM((tokens, model), bf16),
            pltpu.VMEM((model, tokens), bf16),
            sem((4,)),
        ],
        flops=token_flops * 5 * feed,
        name="feed",
    )
    feed_near = flip(feed_send, "fsdp", 1)

    d_after, d_projected, d_mixed, table, grad_feed_gain, grad_mix_gain = call(
        feed_back_kernel,
        (
            info, d_gate, d_up, after, projected, attended, total, cotangent, gains,
            *feed_blocks, *output_blocks,
        ),
        [SMEM] + [VMEM] * 8 + [ANY] * 4,
        [
            ((tokens, model), f32),
            ((tokens, model), bf16),
            ((tokens, wide), bf16),
            ((2 * heads, tokens), f32),
            ((1, model), f32),
            ((1, model), f32),
        ],
        [
            pltpu.VMEM((model, feed), bf16),
            pltpu.VMEM((model, feed), bf16),
            pltpu.VMEM((wide, model), bf16),
            pltpu.VMEM((tokens, model), f32),
            sem((3, 4)),
        ],
        flops=token_flops * (2 * feed + wide),
        name="feed_back",
    )

    feed_near, d_mixed = tie(feed_near, d_mixed)
    gate_rows = (feed // lanes) * rows
    half_rows = feed_rows // 2
    cuts = (0, half_rows, feed_rows)
    feed_sums = [
        add_low(feed_keep[1, i:j], feed_near[1, i:j]) for i, j in zip(cuts[:-1], cuts[1:])
    ]
    d_mixed, *feed_sums = tie(d_mixed, *feed_sums)
    left_far = flip(feed_sums[0], "fsdp", 2)
    right_far = flip(feed_sums[1], "fsdp", 2)

    query_grads = ()
    arrived = []
    waiting = None
    last = len(sources) - 1
    for number, (arrays, starts) in enumerate(reversed(sources)):
        first = number == 0
        count = len(arrays)

        def attend_back(*args, first=first, count=count):
            attend_back_kernel(first, count, *args)

        results = call(
            attend_back,
            (facts(*starts), queries, d_mixed, table, place_row, *arrays, *query_grads),
            [SMEM] + [VMEM] * (4 + count + len(query_grads)),
            [((tokens, wide), f32)] + [(a.shape, bf16) for a in arrays],
            [pltpu.VMEM((tokens, head_dim), f32), pltpu.VMEM((tokens, head_dim), f32)],
            flops=chunk_flops * 5,
            limit=vmem_bytes if ring else 3 * vmem_bytes,
            name="attend_back",
        )
        query_grads = results[:1]
        if not ring:
            arrived.append(
                lax.psum_scatter(results[1], "ctx", scatter_dimension=0, tiled=True)
            )
            continue
        shift = last - number
        own, other = results[1:]
        if waiting is not None:
            crossed, held, *arrived = tie(waiting[1], query_grads[0], *arrived)
            if number == last - 1:
                held, left_far = tie(held, left_far)
            query_grads = (held,)
            arrived = [send_back(add_low(waiting[0], crossed, *arrived), 2, groups)]
        waiting = (own, flip(other, "ctx", 1))
    if ring:
        arrived += list(waiting)

    query_rows = (wide // lanes) * rows
    output_rows = (model // lanes) * mixed_rows
    d_normed_query, grad_query_gain, query_keep, query_send = call(
        query_back_kernel,
        (
            info, query_grads[0], query_raw, cosine, sine, gains, normed, mixed, d_projected,
            *query_blocks,
        ),
        [SMEM] + [VMEM] * 8 + [ANY] * 2,
        [
            ((tokens, model), f32),
            ((1, head_dim), f32),
            ((2, query_rows + output_rows, lanes), bf16),
            ((2, query_rows + output_rows, lanes), bf16),
        ],
        [
            pltpu.VMEM((model, wide), bf16),
            pltpu.VMEM((tokens, wide), bf16),
            pltpu.VMEM((model, tokens), bf16),
            sem((4,)),
        ],
        flops=token_flops * 3 * wide,
        name="query_back",
    )
    arrived_count = len(arrived)
    query_near = [
        flip(query_send[:, :query_rows], "fsdp", 1),
        flip(query_send[:, query_rows:], "fsdp", 1),
    ]
    both_rows = (2 * head_dim // lanes) * rows + lanes

    def key_back(*args):
        key_back_kernel(arrived_count, *args)

    grad_input, both_keep, both_send = call(
        key_back,
        (
            info, cosine, sine, gains, key_raw, normed, hidden, d_after,
            d_normed_query, grad_mix_gain, grad_feed_gain, grad_final, grad_query_gain,
            *both_blocks, *arrived,
        ),
        [SMEM] + [VMEM] * 12 + [ANY] * 2 + [VMEM] * arrived_count,
        [
            ((tokens, model), f32),
            ((2, both_rows, lanes), bf16),
            ((2, both_rows, lanes), bf16),
        ],
        [
            pltpu.VMEM((model, 2 * head_dim), bf16),
            pltpu.VMEM((tokens, 2 * head_dim), bf16),
            pltpu.VMEM((model, tokens), bf16),
            pltpu.VMEM((gain_pad, model), f32),
            sem((4,)),
        ],
        flops=token_flops * 4 * head_dim,
        name="key_back",
    )
    both_send, right_far = tie(both_send, right_far)
    query_near = jnp.concatenate(query_near, axis=1)
    query_far = flip(add_low(query_keep[1], query_near[1]), "fsdp", 2)
    both_near = flip(both_send, "fsdp", 1)

    left = add_low(feed_keep[0, :half_rows], feed_near[0, :half_rows], left_far)
    right = add_low(feed_keep[0, half_rows:], feed_near[0, half_rows:], right_far)
    bits = ctx_bits()
    turned = bits[1:] + bits[:1]
    steps = len(bits)
    query_part = both_part = None
    for number in range(2 * steps + 2):
        if number < steps:
            left = scatter_step(left, bits[number])
            right = scatter_step(right, turned[number])
        elif number < 2 * steps:
            left = gather_step(left, bits[2 * steps - 1 - number])
            right = gather_step(right, turned[2 * steps - 1 - number])
        if number == 0:
            both_far = flip(add_low(both_keep[1], both_near[1]), "fsdp", 2)
            left, right, query_far, both_near = tie(left, right, query_far, both_near)
            query_part = add_low(query_keep[0], query_near[0], query_far)
        elif number == 1:
            query_part = scatter_step(query_part, bits[0])
            left, right, query_part, both_far = tie(left, right, query_part, both_far)
            both_part = add_low(both_keep[0], both_near[0], both_far)
        else:
            place_now = number - 1
            if place_now < steps:
                query_part = scatter_step(query_part, bits[place_now])
            elif place_now < 2 * steps:
                query_part = gather_step(query_part, bits[2 * steps - 1 - place_now])
            if number - 2 < steps:
                bit = bits[number - 2]
                both_part = add_low(both_part, flip(both_part, "ctx", bit))
            left, right, query_part, both_part = tie(left, right, query_part, both_part)

    def unpack(packs, shapes):
        def kernel(*args):
            unpack_kernel(shapes, len(packs), *args)

        specs = [VMEM] * len(packs)
        return call(kernel, packs, specs, [(s, f32) for s in shapes], name="unpack")

    grad_gate, grad_up, grad_down = unpack(
        (left, right), [gate_weight.shape, up_weight.shape, down_weight.shape]
    )
    grad_query, grad_output = unpack((query_part,), [query_weight.shape, output_weight.shape])
    grad_key, grad_value, wide_gains, head_gains = unpack(
        (both_part,),
        [key_weight.shape, value_weight.shape, (gain_pad, 2 * lanes), (gain_pad, lanes)],
    )
    gain_shards = [wide_gains[i, :rows] for i in range(4)]
    gain_shards += [head_gains[i, : query_gain.shape[0]] for i in (4, 5)]
    return (
        hidden_out[None],
        grad_input[None],
        grad_query,
        grad_key,
        grad_value,
        grad_output,
        grad_gate,
        grad_up,
        grad_down,
        *gain_shards,
    )


def solution(mesh):
    token = P("fsdp", "ctx", None)
    weight = P("fsdp", None)
    gain = P("fsdp")
    return jax.shard_map(
        on_device,
        mesh=mesh,
        in_specs=(token, P("fsdp", "ctx")) + (weight,) * 7 + (gain,) * 6 + (token,),
        out_specs=(token, token) + (weight,) * 7 + (gain,) * 6,
        check_vma=False,
    )
```

```python
import jax
import jax.numpy as jnp
from jax import lax
from jax.experimental import pallas as pl
from jax.experimental.pallas import tpu as pltpu
from jax.sharding import PartitionSpec as P

eps = 1e-06
rope_base = 1000000.0
lanes = 128
order = (0, 2, 1, 3)
vmem_bytes = 16 * 1024 * 1024
gain_pad = 16
f32 = jnp.float32
bf16 = jnp.bfloat16

ANY = pl.BlockSpec(memory_space=pl.ANY)
SMEM = pl.BlockSpec(memory_space=pltpu.SMEM)
VMEM = pl.BlockSpec(memory_space=pltpu.VMEM)


def tie(*values):
    return lax.optimization_barrier(values)


def call(kernel, inputs, specs, outs, scratch=(), flops=0, limit=vmem_bytes, name=None):
    return pl.pallas_call(
        kernel,
        out_shape=tuple(jax.ShapeDtypeStruct(s, d) for s, d in outs),
        in_specs=list(specs),
        out_specs=tuple(VMEM for _ in outs),
        scratch_shapes=list(scratch),
        compiler_params=pltpu.CompilerParams(vmem_limit_bytes=limit),
        cost_estimate=pl.CostEstimate(flops=1, bytes_accessed=1, transcendentals=0),
        name=name,
    )(*inputs)


def nn(left, right):
    return lax.dot_general(left, right, (((1,), (0,)), ((), ())), preferred_element_type=f32)


def nt(left, right):
    return lax.dot_general(left, right, (((1,), (1,)), ((), ())), preferred_element_type=f32)


def tn(left, right):
    return lax.dot_general(left, right, (((0,), (0,)), ((), ())), preferred_element_type=f32)


def unit(value):
    inverse = lax.rsqrt(jnp.mean(value * value, axis=-1, keepdims=True) + eps)
    return value * inverse, inverse


def unit_back(hat, inverse, grad_hat):
    return inverse * (grad_hat - hat * jnp.mean(grad_hat * hat, axis=-1, keepdims=True))


def spin(value, cosine, sine):
    half = value.shape[-1] // 2
    first, second = value[:, :half], value[:, half:]
    return jnp.concatenate(
        [first * cosine - second * sine, second * cosine + first * sine], axis=-1
    )


def place(index, pairs, full, sems, columns=None):
    rows = full.shape[0] // 4
    pitch = pairs[0].shape[0] // 2
    copies = []
    for step in range(4):
        begin = pl.multiple_of((index ^ step) * rows, 16)
        source = pairs[step % 2].at[pl.ds((step // 2) * pitch, rows)]
        if columns is not None:
            source = source.at[:, pl.ds(columns, full.shape[1])]
        copy = pltpu.make_async_copy(source, full.at[pl.ds(begin, rows)], sems.at[step])
        copy.start()
        copies.append(copy)
    return copies


def finish(copies):
    for copy in copies:
        copy.wait()


def kv_kernel(
    info, hidden, cosine, sine,
    b0, b1,
    normed_out, key_raw_out, kv_out, gains_out,
    both_full, gain_parts, sems,
):
    index = info[0]
    copies = place(index, (b0, b1), both_full, sems.at[0])
    model = hidden.shape[1]
    rows = model // 4
    width = key_raw_out.shape[1]
    piece = width // 4
    gain_copies = []
    for step in range(4):
        begin = pl.multiple_of((index ^ step) * gain_pad, gain_pad)
        source = (b0, b1)[step % 2].at[pl.ds((step // 2) * (rows + gain_pad) + rows, gain_pad)]
        copy = pltpu.make_async_copy(
            source, gain_parts.at[pl.ds(begin, gain_pad)], sems.at[1, step]
        )
        copy.start()
        gain_copies.append(copy)
    hat, _ = unit(hidden[...].astype(f32))
    finish(gain_copies)
    span = 2 * lanes
    line = lax.broadcasted_iota(jnp.int32, (span, model), 0)
    column = lax.broadcasted_iota(jnp.int32, (span, model), 1)
    wide_gain = jnp.zeros((gain_pad, model), f32)
    head_gain = jnp.zeros((gain_pad, model), f32)
    for owner in range(4):
        values = gain_parts[owner * gain_pad : (owner + 1) * gain_pad, :span]
        spots = (column == line + owner * rows) & (line < rows)
        wide_gain += nn(values, spots.astype(f32).astype(bf16))
        spots = (column == line + owner * piece) & (line < piece)
        head_gain += nn(values, spots.astype(f32).astype(bf16))
    which = lax.broadcasted_iota(jnp.int32, (gain_pad, model), 0)
    gains = jnp.where(which < 4, wide_gain, head_gain)
    gains_out[...] = gains
    normed = (hat * (1.0 + gains[0:1, :])).astype(bf16)
    normed_out[...] = normed
    finish(copies)
    raw = nn(normed, both_full[:, :width])
    key_raw_out[...] = raw
    hat, _ = unit(raw)
    scale = 1.0 + gains[5:6, :width]
    kv_out[:, :width] = spin(hat * scale, cosine[...], sine[...]).astype(bf16)
    kv_out[:, width:] = nn(normed, both_full[:, width:]).astype(bf16)


def query_kernel(
    info, normed, gains, cosine, sine, q0, q1,
    raw_out, query_out, query_full, sems,
):
    finish(place(info[0], (q0, q1), query_full, sems))
    head_dim = 2 * cosine.shape[1]
    for start in range(0, query_full.shape[1], head_dim):
        part = slice(start, start + head_dim)
        raw = nn(normed[...], query_full[:, part])
        raw_out[:, part] = raw
        hat, _ = unit(raw)
        turned = spin(hat * (1.0 + gains[4:5, :head_dim]), cosine[...], sine[...])
        query_out[:, part] = (turned * head_dim ** (-0.5)).astype(bf16)


def attend_kernel(first, count, info, queries, places, *refs):
    chunks = refs[:count]
    refs = refs[count:]
    if not first:
        weighted_in, total_in = refs[:2]
        refs = refs[2:]
    weighted, total = refs
    tokens = queries.shape[0]
    head_dim = chunks[0].shape[1] // 2
    heads = queries.shape[1] // head_dim
    if first:
        weighted[...] = jnp.zeros_like(weighted)
        total[...] = jnp.zeros_like(total)
    else:
        weighted[...] = weighted_in[...]
        total[...] = total_in[...]
    first_row = info[1]
    for number, chunk in enumerate(chunks):
        base = info[2 + number]

        @pl.loop(0, chunk.shape[0] // tokens)
        def _(step):
            start = base + step * tokens

            @pl.when((start >= 0) & (start <= first_row))
            def _():
                local = pl.ds(pl.multiple_of(step * tokens, tokens), tokens)
                row = first_row + lax.broadcasted_iota(jnp.int32, (tokens, tokens), 0)
                col = start + lax.broadcasted_iota(jnp.int32, (tokens, tokens), 1)
                allowed = (col <= row) & (col >= row - places[...])
                keys = chunk[local, :head_dim]
                values = chunk[local, head_dim:]
                for head in range(heads):
                    part = slice(head * head_dim, (head + 1) * head_dim)
                    scores = nt(queries[:, part], keys)
                    expo = jnp.where(allowed, jnp.exp(scores), 0.0)
                    spot = slice(head * lanes, (head + 1) * lanes)
                    total[:, spot] += jnp.sum(expo, axis=1, keepdims=True)
                    weighted[:, part] += nn(expo.astype(bf16), values)


def mix_kernel(
    info, weighted, total, hidden, gains,
    o0, o1, g0, g1,
    attended_out, mixed_out, projected_out, after_out, normed_out, gate_out, up_out, act_out,
    output_full, gate_full, up_full, sems,
):
    index = info[0]
    feed = gate_full.shape[1]
    output_copies = place(index, (o0, o1), output_full, sems.at[0])
    gate_copies = place(index, (g0, g1), gate_full, sems.at[1], 0)
    up_copies = place(index, (g0, g1), up_full, sems.at[2], feed)
    heads = total.shape[1] // lanes
    head_dim = weighted.shape[1] // heads
    for head in range(heads):
        part = slice(head * head_dim, (head + 1) * head_dim)
        ratio = weighted[:, part] / total[:, head * lanes : head * lanes + 1]
        attended_out[:, part] = ratio
        mixed_out[:, part] = ratio.astype(bf16)
    finish(output_copies)
    projected = nn(mixed_out[...], output_full[...])
    projected_out[...] = projected
    hat, _ = unit(projected)
    after = hidden[...].astype(f32) + hat * (1.0 + gains[1:2, :])
    after_out[...] = after
    hat, _ = unit(after)
    normed_out[...] = (hat * (1.0 + gains[2:3, :])).astype(bf16)
    finish(gate_copies)
    finish(up_copies)
    step_width = 512

    @pl.loop(0, gate_full.shape[1] // step_width)
    def _(step):
        part = pl.ds(pl.multiple_of(step * step_width, step_width), step_width)
        gate = nn(normed_out[...], gate_full[:, part])
        up = nn(normed_out[...], up_full[:, part])
        gate_out[:, part] = gate
        up_out[:, part] = up
        inner = 0.7978845608028654 * (gate + 0.044715 * gate * gate * gate)
        act_out[:, part] = (0.5 * gate * (1.0 + jnp.tanh(inner)) * up).astype(bf16)


def store_columns(keep, send, slot, base, rows, block):
    target = keep if slot < 2 else send
    for number in range(block.shape[1] // lanes):
        target[slot % 2, base + number * rows : base + (number + 1) * rows, :] = block[
            :, number * lanes : (number + 1) * lanes
        ].astype(bf16)


def feed_kernel(
    info, act, gate, up, normed, after, cotangent, gains,
    d0, d1,
    hidden_out, d_gate, d_up, gain_grad, keep, send,
    down_full, d_down, turned, sems,
):
    index = info[0]
    finish(place(index, (d0, d1), down_full, sems))
    down = nn(act[...], down_full[...])
    hat, inverse = unit(down)
    scale = 1.0 + gains[3:4, :]
    hidden_out[...] = (after[...] + hat * scale).astype(bf16)
    grad = cotangent[...].astype(f32)
    gain_grad[...] = jnp.sum(grad * hat, axis=0, keepdims=True)
    d_down[...] = unit_back(hat, inverse, grad * scale).astype(bf16)
    turned[...] = normed[...].astype(f32).T.astype(bf16)
    step_width = 512

    @pl.loop(0, down_full.shape[0] // step_width)
    def _(step):
        part = pl.ds(pl.multiple_of(step * step_width, step_width), step_width)
        d_act = nt(d_down[...], down_full[part, :])
        x = gate[:, part]
        curve = jnp.tanh(0.7978845608028654 * (x + 0.044715 * x * x * x))
        slope = 0.5 * (1.0 + curve) + 0.5 * x * (1.0 - curve * curve) * (
            0.7978845608028654 * (1.0 + 3.0 * 0.044715 * x * x)
        )
        d_gate[:, part] = (d_act * up[:, part] * slope).astype(bf16)
        d_up[:, part] = (d_act * (0.5 * x * (1.0 + curve))).astype(bf16)

    model = normed.shape[1]
    rows = model // 4
    wide = gate.shape[1]
    down_rows = wide // 4
    part_rows = (wide // lanes) * rows
    for slot, step in enumerate(order):
        target = keep if slot < 2 else send
        owner = index ^ step
        lhs = turned[pl.ds(pl.multiple_of(owner * rows, 16), rows), :]
        for base, source in ((0, d_gate), (part_rows, d_up)):

            @pl.loop(0, wide // step_width)
            def _(move):
                part = pl.ds(pl.multiple_of(move * step_width, step_width), step_width)
                block = nn(lhs, source[:, part]).astype(bf16)
                for number in range(step_width // lanes):
                    begin = base + (move * (step_width // lanes) + number) * rows
                    target[slot % 2, pl.ds(pl.multiple_of(begin, 16), rows), :] = block[
                        :, number * lanes : (number + 1) * lanes
                    ]

        left = act[:, pl.ds(pl.multiple_of(owner * down_rows, lanes), down_rows)]
        store_columns(keep, send, slot, 2 * part_rows, down_rows, tn(left, d_down[...]))


def feed_back_kernel(
    info, d_gate, d_up, after, projected, attended, total, cotangent, gains,
    g0, g1, o0, o1,
    d_after_out, d_projected_out, d_mixed_out, rows_out, feed_grad, mix_grad,
    gate_full, up_full, output_full, total_grad, sems,
):
    index = info[0]
    gate_copies = place(index, (g0, g1), gate_full, sems.at[0], 0)
    up_copies = place(index, (g0, g1), up_full, sems.at[1], gate_full.shape[1])
    output_copies = place(index, (o0, o1), output_full, sems.at[2])
    finish(gate_copies)
    total_grad[...] = nt(d_gate[...], gate_full[...])
    finish(up_copies)
    grad = total_grad[...] + nt(d_up[...], up_full[...])
    hat, inverse = unit(after[...])
    feed_grad[...] = jnp.sum(grad * hat, axis=0, keepdims=True)
    d_after = cotangent[...].astype(f32) + unit_back(hat, inverse, grad * (1.0 + gains[2:3, :]))
    d_after_out[...] = d_after
    hat, inverse = unit(projected[...])
    mix_grad[...] = jnp.sum(d_after * hat, axis=0, keepdims=True)
    d_projected = unit_back(hat, inverse, d_after * (1.0 + gains[1:2, :])).astype(bf16)
    d_projected_out[...] = d_projected
    finish(output_copies)
    d_mixed = nt(d_projected, output_full[...]).astype(bf16)
    d_mixed_out[...] = d_mixed
    heads = total.shape[1] // lanes
    head_dim = attended.shape[1] // heads
    tokens = attended.shape[0]
    lane = lax.broadcasted_iota(jnp.int32, (tokens, lanes), 1)
    table = jnp.zeros((tokens, lanes), f32)
    for head in range(heads):
        part = slice(head * head_dim, (head + 1) * head_dim)
        delta = jnp.sum(d_mixed[:, part].astype(f32) * attended[:, part], axis=1, keepdims=True)
        table = jnp.where(lane == head, delta, table)
        share = 1.0 / total[:, head * lanes : (head + 1) * lanes]
        table = jnp.where(lane == heads + head, share, table)
    rows_out[...] = table.T[: rows_out.shape[0], :]


def attend_back_kernel(first, count, info, queries, d_mixed, table, places, *refs):
    chunks = refs[:count]
    refs = refs[count:]
    if not first:
        query_in = refs[0]
        refs = refs[1:]
    query_grads = refs[0]
    chunk_grads = refs[1 : 1 + count]
    key_sum, value_sum = refs[1 + count :]
    tokens = queries.shape[0]
    head_dim = chunks[0].shape[1] // 2
    heads = queries.shape[1] // head_dim
    if first:
        query_grads[...] = jnp.zeros_like(query_grads)
    else:
        query_grads[...] = query_in[...]
    first_row = info[1]
    for number, (chunk, chunk_grad) in enumerate(zip(chunks, chunk_grads)):
        base = info[2 + number]
        chunk_grad[...] = jnp.zeros_like(chunk_grad)

        @pl.loop(0, chunk.shape[0] // tokens)
        def _(step):
            start = base + step * tokens

            @pl.when((start >= 0) & (start <= first_row))
            def _():
                local = pl.ds(pl.multiple_of(step * tokens, tokens), tokens)
                row = first_row + lax.broadcasted_iota(jnp.int32, (tokens, tokens), 1)
                col = start + lax.broadcasted_iota(jnp.int32, (tokens, tokens), 0)
                allowed = (col <= row) & (col >= row - places[...])
                keys = chunk[local, :head_dim]
                values = chunk[local, head_dim:]
                for head in range(heads):
                    part = slice(head * head_dim, (head + 1) * head_dim)
                    query = queries[:, part]
                    grad = d_mixed[:, part]
                    expo = jnp.where(allowed, jnp.exp(nt(keys, query)), 0.0)
                    probs = expo * table[heads + head : heads + head + 1, :]
                    back = nt(values, grad) - table[head : head + 1, :]
                    d_scores = (probs * back).astype(bf16)
                    d_value = nn(probs.astype(bf16), grad)
                    d_key = nn(d_scores, query)
                    if head == 0:
                        key_sum[...] = d_key
                        value_sum[...] = d_value
                    else:
                        key_sum[...] += d_key
                        value_sum[...] += d_value
                    query_grads[:, part] += tn(d_scores, keys)
                chunk_grad[local, :head_dim] = key_sum[...].astype(bf16)
                chunk_grad[local, head_dim:] = value_sum[...].astype(bf16)


def unspin(value, cosine, sine):
    half = value.shape[-1] // 2
    first, second = value[:, :half], value[:, half:]
    return jnp.concatenate(
        [first * cosine + second * sine, second * cosine - first * sine], axis=-1
    )


def query_back_kernel(
    info, query_grads, raw, cosine, sine, gains, normed, mixed, d_projected,
    q0, q1,
    d_normed_out, gain_grad, keep, send,
    query_full, d_raw, turned, sems,
):
    index = info[0]
    copies = place(index, (q0, q1), query_full, sems)
    head_dim = 2 * cosine.shape[1]
    wide = raw.shape[1]
    scale = 1.0 + gains[4:5, :head_dim]
    gain_sum = jnp.zeros((1, head_dim), f32)
    for start in range(0, wide, head_dim):
        part = slice(start, start + head_dim)
        hat, inverse = unit(raw[:, part])
        grad = unspin(query_grads[:, part] * head_dim ** (-0.5), cosine[...], sine[...])
        gain_sum += jnp.sum(grad * hat, axis=0, keepdims=True)
        d_raw[:, part] = unit_back(hat, inverse, grad * scale).astype(bf16)
    gain_grad[...] = gain_sum
    turned[...] = normed[...].astype(f32).T.astype(bf16)
    rows = normed.shape[1] // 4
    mixed_rows = mixed.shape[1] // 4
    for slot, step in enumerate(order):
        owner = index ^ step
        lhs = turned[pl.ds(pl.multiple_of(owner * rows, 16), rows), :]
        store_columns(keep, send, slot, 0, rows, nn(lhs, d_raw[...]))
        left = mixed[:, pl.ds(pl.multiple_of(owner * mixed_rows, lanes), mixed_rows)]
        store_columns(
            keep, send, slot, (wide // lanes) * rows, mixed_rows, tn(left, d_projected[...])
        )
    finish(copies)
    d_normed_out[...] = nt(d_raw[...], query_full[...])


def key_back_kernel(
    count, info, cosine, sine, gains, raw, normed, hidden, d_after, d_normed_query,
    mix_grad, feed_grad, final_grad, query_grad, b0, b1, *refs,
):
    parts = refs[:count]
    (
        input_grad, keep, send,
        both_full, d_both, turned, gain_grads, sems,
    ) = refs[count:]
    index = info[0]
    copies = place(index, (b0, b1), both_full, sems)
    width = raw.shape[1]
    both = parts[0][...].astype(f32)
    for piece in parts[1:]:
        both = both + piece[...].astype(f32)
    hat, inverse = unit(raw[...])
    grad = unspin(both[:, :width], cosine[...], sine[...])
    gain_grads[...] = jnp.zeros_like(gain_grads)
    gain_grads[5:6, :width] = jnp.sum(grad * hat, axis=0, keepdims=True)
    d_both[:, :width] = unit_back(hat, inverse, grad * (1.0 + gains[5:6, :width])).astype(bf16)
    d_both[:, width:] = both[:, width:].astype(bf16)
    turned[...] = normed[...].astype(f32).T.astype(bf16)
    rows = normed.shape[1] // 4
    for slot, step in enumerate(order):
        owner = index ^ step
        lhs = turned[pl.ds(pl.multiple_of(owner * rows, 16), rows), :]
        store_columns(keep, send, slot, 0, rows, nn(lhs, d_both[...]))
    finish(copies)
    d_normed = d_normed_query[...] + nt(d_both[...], both_full[...])
    hat, inverse = unit(hidden[...].astype(f32))
    gain_grads[0:1, :] = jnp.sum(d_normed * hat, axis=0, keepdims=True)
    gain_grads[1:2, :] = mix_grad[...]
    gain_grads[2:3, :] = feed_grad[...]
    gain_grads[3:4, :] = final_grad[...]
    gain_grads[4:5, :width] = query_grad[...]
    input_grad[...] = d_after[...] + unit_back(hat, inverse, d_normed * (1.0 + gains[0:1, :]))
    model = normed.shape[1]
    piece = width // 4
    span = 2 * lanes
    line = lax.broadcasted_iota(jnp.int32, (model, span), 0)
    column = lax.broadcasted_iota(jnp.int32, (model, span), 1)
    values = gain_grads[...].astype(bf16)
    base = (2 * width // lanes) * rows
    for slot, step in enumerate(order):
        target = keep if slot < 2 else send
        owner = index ^ step
        spots = (line == column + owner * rows) & (column < rows)
        wide_part = nn(values, spots.astype(f32).astype(bf16)).astype(bf16)
        spots = (line == column + owner * piece) & (column < piece)
        head_part = nn(values, spots.astype(f32).astype(bf16)).astype(bf16)
        begin = base
        for part in (wide_part[:, :lanes], wide_part[:, lanes:], head_part[:, :lanes]):
            target[slot % 2, begin : begin + gain_pad, :] = part
            begin += gain_pad
        target[slot % 2, begin:, :] = jnp.zeros((target.shape[1] - begin, lanes), bf16)


def unpack_kernel(shapes, count, *refs):
    packs, outs = refs[:count], refs[count:]
    number, base = 0, 0
    for out, (rows, width) in zip(outs, shapes):
        for start in range(0, width, lanes):
            if base == packs[number].shape[0]:
                number, base = number + 1, 0
            out[:, start : start + lanes] = packs[number][base : base + rows, :].astype(f32)
            base += rows


def flip(value, axis, bit):
    size = lax.axis_size(axis)
    return lax.ppermute(value, axis, [(i, i ^ bit) for i in range(size)])


def pair_up(shard, far):
    both = jnp.concatenate([shard, far], axis=0)
    return both, flip(both, "fsdp", 1)


def add_low(*values):
    total = values[0].astype(f32)
    for value in values[1:]:
        total = total + value.astype(f32)
    return total.astype(bf16)


def take_half(value, which):
    axis = value.ndim - 2
    half = value.shape[axis] // 2
    return lax.dynamic_slice_in_dim(value, which * half, half, axis)


def ctx_bits():
    return [1 << i for i in range(lax.axis_size("ctx").bit_length() - 1)]


def scatter_step(value, bit):
    mine = (lax.axis_index("ctx") // bit) % 2
    sent = flip(take_half(value, 1 - mine), "ctx", bit)
    return add_low(take_half(value, mine), sent)


def gather_step(value, bit):
    mine = (lax.axis_index("ctx") // bit) % 2
    other = flip(value, "ctx", bit)
    low = jnp.where(mine == 0, value, other)
    high = jnp.where(mine == 0, other, value)
    return jnp.concatenate([low, high], axis=0)


def send_on(value, shift, groups):
    return lax.ppermute(value, "ctx", [(i, i + shift) for i in range(groups - shift)])


def send_back(value, shift, groups):
    return lax.ppermute(value, "ctx", [(i + shift, i) for i in range(groups - shift)])


def on_device(
    hidden_in, positions, query_weight, key_weight, value_weight, output_weight, gate_weight,
    up_weight, down_weight, input_gain, mixer_gain, feed_gain, final_gain, query_gain, key_gain,
    out_grad,
):
    tokens = hidden_in.shape[1]
    model = hidden_in.shape[2]
    rows = key_weight.shape[0]
    head_dim = key_weight.shape[1]
    wide = query_weight.shape[1]
    heads = wide // head_dim
    feed = gate_weight.shape[1]
    mixed_rows = output_weight.shape[0]
    down_rows = down_weight.shape[0]
    me = lax.axis_index("fsdp")
    ctx = lax.axis_index("ctx")
    groups = lax.axis_size("ctx")
    first_row = ctx * tokens

    gains = jnp.zeros((gain_pad, 2 * head_dim), bf16)
    shards = (input_gain, mixer_gain, feed_gain, final_gain, query_gain, key_gain)
    for number, gain in enumerate(shards):
        gains = gains + jnp.pad(
            gain[None], ((number, gain_pad - 1 - number), (0, 2 * head_dim - gain.shape[0]))
        )
    both_shard = jnp.concatenate(
        [jnp.concatenate([key_weight, value_weight], axis=1), gains], axis=0
    )
    far_both = flip(both_shard, "fsdp", 2)
    far_query = flip(query_weight, "fsdp", 2)
    far_both, output_weight = tie(far_both, output_weight)
    far_output = flip(output_weight, "fsdp", 2)
    both_blocks = pair_up(both_shard, far_both)
    feed_pair = jnp.concatenate([gate_weight, up_weight], axis=1)

    hidden = hidden_in[0]
    cotangent = out_grad[0]
    places = positions[0]
    place_col = places[:, None]
    place_row = places[None, :]
    half = head_dim // 2
    freqs = rope_base ** (-(jnp.arange(half, dtype=f32) * 2.0) / head_dim)
    angles = places.astype(f32)[:, None] * freqs[None, :]
    cosine, sine = jnp.cos(angles), jnp.sin(angles)

    def facts(*starts):
        return jnp.stack([me, first_row, *starts]).astype(jnp.int32)

    info = facts()
    sem = pltpu.SemaphoreType.DMA
    token_flops = 2 * tokens * model

    normed, key_raw, kv, gains = call(
        kv_kernel,
        (info, hidden, cosine, sine, *both_blocks),
        [SMEM] + [VMEM] * 3 + [ANY] * 2,
        [
            ((tokens, model), bf16),
            ((tokens, head_dim), f32),
            ((tokens, 2 * head_dim), bf16),
            ((gain_pad, model), f32),
        ],
        [
            pltpu.VMEM((model, 2 * head_dim), bf16),
            pltpu.VMEM((4 * gain_pad, 2 * head_dim), bf16),
            sem((2, 4)),
        ],
        flops=token_flops * 2 * head_dim,
        name="key_value",
    )
    ring = groups == 8
    if ring:
        side = ctx % 2
        stage = ctx // 2
        moved = [kv, send_on(kv, 2, groups)]
        others = [flip(kv, "ctx", 1)]
        moved[1], far_query, far_output, feed_pair = tie(
            moved[1], far_query, far_output, feed_pair
        )
        moved.append(send_on(moved[1], 2, groups))
        others.append(flip(moved[1], "ctx", 1))
    else:
        gathered = lax.all_gather(kv, "ctx", axis=0, tiled=True)
    query_blocks = pair_up(query_weight, far_query)
    query_raw, queries = call(
        query_kernel,
        (info, normed, gains, cosine, sine, *query_blocks),
        [SMEM] + [VMEM] * 4 + [ANY] * 2,
        [((tokens, wide), f32), ((tokens, wide), bf16)],
        [pltpu.VMEM((model, wide), bf16), sem((4,))],
        flops=token_flops * wide,
        name="query",
    )

    far_feed = flip(feed_pair, "fsdp", 2)
    if ring:
        queries, moved[2] = tie(queries, moved[2])
        moved.append(send_on(moved[2], 2, groups))
        others.append(flip(moved[2], "ctx", 1))

    state = ()
    chunk_flops = 4 * tokens * tokens * wide
    sources = []
    for number in range(groups // 2 if ring else 1):
        if ring:
            if number == 1:
                moved[3], total, far_output = tie(moved[3], state[1], far_output)
                state = (state[0], total)
                others.append(flip(moved[3], "ctx", 1))
            if number == groups // 2 - 1:
                far_feed, down_weight, total, others[3] = tie(
                    far_feed, down_weight, state[1], others[3]
                )
                state = (state[0], total)
            arrays = (moved[number], others[number])
            base = (stage - number) * 2
            starts = ((base + side) * tokens, (base + 1 - side) * tokens)
        else:
            arrays, starts = (gathered,), (jnp.int32(0),)
        sources.append((arrays, starts))
        first = number == 0
        count = len(arrays)

        def attend(*args, first=first, count=count):
            attend_kernel(first, count, *args)

        state = call(
            attend,
            (facts(*starts), queries, place_col, *arrays, *state),
            [SMEM] + [VMEM] * (2 + count + len(state)),
            [((tokens, wide), f32), ((tokens, heads * lanes), f32)],
            flops=chunk_flops * 2,
            limit=vmem_bytes if ring else 3 * vmem_bytes,
            name="attend",
        )
    weighted, total = state
    if not ring:
        total, far_feed, down_weight = tie(total, far_feed, down_weight)
    output_blocks = pair_up(output_weight, far_output)
    feed_blocks = pair_up(feed_pair, far_feed)
    far_down = flip(down_weight, "fsdp", 2)

    attended, mixed, projected, after, normed_feed, gate_value, up_value, activated = call(
        mix_kernel,
        (
            info, weighted, total, hidden, gains,
            *output_blocks, *feed_blocks,
        ),
        [SMEM] + [VMEM] * 4 + [ANY] * 4,
        [
            ((tokens, wide), f32),
            ((tokens, wide), bf16),
            ((tokens, model), f32),
            ((tokens, model), f32),
            ((tokens, model), bf16),
            ((tokens, feed), f32),
            ((tokens, feed), f32),
            ((tokens, feed), bf16),
        ],
        [
            pltpu.VMEM((wide, model), bf16),
            pltpu.VMEM((model, feed), bf16),
            pltpu.VMEM((model, feed), bf16),
            sem((3, 4)),
        ],
        flops=token_flops * (wide + 2 * feed),
        name="mix",
    )
    far_down, mixed = tie(far_down, mixed)
    down_blocks = pair_up(down_weight, far_down)
    feed_rows = 2 * (feed // lanes) * rows + (model // lanes) * down_rows
    hidden_out, d_gate, d_up, grad_final, feed_keep, feed_send = call(
        feed_kernel,
        (
            info, activated, gate_value, up_value, normed_feed, after, cotangent, gains,
            *down_blocks,
        ),
        [SMEM] + [VMEM] * 7 + [ANY] * 2,
        [
            ((tokens, model), bf16),
            ((tokens, feed), bf16),
            ((tokens, feed), bf16),
            ((1, model), f32),
            ((2, feed_rows, lanes), bf16),
            ((2, feed_rows, lanes), bf16),
        ],
        [
            pltpu.VMEM((feed, model), bf16),
            pltpu.VMEM((tokens, model), bf16),
            pltpu.VMEM((model, tokens), bf16),
            sem((4,)),
        ],
        flops=token_flops * 5 * feed,
        name="feed",
    )
    feed_near = flip(feed_send, "fsdp", 1)

    d_after, d_projected, d_mixed, table, grad_feed_gain, grad_mix_gain = call(
        feed_back_kernel,
        (
            info, d_gate, d_up, after, projected, attended, total, cotangent, gains,
            *feed_blocks, *output_blocks,
        ),
        [SMEM] + [VMEM] * 8 + [ANY] * 4,
        [
            ((tokens, model), f32),
            ((tokens, model), bf16),
            ((tokens, wide), bf16),
            ((2 * heads, tokens), f32),
            ((1, model), f32),
            ((1, model), f32),
        ],
        [
            pltpu.VMEM((model, feed), bf16),
            pltpu.VMEM((model, feed), bf16),
            pltpu.VMEM((wide, model), bf16),
            pltpu.VMEM((tokens, model), f32),
            sem((3, 4)),
        ],
        flops=token_flops * (2 * feed + wide),
        name="feed_back",
    )

    feed_near, d_mixed = tie(feed_near, d_mixed)
    gate_rows = (feed // lanes) * rows
    half_rows = feed_rows // 2
    left_sum = add_low(feed_keep[1, :half_rows], feed_near[1, :half_rows])
    right_sum = add_low(feed_keep[:, half_rows:], feed_near[:, half_rows:])
    d_mixed, left_sum, right_sum = tie(d_mixed, left_sum, right_sum)
    left_far = flip(left_sum, "fsdp", 2)
    bits = ctx_bits()
    steps = len(bits)
    turned = [bits[1], bits[0], *bits[2:]]
    right_sum = scatter_step(right_sum, turned[0])

    query_grads = ()
    arrived = []
    waiting = None
    last = len(sources) - 1
    for number, (arrays, starts) in enumerate(reversed(sources)):
        first = number == 0
        count = len(arrays)

        def attend_back(*args, first=first, count=count):
            attend_back_kernel(first, count, *args)

        results = call(
            attend_back,
            (facts(*starts), queries, d_mixed, table, place_row, *arrays, *query_grads),
            [SMEM] + [VMEM] * (4 + count + len(query_grads)),
            [((tokens, wide), f32)] + [(a.shape, bf16) for a in arrays],
            [pltpu.VMEM((tokens, head_dim), f32), pltpu.VMEM((tokens, head_dim), f32)],
            flops=chunk_flops * 5,
            limit=vmem_bytes if ring else 3 * vmem_bytes,
            name="attend_back",
        )
        query_grads = results[:1]
        if not ring:
            arrived.append(
                lax.psum_scatter(results[1], "ctx", scatter_dimension=0, tiled=True)
            )
            continue
        shift = last - number
        own, other = results[1:]
        if waiting is not None:
            crossed, held, *arrived = tie(waiting[1], query_grads[0], *arrived)
            if number == last - 1:
                held, left_far = tie(held, left_far)
            query_grads = (held,)
            arrived = [send_back(add_low(waiting[0], crossed, *arrived), 2, groups)]
        waiting = (own, flip(other, "ctx", 1))
    if ring:
        arrived += list(waiting)
    held, right_sum, left_far = tie(query_grads[0], right_sum, left_far)
    query_grads = (held,)
    left = add_low(feed_keep[0, :half_rows], feed_near[0, :half_rows], left_far)
    right_far = flip(right_sum[1], "fsdp", 2)

    query_rows = (wide // lanes) * rows
    output_rows = (model // lanes) * mixed_rows
    d_normed_query, grad_query_gain, query_keep, query_send = call(
        query_back_kernel,
        (
            info, query_grads[0], query_raw, cosine, sine, gains, normed, mixed, d_projected,
            *query_blocks,
        ),
        [SMEM] + [VMEM] * 8 + [ANY] * 2,
        [
            ((tokens, model), f32),
            ((1, head_dim), f32),
            ((2, query_rows + output_rows, lanes), bf16),
            ((2, query_rows + output_rows, lanes), bf16),
        ],
        [
            pltpu.VMEM((model, wide), bf16),
            pltpu.VMEM((tokens, wide), bf16),
            pltpu.VMEM((model, tokens), bf16),
            sem((4,)),
        ],
        flops=token_flops * 3 * wide,
        name="query_back",
    )
    arrived_count = len(arrived)
    left, *arrived = tie(left, *arrived)
    left = scatter_step(left, bits[0])
    query_near = [
        flip(query_send[:, :query_rows], "fsdp", 1),
        flip(query_send[:, query_rows:], "fsdp", 1),
    ]
    both_rows = (2 * head_dim // lanes) * rows + lanes

    def key_back(*args):
        key_back_kernel(arrived_count, *args)

    grad_input, both_keep, both_send = call(
        key_back,
        (
            info, cosine, sine, gains, key_raw, normed, hidden, d_after,
            d_normed_query, grad_mix_gain, grad_feed_gain, grad_final, grad_query_gain,
            *both_blocks, *arrived,
        ),
        [SMEM] + [VMEM] * 12 + [ANY] * 2 + [VMEM] * arrived_count,
        [
            ((tokens, model), f32),
            ((2, both_rows, lanes), bf16),
            ((2, both_rows, lanes), bf16),
        ],
        [
            pltpu.VMEM((model, 2 * head_dim), bf16),
            pltpu.VMEM((tokens, 2 * head_dim), bf16),
            pltpu.VMEM((model, tokens), bf16),
            pltpu.VMEM((gain_pad, model), f32),
            sem((4,)),
        ],
        flops=token_flops * 4 * head_dim,
        name="key_back",
    )
    both_send, right_far, left = tie(both_send, right_far, left)
    query_near = jnp.concatenate(query_near, axis=1)
    query_far = flip(add_low(query_keep[1], query_near[1]), "fsdp", 2)
    both_near = flip(both_send, "fsdp", 1)

    right = add_low(right_sum[0], right_far)
    query_part = both_part = None
    for number in range(1, 2 * steps + 2):
        if number < steps:
            left = scatter_step(left, bits[number])
            right = scatter_step(right, turned[number])
        elif number < 2 * steps:
            left = gather_step(left, bits[2 * steps - 1 - number])
            right = gather_step(right, turned[2 * steps - 1 - number])
        if number == 1:
            both_far = flip(add_low(both_keep[1], both_near[1]), "fsdp", 2)
            left, right, query_far, both_near = tie(left, right, query_far, both_near)
            query_part = add_low(query_keep[0], query_near[0], query_far)
            continue
        now = number - 2
        if now < steps:
            query_part = scatter_step(query_part, bits[now])
        elif now < 2 * steps:
            query_part = gather_step(query_part, bits[2 * steps - 1 - now])
        if number == 2:
            left, right, query_part, both_far = tie(left, right, query_part, both_far)
            both_part = add_low(both_keep[0], both_near[0], both_far)
            both_part = scatter_step(both_part, bits[0])
            continue
        if number - 2 < steps:
            both_part = add_low(both_part, flip(both_part, "ctx", bits[number - 2]))
        elif number - 2 == steps:
            both_part = gather_step(both_part, bits[0])
        left, right, query_part, both_part = tie(left, right, query_part, both_part)

    def unpack(packs, shapes):
        def kernel(*args):
            unpack_kernel(shapes, len(packs), *args)

        specs = [VMEM] * len(packs)
        return call(kernel, packs, specs, [(s, f32) for s in shapes], name="unpack")

    grad_gate, grad_up, grad_down = unpack(
        (left, right), [gate_weight.shape, up_weight.shape, down_weight.shape]
    )
    grad_query, grad_output = unpack((query_part,), [query_weight.shape, output_weight.shape])
    grad_key, grad_value, wide_gains, head_gains = unpack(
        (both_part,),
        [key_weight.shape, value_weight.shape, (gain_pad, 2 * lanes), (gain_pad, lanes)],
    )
    gain_shards = [wide_gains[i, :rows] for i in range(4)]
    gain_shards += [head_gains[i, : query_gain.shape[0]] for i in (4, 5)]
    return (
        hidden_out[None],
        grad_input[None],
        grad_query,
        grad_key,
        grad_value,
        grad_output,
        grad_gate,
        grad_up,
        grad_down,
        *gain_shards,
    )


def solution(mesh):
    token = P("fsdp", "ctx", None)
    weight = P("fsdp", None)
    gain = P("fsdp")
    return jax.shard_map(
        on_device,
        mesh=mesh,
        in_specs=(token, P("fsdp", "ctx")) + (weight,) * 7 + (gain,) * 6 + (token,),
        out_specs=(token, token) + (weight,) * 7 + (gain,) * 6,
        check_vma=False,
    )
```

```python
import jax
import jax.numpy as jnp
from jax import lax
from jax.experimental import pallas as pl
from jax.experimental.pallas import tpu as pltpu
from jax.sharding import PartitionSpec as P

eps = 1e-06
rope_base = 1000000.0
lanes = 128
order = (0, 2, 1, 3)
vmem_bytes = 16 * 1024 * 1024
gain_pad = 16
f32 = jnp.float32
bf16 = jnp.bfloat16

ANY = pl.BlockSpec(memory_space=pl.ANY)
SMEM = pl.BlockSpec(memory_space=pltpu.SMEM)
VMEM = pl.BlockSpec(memory_space=pltpu.VMEM)


def tie(*values):
    return lax.optimization_barrier(values)


def call(kernel, inputs, specs, outs, scratch=(), flops=0, limit=vmem_bytes, name=None):
    return pl.pallas_call(
        kernel,
        out_shape=tuple(jax.ShapeDtypeStruct(s, d) for s, d in outs),
        in_specs=list(specs),
        out_specs=tuple(VMEM for _ in outs),
        scratch_shapes=list(scratch),
        compiler_params=pltpu.CompilerParams(vmem_limit_bytes=limit),
        cost_estimate=pl.CostEstimate(flops=1, bytes_accessed=1, transcendentals=0),
        name=name,
    )(*inputs)


def nn(left, right):
    return lax.dot_general(left, right, (((1,), (0,)), ((), ())), preferred_element_type=f32)


def nt(left, right):
    return lax.dot_general(left, right, (((1,), (1,)), ((), ())), preferred_element_type=f32)


def tn(left, right):
    return lax.dot_general(left, right, (((0,), (0,)), ((), ())), preferred_element_type=f32)


def unit(value):
    inverse = lax.rsqrt(jnp.mean(value * value, axis=-1, keepdims=True) + eps)
    return value * inverse, inverse


def unit_back(hat, inverse, grad_hat):
    return inverse * (grad_hat - hat * jnp.mean(grad_hat * hat, axis=-1, keepdims=True))


def spin(value, cosine, sine):
    half = value.shape[-1] // 2
    first, second = value[:, :half], value[:, half:]
    return jnp.concatenate(
        [first * cosine - second * sine, second * cosine + first * sine], axis=-1
    )


def place(index, pairs, full, sems, columns=None):
    rows = full.shape[0] // 4
    pitch = pairs[0].shape[0] // 2
    copies = []
    for step in range(4):
        begin = pl.multiple_of((index ^ step) * rows, 16)
        source = pairs[step % 2].at[pl.ds((step // 2) * pitch, rows)]
        if columns is not None:
            source = source.at[:, pl.ds(columns, full.shape[1])]
        copy = pltpu.make_async_copy(source, full.at[pl.ds(begin, rows)], sems.at[step])
        copy.start()
        copies.append(copy)
    return copies


def finish(copies):
    for copy in copies:
        copy.wait()


def kv_kernel(
    info, hidden, cosine, sine,
    b0, b1,
    normed_out, key_raw_out, kv_out, gains_out,
    both_full, gain_parts, sems,
):
    index = info[0]
    copies = place(index, (b0, b1), both_full, sems.at[0])
    model = hidden.shape[1]
    rows = model // 4
    width = key_raw_out.shape[1]
    piece = width // 4
    gain_copies = []
    for step in range(4):
        begin = pl.multiple_of((index ^ step) * gain_pad, gain_pad)
        source = (b0, b1)[step % 2].at[pl.ds((step // 2) * (rows + gain_pad) + rows, gain_pad)]
        copy = pltpu.make_async_copy(
            source, gain_parts.at[pl.ds(begin, gain_pad)], sems.at[1, step]
        )
        copy.start()
        gain_copies.append(copy)
    hat, _ = unit(hidden[...].astype(f32))
    finish(gain_copies)
    span = 2 * lanes
    line = lax.broadcasted_iota(jnp.int32, (span, model), 0)
    column = lax.broadcasted_iota(jnp.int32, (span, model), 1)
    wide_gain = jnp.zeros((gain_pad, model), f32)
    head_gain = jnp.zeros((gain_pad, model), f32)
    for owner in range(4):
        values = gain_parts[owner * gain_pad : (owner + 1) * gain_pad, :span]
        spots = (column == line + owner * rows) & (line < rows)
        wide_gain += nn(values, spots.astype(f32).astype(bf16))
        spots = (column == line + owner * piece) & (line < piece)
        head_gain += nn(values, spots.astype(f32).astype(bf16))
    which = lax.broadcasted_iota(jnp.int32, (gain_pad, model), 0)
    gains = jnp.where(which < 4, wide_gain, head_gain)
    gains_out[...] = gains
    normed = (hat * (1.0 + gains[0:1, :])).astype(bf16)
    normed_out[...] = normed
    finish(copies)
    raw = nn(normed, both_full[:, :width])
    key_raw_out[...] = raw
    hat, _ = unit(raw)
    scale = 1.0 + gains[5:6, :width]
    kv_out[:, :width] = spin(hat * scale, cosine[...], sine[...]).astype(bf16)
    kv_out[:, width:] = nn(normed, both_full[:, width:]).astype(bf16)


def query_kernel(
    info, normed, gains, cosine, sine, q0, q1,
    raw_out, query_out, query_full, sems,
):
    finish(place(info[0], (q0, q1), query_full, sems))
    head_dim = 2 * cosine.shape[1]
    for start in range(0, query_full.shape[1], head_dim):
        part = slice(start, start + head_dim)
        raw = nn(normed[...], query_full[:, part])
        raw_out[:, part] = raw
        hat, _ = unit(raw)
        turned = spin(hat * (1.0 + gains[4:5, :head_dim]), cosine[...], sine[...])
        query_out[:, part] = (turned * head_dim ** (-0.5)).astype(bf16)


def attend_kernel(first, count, info, queries, places, *refs):
    chunks = refs[:count]
    refs = refs[count:]
    if not first:
        weighted_in, total_in = refs[:2]
        refs = refs[2:]
    weighted, total = refs
    tokens = queries.shape[0]
    head_dim = chunks[0].shape[1] // 2
    heads = queries.shape[1] // head_dim
    if first:
        weighted[...] = jnp.zeros_like(weighted)
        total[...] = jnp.zeros_like(total)
    else:
        weighted[...] = weighted_in[...]
        total[...] = total_in[...]
    first_row = info[1]
    for number, chunk in enumerate(chunks):
        base = info[2 + number]

        @pl.loop(0, chunk.shape[0] // tokens)
        def _(step):
            start = base + step * tokens

            @pl.when((start >= 0) & (start <= first_row))
            def _():
                local = pl.ds(pl.multiple_of(step * tokens, tokens), tokens)
                row = first_row + lax.broadcasted_iota(jnp.int32, (tokens, tokens), 0)
                col = start + lax.broadcasted_iota(jnp.int32, (tokens, tokens), 1)
                allowed = (col <= row) & (col >= row - places[...])
                keys = chunk[local, :head_dim]
                values = chunk[local, head_dim:]
                for head in range(heads):
                    part = slice(head * head_dim, (head + 1) * head_dim)
                    scores = nt(queries[:, part], keys)
                    expo = jnp.where(allowed, jnp.exp(scores), 0.0)
                    spot = slice(head * lanes, (head + 1) * lanes)
                    total[:, spot] += jnp.sum(expo, axis=1, keepdims=True)
                    weighted[:, part] += nn(expo.astype(bf16), values)


def mix_kernel(
    info, weighted, total, hidden, gains,
    o0, o1, g0, g1,
    attended_out, mixed_out, projected_out, after_out, normed_out, gate_out, up_out, act_out,
    output_full, gate_full, up_full, sems,
):
    index = info[0]
    feed = gate_full.shape[1]
    output_copies = place(index, (o0, o1), output_full, sems.at[0])
    gate_copies = place(index, (g0, g1), gate_full, sems.at[1], 0)
    up_copies = place(index, (g0, g1), up_full, sems.at[2], feed)
    heads = total.shape[1] // lanes
    head_dim = weighted.shape[1] // heads
    for head in range(heads):
        part = slice(head * head_dim, (head + 1) * head_dim)
        ratio = weighted[:, part] / total[:, head * lanes : head * lanes + 1]
        attended_out[:, part] = ratio
        mixed_out[:, part] = ratio.astype(bf16)
    finish(output_copies)
    projected = nn(mixed_out[...], output_full[...])
    projected_out[...] = projected
    hat, _ = unit(projected)
    after = hidden[...].astype(f32) + hat * (1.0 + gains[1:2, :])
    after_out[...] = after
    hat, _ = unit(after)
    normed_out[...] = (hat * (1.0 + gains[2:3, :])).astype(bf16)
    finish(gate_copies)
    finish(up_copies)
    step_width = 512

    @pl.loop(0, gate_full.shape[1] // step_width)
    def _(step):
        part = pl.ds(pl.multiple_of(step * step_width, step_width), step_width)
        gate = nn(normed_out[...], gate_full[:, part])
        up = nn(normed_out[...], up_full[:, part])
        gate_out[:, part] = gate
        up_out[:, part] = up
        inner = 0.7978845608028654 * (gate + 0.044715 * gate * gate * gate)
        act_out[:, part] = (0.5 * gate * (1.0 + jnp.tanh(inner)) * up).astype(bf16)


def store_columns(keep, send, slot, base, rows, block):
    target = keep if slot < 2 else send
    for number in range(block.shape[1] // lanes):
        target[slot % 2, base + number * rows : base + (number + 1) * rows, :] = block[
            :, number * lanes : (number + 1) * lanes
        ].astype(bf16)


def feed_kernel(
    info, act, gate, up, normed, after, cotangent, gains,
    d0, d1,
    hidden_out, d_gate, d_up, gain_grad, keep, send,
    down_full, d_down, turned, sems,
):
    index = info[0]
    finish(place(index, (d0, d1), down_full, sems))
    down = nn(act[...], down_full[...])
    hat, inverse = unit(down)
    scale = 1.0 + gains[3:4, :]
    hidden_out[...] = (after[...] + hat * scale).astype(bf16)
    grad = cotangent[...].astype(f32)
    gain_grad[...] = jnp.sum(grad * hat, axis=0, keepdims=True)
    d_down[...] = unit_back(hat, inverse, grad * scale).astype(bf16)
    turned[...] = normed[...].astype(f32).T.astype(bf16)
    step_width = 512

    @pl.loop(0, down_full.shape[0] // step_width)
    def _(step):
        part = pl.ds(pl.multiple_of(step * step_width, step_width), step_width)
        d_act = nt(d_down[...], down_full[part, :])
        x = gate[:, part]
        curve = jnp.tanh(0.7978845608028654 * (x + 0.044715 * x * x * x))
        slope = 0.5 * (1.0 + curve) + 0.5 * x * (1.0 - curve * curve) * (
            0.7978845608028654 * (1.0 + 3.0 * 0.044715 * x * x)
        )
        d_gate[:, part] = (d_act * up[:, part] * slope).astype(bf16)
        d_up[:, part] = (d_act * (0.5 * x * (1.0 + curve))).astype(bf16)

    model = normed.shape[1]
    rows = model // 4
    wide = gate.shape[1]
    down_rows = wide // 4
    part_rows = (wide // lanes) * rows
    for slot, step in enumerate(order):
        target = keep if slot < 2 else send
        owner = index ^ step
        lhs = turned[pl.ds(pl.multiple_of(owner * rows, 16), rows), :]
        for base, source in ((0, d_gate), (part_rows, d_up)):

            @pl.loop(0, wide // step_width)
            def _(move):
                part = pl.ds(pl.multiple_of(move * step_width, step_width), step_width)
                block = nn(lhs, source[:, part]).astype(bf16)
                for number in range(step_width // lanes):
                    begin = base + (move * (step_width // lanes) + number) * rows
                    target[slot % 2, pl.ds(pl.multiple_of(begin, 16), rows), :] = block[
                        :, number * lanes : (number + 1) * lanes
                    ]

        left = act[:, pl.ds(pl.multiple_of(owner * down_rows, lanes), down_rows)]
        store_columns(keep, send, slot, 2 * part_rows, down_rows, tn(left, d_down[...]))


def feed_back_kernel(
    info, d_gate, d_up, after, projected, attended, total, cotangent, gains,
    g0, g1, o0, o1,
    d_after_out, d_projected_out, d_mixed_out, rows_out, feed_grad, mix_grad,
    gate_full, up_full, output_full, total_grad, sems,
):
    index = info[0]
    gate_copies = place(index, (g0, g1), gate_full, sems.at[0], 0)
    up_copies = place(index, (g0, g1), up_full, sems.at[1], gate_full.shape[1])
    output_copies = place(index, (o0, o1), output_full, sems.at[2])
    finish(gate_copies)
    total_grad[...] = nt(d_gate[...], gate_full[...])
    finish(up_copies)
    grad = total_grad[...] + nt(d_up[...], up_full[...])
    hat, inverse = unit(after[...])
    feed_grad[...] = jnp.sum(grad * hat, axis=0, keepdims=True)
    d_after = cotangent[...].astype(f32) + unit_back(hat, inverse, grad * (1.0 + gains[2:3, :]))
    d_after_out[...] = d_after
    hat, inverse = unit(projected[...])
    mix_grad[...] = jnp.sum(d_after * hat, axis=0, keepdims=True)
    d_projected = unit_back(hat, inverse, d_after * (1.0 + gains[1:2, :])).astype(bf16)
    d_projected_out[...] = d_projected
    finish(output_copies)
    d_mixed = nt(d_projected, output_full[...]).astype(bf16)
    d_mixed_out[...] = d_mixed
    heads = total.shape[1] // lanes
    head_dim = attended.shape[1] // heads
    tokens = attended.shape[0]
    lane = lax.broadcasted_iota(jnp.int32, (tokens, lanes), 1)
    table = jnp.zeros((tokens, lanes), f32)
    for head in range(heads):
        part = slice(head * head_dim, (head + 1) * head_dim)
        delta = jnp.sum(d_mixed[:, part].astype(f32) * attended[:, part], axis=1, keepdims=True)
        table = jnp.where(lane == head, delta, table)
        share = 1.0 / total[:, head * lanes : (head + 1) * lanes]
        table = jnp.where(lane == heads + head, share, table)
    rows_out[...] = table.T[: rows_out.shape[0], :]


def attend_back_kernel(first, count, info, queries, d_mixed, table, places, *refs):
    chunks = refs[:count]
    refs = refs[count:]
    if not first:
        query_in = refs[0]
        refs = refs[1:]
    query_grads = refs[0]
    chunk_grads = refs[1 : 1 + count]
    key_sum, value_sum = refs[1 + count :]
    tokens = queries.shape[0]
    head_dim = chunks[0].shape[1] // 2
    heads = queries.shape[1] // head_dim
    if first:
        query_grads[...] = jnp.zeros_like(query_grads)
    else:
        query_grads[...] = query_in[...]
    first_row = info[1]
    for number, (chunk, chunk_grad) in enumerate(zip(chunks, chunk_grads)):
        base = info[2 + number]
        chunk_grad[...] = jnp.zeros_like(chunk_grad)

        @pl.loop(0, chunk.shape[0] // tokens)
        def _(step):
            start = base + step * tokens

            @pl.when((start >= 0) & (start <= first_row))
            def _():
                local = pl.ds(pl.multiple_of(step * tokens, tokens), tokens)
                row = first_row + lax.broadcasted_iota(jnp.int32, (tokens, tokens), 1)
                col = start + lax.broadcasted_iota(jnp.int32, (tokens, tokens), 0)
                allowed = (col <= row) & (col >= row - places[...])
                keys = chunk[local, :head_dim]
                values = chunk[local, head_dim:]
                for head in range(heads):
                    part = slice(head * head_dim, (head + 1) * head_dim)
                    query = queries[:, part]
                    grad = d_mixed[:, part]
                    expo = jnp.where(allowed, jnp.exp(nt(keys, query)), 0.0)
                    probs = expo * table[heads + head : heads + head + 1, :]
                    back = nt(values, grad) - table[head : head + 1, :]
                    d_scores = (probs * back).astype(bf16)
                    d_value = nn(probs.astype(bf16), grad)
                    d_key = nn(d_scores, query)
                    if head == 0:
                        key_sum[...] = d_key
                        value_sum[...] = d_value
                    else:
                        key_sum[...] += d_key
                        value_sum[...] += d_value
                    query_grads[:, part] += tn(d_scores, keys)
                chunk_grad[local, :head_dim] = key_sum[...].astype(bf16)
                chunk_grad[local, head_dim:] = value_sum[...].astype(bf16)


def unspin(value, cosine, sine):
    half = value.shape[-1] // 2
    first, second = value[:, :half], value[:, half:]
    return jnp.concatenate(
        [first * cosine + second * sine, second * cosine - first * sine], axis=-1
    )


def query_back_kernel(
    info, query_grads, raw, cosine, sine, gains, normed, mixed, d_projected,
    q0, q1,
    d_normed_out, gain_grad, keep, send,
    query_full, d_raw, turned, sems,
):
    index = info[0]
    copies = place(index, (q0, q1), query_full, sems)
    head_dim = 2 * cosine.shape[1]
    wide = raw.shape[1]
    scale = 1.0 + gains[4:5, :head_dim]
    gain_sum = jnp.zeros((1, head_dim), f32)
    for start in range(0, wide, head_dim):
        part = slice(start, start + head_dim)
        hat, inverse = unit(raw[:, part])
        grad = unspin(query_grads[:, part] * head_dim ** (-0.5), cosine[...], sine[...])
        gain_sum += jnp.sum(grad * hat, axis=0, keepdims=True)
        d_raw[:, part] = unit_back(hat, inverse, grad * scale).astype(bf16)
    gain_grad[...] = gain_sum
    turned[...] = normed[...].astype(f32).T.astype(bf16)
    rows = normed.shape[1] // 4
    mixed_rows = mixed.shape[1] // 4
    for slot, step in enumerate(order):
        owner = index ^ step
        lhs = turned[pl.ds(pl.multiple_of(owner * rows, 16), rows), :]
        store_columns(keep, send, slot, 0, rows, nn(lhs, d_raw[...]))
        left = mixed[:, pl.ds(pl.multiple_of(owner * mixed_rows, lanes), mixed_rows)]
        store_columns(
            keep, send, slot, (wide // lanes) * rows, mixed_rows, tn(left, d_projected[...])
        )
    finish(copies)
    d_normed_out[...] = nt(d_raw[...], query_full[...])


def key_back_kernel(
    count, info, cosine, sine, gains, raw, normed, hidden, d_after, d_normed_query,
    mix_grad, feed_grad, final_grad, query_grad, b0, b1, *refs,
):
    parts = refs[:count]
    (
        input_grad, keep, send,
        both_full, d_both, turned, gain_grads, sems,
    ) = refs[count:]
    index = info[0]
    copies = place(index, (b0, b1), both_full, sems)
    width = raw.shape[1]
    both = parts[0][...].astype(f32)
    for piece in parts[1:]:
        both = both + piece[...].astype(f32)
    hat, inverse = unit(raw[...])
    grad = unspin(both[:, :width], cosine[...], sine[...])
    gain_grads[...] = jnp.zeros_like(gain_grads)
    gain_grads[5:6, :width] = jnp.sum(grad * hat, axis=0, keepdims=True)
    d_both[:, :width] = unit_back(hat, inverse, grad * (1.0 + gains[5:6, :width])).astype(bf16)
    d_both[:, width:] = both[:, width:].astype(bf16)
    turned[...] = normed[...].astype(f32).T.astype(bf16)
    rows = normed.shape[1] // 4
    for slot, step in enumerate(order):
        owner = index ^ step
        lhs = turned[pl.ds(pl.multiple_of(owner * rows, 16), rows), :]
        store_columns(keep, send, slot, 0, rows, nn(lhs, d_both[...]))
    finish(copies)
    d_normed = d_normed_query[...] + nt(d_both[...], both_full[...])
    hat, inverse = unit(hidden[...].astype(f32))
    gain_grads[0:1, :] = jnp.sum(d_normed * hat, axis=0, keepdims=True)
    gain_grads[1:2, :] = mix_grad[...]
    gain_grads[2:3, :] = feed_grad[...]
    gain_grads[3:4, :] = final_grad[...]
    gain_grads[4:5, :width] = query_grad[...]
    input_grad[...] = d_after[...] + unit_back(hat, inverse, d_normed * (1.0 + gains[0:1, :]))
    model = normed.shape[1]
    piece = width // 4
    span = 2 * lanes
    line = lax.broadcasted_iota(jnp.int32, (model, span), 0)
    column = lax.broadcasted_iota(jnp.int32, (model, span), 1)
    values = gain_grads[...].astype(bf16)
    base = (2 * width // lanes) * rows
    for slot, step in enumerate(order):
        target = keep if slot < 2 else send
        owner = index ^ step
        spots = (line == column + owner * rows) & (column < rows)
        wide_part = nn(values, spots.astype(f32).astype(bf16)).astype(bf16)
        spots = (line == column + owner * piece) & (column < piece)
        head_part = nn(values, spots.astype(f32).astype(bf16)).astype(bf16)
        begin = base
        for part in (wide_part[:, :lanes], wide_part[:, lanes:], head_part[:, :lanes]):
            target[slot % 2, begin : begin + gain_pad, :] = part
            begin += gain_pad
        target[slot % 2, begin:, :] = jnp.zeros((target.shape[1] - begin, lanes), bf16)


def unpack_kernel(shapes, count, *refs):
    packs, outs = refs[:count], refs[count:]
    number, base = 0, 0
    for out, (rows, width) in zip(outs, shapes):
        for start in range(0, width, lanes):
            if base == packs[number].shape[0]:
                number, base = number + 1, 0
            out[:, start : start + lanes] = packs[number][base : base + rows, :].astype(f32)
            base += rows


def flip(value, axis, bit):
    size = lax.axis_size(axis)
    return lax.ppermute(value, axis, [(i, i ^ bit) for i in range(size)])


def pair_up(shard, far):
    both = jnp.concatenate([shard, far], axis=0)
    return both, flip(both, "fsdp", 1)


def add_low(*values):
    total = values[0].astype(f32)
    for value in values[1:]:
        total = total + value.astype(f32)
    return total.astype(bf16)


def take_half(value, which):
    axis = value.ndim - 2
    half = value.shape[axis] // 2
    return lax.dynamic_slice_in_dim(value, which * half, half, axis)


def ctx_bits():
    return [1 << i for i in range(lax.axis_size("ctx").bit_length() - 1)]


def scatter_step(value, bit):
    mine = (lax.axis_index("ctx") // bit) % 2
    sent = flip(take_half(value, 1 - mine), "ctx", bit)
    return add_low(take_half(value, mine), sent)


def gather_step(value, bit):
    mine = (lax.axis_index("ctx") // bit) % 2
    other = flip(value, "ctx", bit)
    low = jnp.where(mine == 0, value, other)
    high = jnp.where(mine == 0, other, value)
    return jnp.concatenate([low, high], axis=0)


def send_on(value, shift, groups):
    return lax.ppermute(value, "ctx", [(i, i + shift) for i in range(groups - shift)])


def send_back(value, shift, groups):
    return lax.ppermute(value, "ctx", [(i + shift, i) for i in range(groups - shift)])


def on_device(
    hidden_in, positions, query_weight, key_weight, value_weight, output_weight, gate_weight,
    up_weight, down_weight, input_gain, mixer_gain, feed_gain, final_gain, query_gain, key_gain,
    out_grad,
):
    tokens = hidden_in.shape[1]
    model = hidden_in.shape[2]
    rows = key_weight.shape[0]
    head_dim = key_weight.shape[1]
    wide = query_weight.shape[1]
    heads = wide // head_dim
    feed = gate_weight.shape[1]
    mixed_rows = output_weight.shape[0]
    down_rows = down_weight.shape[0]
    me = lax.axis_index("fsdp")
    ctx = lax.axis_index("ctx")
    groups = lax.axis_size("ctx")
    first_row = ctx * tokens

    gains = jnp.zeros((gain_pad, 2 * head_dim), bf16)
    shards = (input_gain, mixer_gain, feed_gain, final_gain, query_gain, key_gain)
    for number, gain in enumerate(shards):
        gains = gains + jnp.pad(
            gain[None], ((number, gain_pad - 1 - number), (0, 2 * head_dim - gain.shape[0]))
        )
    both_shard = jnp.concatenate(
        [jnp.concatenate([key_weight, value_weight], axis=1), gains], axis=0
    )
    far_both = flip(both_shard, "fsdp", 2)
    far_query = flip(query_weight, "fsdp", 2)
    far_both, output_weight = tie(far_both, output_weight)
    far_output = flip(output_weight, "fsdp", 2)
    both_blocks = pair_up(both_shard, far_both)
    feed_pair = jnp.concatenate([gate_weight, up_weight], axis=1)

    hidden = hidden_in[0]
    cotangent = out_grad[0]
    places = positions[0]
    place_col = places[:, None]
    place_row = places[None, :]
    half = head_dim // 2
    freqs = rope_base ** (-(jnp.arange(half, dtype=f32) * 2.0) / head_dim)
    angles = places.astype(f32)[:, None] * freqs[None, :]
    cosine, sine = jnp.cos(angles), jnp.sin(angles)

    def facts(*starts):
        return jnp.stack([me, first_row, *starts]).astype(jnp.int32)

    info = facts()
    sem = pltpu.SemaphoreType.DMA
    token_flops = 2 * tokens * model

    normed, key_raw, kv, gains = call(
        kv_kernel,
        (info, hidden, cosine, sine, *both_blocks),
        [SMEM] + [VMEM] * 3 + [ANY] * 2,
        [
            ((tokens, model), bf16),
            ((tokens, head_dim), f32),
            ((tokens, 2 * head_dim), bf16),
            ((gain_pad, model), f32),
        ],
        [
            pltpu.VMEM((model, 2 * head_dim), bf16),
            pltpu.VMEM((4 * gain_pad, 2 * head_dim), bf16),
            sem((2, 4)),
        ],
        flops=token_flops * 2 * head_dim,
        name="key_value",
    )
    normed, far_query = tie(normed, far_query)

    ring = groups == 8
    if ring:
        side = ctx % 2
        stage = ctx // 2
        moved = [kv, send_on(kv, 2, groups)]
        others = [flip(kv, "ctx", 1)]
        moved[1], far_output, feed_pair = tie(moved[1], far_output, feed_pair)
        moved.append(send_on(moved[1], 2, groups))
        others.append(flip(moved[1], "ctx", 1))
    else:
        gathered = lax.all_gather(kv, "ctx", axis=0, tiled=True)
    query_blocks = pair_up(query_weight, far_query)
    query_raw, queries = call(
        query_kernel,
        (info, normed, gains, cosine, sine, *query_blocks),
        [SMEM] + [VMEM] * 4 + [ANY] * 2,
        [((tokens, wide), f32), ((tokens, wide), bf16)],
        [pltpu.VMEM((model, wide), bf16), sem((4,))],
        flops=token_flops * wide,
        name="query",
    )

    far_feed = flip(feed_pair, "fsdp", 2)
    if ring:
        queries, moved[2], others[1] = tie(queries, moved[2], others[1])
        moved.append(send_on(moved[2], 2, groups))
        others.append(flip(moved[2], "ctx", 1))

    state = ()
    chunk_flops = 4 * tokens * tokens * wide
    sources = []
    for number in range(groups // 2 if ring else 1):
        if ring:
            if number == 1:
                moved[3], total, far_output = tie(moved[3], state[1], far_output)
                state = (state[0], total)
                others.append(flip(moved[3], "ctx", 1))
                output_blocks = pair_up(output_weight, far_output)
            if number == 2:
                total, others[2] = tie(state[1], others[2])
                state = (state[0], total)
            if number == 3:
                far_feed, down_weight, total, output_blocks, others[3] = tie(
                    far_feed, down_weight, state[1], output_blocks, others[3]
                )
                state = (state[0], total)
                feed_blocks = pair_up(feed_pair, far_feed)
                far_down = flip(down_weight, "fsdp", 2)
            arrays = (moved[number], others[number])
            base = (stage - number) * 2
            starts = ((base + side) * tokens, (base + 1 - side) * tokens)
        else:
            arrays, starts = (gathered,), (jnp.int32(0),)
        sources.append((arrays, starts))
        first = number == 0
        count = len(arrays)

        def attend(*args, first=first, count=count):
            attend_kernel(first, count, *args)

        state = call(
            attend,
            (facts(*starts), queries, place_col, *arrays, *state),
            [SMEM] + [VMEM] * (2 + count + len(state)),
            [((tokens, wide), f32), ((tokens, heads * lanes), f32)],
            flops=chunk_flops * 2,
            limit=vmem_bytes if ring else 3 * vmem_bytes,
            name="attend",
        )
    weighted, total = state
    if not ring:
        output_blocks = pair_up(output_weight, far_output)
        feed_blocks = pair_up(feed_pair, far_feed)
        far_down = flip(down_weight, "fsdp", 2)

    attended, mixed, projected, after, normed_feed, gate_value, up_value, activated = call(
        mix_kernel,
        (
            info, weighted, total, hidden, gains,
            *output_blocks, *feed_blocks,
        ),
        [SMEM] + [VMEM] * 4 + [ANY] * 4,
        [
            ((tokens, wide), f32),
            ((tokens, wide), bf16),
            ((tokens, model), f32),
            ((tokens, model), f32),
            ((tokens, model), bf16),
            ((tokens, feed), f32),
            ((tokens, feed), f32),
            ((tokens, feed), bf16),
        ],
        [
            pltpu.VMEM((wide, model), bf16),
            pltpu.VMEM((model, feed), bf16),
            pltpu.VMEM((model, feed), bf16),
            sem((3, 4)),
        ],
        flops=token_flops * (wide + 2 * feed),
        name="mix",
    )
    far_down, mixed = tie(far_down, mixed)
    down_blocks = pair_up(down_weight, far_down)
    feed_rows = 2 * (feed // lanes) * rows + (model // lanes) * down_rows
    hidden_out, d_gate, d_up, grad_final, feed_keep, feed_send = call(
        feed_kernel,
        (
            info, activated, gate_value, up_value, normed_feed, after, cotangent, gains,
            *down_blocks,
        ),
        [SMEM] + [VMEM] * 7 + [ANY] * 2,
        [
            ((tokens, model), bf16),
            ((tokens, feed), bf16),
            ((tokens, feed), bf16),
            ((1, model), f32),
            ((2, feed_rows, lanes), bf16),
            ((2, feed_rows, lanes), bf16),
        ],
        [
            pltpu.VMEM((feed, model), bf16),
            pltpu.VMEM((tokens, model), bf16),
            pltpu.VMEM((model, tokens), bf16),
            sem((4,)),
        ],
        flops=token_flops * 5 * feed,
        name="feed",
    )
    feed_near = flip(feed_send, "fsdp", 1)

    d_after, d_projected, d_mixed, table, grad_feed_gain, grad_mix_gain = call(
        feed_back_kernel,
        (
            info, d_gate, d_up, after, projected, attended, total, cotangent, gains,
            *feed_blocks, *output_blocks,
        ),
        [SMEM] + [VMEM] * 8 + [ANY] * 4,
        [
            ((tokens, model), f32),
            ((tokens, model), bf16),
            ((tokens, wide), bf16),
            ((2 * heads, tokens), f32),
            ((1, model), f32),
            ((1, model), f32),
        ],
        [
            pltpu.VMEM((model, feed), bf16),
            pltpu.VMEM((model, feed), bf16),
            pltpu.VMEM((wide, model), bf16),
            pltpu.VMEM((tokens, model), f32),
            sem((3, 4)),
        ],
        flops=token_flops * (2 * feed + wide),
        name="feed_back",
    )

    feed_near, d_mixed = tie(feed_near, d_mixed)
    gate_rows = (feed // lanes) * rows
    half_rows = feed_rows // 2
    left_sum = add_low(feed_keep[1, :half_rows], feed_near[1, :half_rows])
    right_sum = add_low(feed_keep[:, half_rows:], feed_near[:, half_rows:])
    d_mixed, left_sum, right_sum = tie(d_mixed, left_sum, right_sum)
    left_far = flip(left_sum, "fsdp", 2)
    bits = ctx_bits()
    steps = len(bits)
    turned = [bits[1], bits[0], *bits[2:]]
    right_sum = scatter_step(right_sum, turned[0])

    query_grads = ()
    arrived = []
    waiting = None
    last = len(sources) - 1
    for number, (arrays, starts) in enumerate(reversed(sources)):
        first = number == 0
        count = len(arrays)

        def attend_back(*args, first=first, count=count):
            attend_back_kernel(first, count, *args)

        results = call(
            attend_back,
            (facts(*starts), queries, d_mixed, table, place_row, *arrays, *query_grads),
            [SMEM] + [VMEM] * (4 + count + len(query_grads)),
            [((tokens, wide), f32)] + [(a.shape, bf16) for a in arrays],
            [pltpu.VMEM((tokens, head_dim), f32), pltpu.VMEM((tokens, head_dim), f32)],
            flops=chunk_flops * 5,
            limit=vmem_bytes if ring else 3 * vmem_bytes,
            name="attend_back",
        )
        query_grads = results[:1]
        if not ring:
            arrived.append(
                lax.psum_scatter(results[1], "ctx", scatter_dimension=0, tiled=True)
            )
            continue
        shift = last - number
        own, other = results[1:]
        if waiting is not None:
            crossed, held, *arrived = tie(waiting[1], query_grads[0], *arrived)
            query_grads = (held,)
            arrived = [send_back(add_low(waiting[0], crossed, *arrived), 2, groups)]
        waiting = (own, flip(other, "ctx", 1))
    if ring:
        arrived += list(waiting)

    held, left_far = tie(query_grads[0], left_far)
    query_grads = (held,)
    query_rows = (wide // lanes) * rows
    output_rows = (model // lanes) * mixed_rows
    d_normed_query, grad_query_gain, query_keep, query_send = call(
        query_back_kernel,
        (
            info, query_grads[0], query_raw, cosine, sine, gains, normed, mixed, d_projected,
            *query_blocks,
        ),
        [SMEM] + [VMEM] * 8 + [ANY] * 2,
        [
            ((tokens, model), f32),
            ((1, head_dim), f32),
            ((2, query_rows + output_rows, lanes), bf16),
            ((2, query_rows + output_rows, lanes), bf16),
        ],
        [
            pltpu.VMEM((model, wide), bf16),
            pltpu.VMEM((tokens, wide), bf16),
            pltpu.VMEM((model, tokens), bf16),
            sem((4,)),
        ],
        flops=token_flops * 3 * wide,
        name="query_back",
    )
    arrived_count = len(arrived)
    d_normed_query, right_sum, left_far = tie(d_normed_query, right_sum, left_far)
    left = add_low(feed_keep[0, :half_rows], feed_near[0, :half_rows], left_far)
    left = scatter_step(left, bits[0])
    right_far = flip(right_sum[1], "fsdp", 2)
    query_near = [
        flip(query_send[:, :query_rows], "fsdp", 1),
        flip(query_send[:, query_rows:], "fsdp", 1),
    ]
    both_rows = (2 * head_dim // lanes) * rows + lanes

    def key_back(*args):
        key_back_kernel(arrived_count, *args)

    grad_input, both_keep, both_send = call(
        key_back,
        (
            info, cosine, sine, gains, key_raw, normed, hidden, d_after,
            d_normed_query, grad_mix_gain, grad_feed_gain, grad_final, grad_query_gain,
            *both_blocks, *arrived,
        ),
        [SMEM] + [VMEM] * 12 + [ANY] * 2 + [VMEM] * arrived_count,
        [
            ((tokens, model), f32),
            ((2, both_rows, lanes), bf16),
            ((2, both_rows, lanes), bf16),
        ],
        [
            pltpu.VMEM((model, 2 * head_dim), bf16),
            pltpu.VMEM((tokens, 2 * head_dim), bf16),
            pltpu.VMEM((model, tokens), bf16),
            pltpu.VMEM((gain_pad, model), f32),
            sem((4,)),
        ],
        flops=token_flops * 4 * head_dim,
        name="key_back",
    )
    both_send, right_far, left = tie(both_send, right_far, left)
    query_near = jnp.concatenate(query_near, axis=1)
    query_far = flip(add_low(query_keep[1], query_near[1]), "fsdp", 2)
    both_near = flip(both_send, "fsdp", 1)

    right = add_low(right_sum[0], right_far)
    query_part = both_part = None
    for number in range(1, 2 * steps + 2):
        if number < steps:
            left = scatter_step(left, bits[number])
            right = scatter_step(right, turned[number])
        elif number < 2 * steps:
            left = gather_step(left, bits[2 * steps - 1 - number])
            right = gather_step(right, turned[2 * steps - 1 - number])
        if number == 1:
            both_far = flip(add_low(both_keep[1], both_near[1]), "fsdp", 2)
            left, right, query_far, both_near = tie(left, right, query_far, both_near)
            query_part = add_low(query_keep[0], query_near[0], query_far)
            continue
        now = number - 2
        if now < steps:
            query_part = scatter_step(query_part, bits[now])
        elif now < 2 * steps:
            query_part = gather_step(query_part, bits[2 * steps - 1 - now])
        if number == 2:
            left, right, query_part, both_far = tie(left, right, query_part, both_far)
            both_part = add_low(both_keep[0], both_near[0], both_far)
            both_part = scatter_step(both_part, bits[0])
            continue
        if number - 2 < steps:
            both_part = add_low(both_part, flip(both_part, "ctx", bits[number - 2]))
        elif number - 2 == steps:
            both_part = gather_step(both_part, bits[0])
        left, right, query_part, both_part = tie(left, right, query_part, both_part)

    def unpack(packs, shapes):
        def kernel(*args):
            unpack_kernel(shapes, len(packs), *args)

        specs = [VMEM] * len(packs)
        return call(kernel, packs, specs, [(s, f32) for s in shapes], name="unpack")

    grad_gate, grad_up, grad_down = unpack(
        (left, right), [gate_weight.shape, up_weight.shape, down_weight.shape]
    )
    grad_query, grad_output = unpack((query_part,), [query_weight.shape, output_weight.shape])
    grad_key, grad_value, wide_gains, head_gains = unpack(
        (both_part,),
        [key_weight.shape, value_weight.shape, (gain_pad, 2 * lanes), (gain_pad, lanes)],
    )
    gain_shards = [wide_gains[i, :rows] for i in range(4)]
    gain_shards += [head_gains[i, : query_gain.shape[0]] for i in (4, 5)]
    return (
        hidden_out[None],
        grad_input[None],
        grad_query,
        grad_key,
        grad_value,
        grad_output,
        grad_gate,
        grad_up,
        grad_down,
        *gain_shards,
    )


def solution(mesh):
    token = P("fsdp", "ctx", None)
    weight = P("fsdp", None)
    gain = P("fsdp")
    return jax.shard_map(
        on_device,
        mesh=mesh,
        in_specs=(token, P("fsdp", "ctx")) + (weight,) * 7 + (gain,) * 6 + (token,),
        out_specs=(token, token) + (weight,) * 7 + (gain,) * 6,
        check_vma=False,
    )
```

```python
import jax
import jax.numpy as jnp
from jax import lax
from jax.experimental import pallas as pl
from jax.experimental.pallas import tpu as pltpu
from jax.sharding import PartitionSpec as P

eps = 1e-06
rope_base = 1000000.0
lanes = 128
order = (0, 2, 1, 3)
vmem_bytes = 16 * 1024 * 1024
gain_pad = 16
f32 = jnp.float32
bf16 = jnp.bfloat16

ANY = pl.BlockSpec(memory_space=pl.ANY)
SMEM = pl.BlockSpec(memory_space=pltpu.SMEM)
VMEM = pl.BlockSpec(memory_space=pltpu.VMEM)


def tie(*values):
    return lax.optimization_barrier(values)


def call(kernel, inputs, specs, outs, scratch=(), flops=0, limit=vmem_bytes, name=None):
    return pl.pallas_call(
        kernel,
        out_shape=tuple(jax.ShapeDtypeStruct(s, d) for s, d in outs),
        in_specs=list(specs),
        out_specs=tuple(VMEM for _ in outs),
        scratch_shapes=list(scratch),
        compiler_params=pltpu.CompilerParams(vmem_limit_bytes=limit),
        cost_estimate=pl.CostEstimate(flops=1, bytes_accessed=1, transcendentals=0),
        name=name,
    )(*inputs)


def nn(left, right):
    return lax.dot_general(left, right, (((1,), (0,)), ((), ())), preferred_element_type=f32)


def nt(left, right):
    return lax.dot_general(left, right, (((1,), (1,)), ((), ())), preferred_element_type=f32)


def tn(left, right):
    return lax.dot_general(left, right, (((0,), (0,)), ((), ())), preferred_element_type=f32)


def unit(value):
    inverse = lax.rsqrt(jnp.mean(value * value, axis=-1, keepdims=True) + eps)
    return value * inverse, inverse


def unit_back(hat, inverse, grad_hat):
    return inverse * (grad_hat - hat * jnp.mean(grad_hat * hat, axis=-1, keepdims=True))


def spin(value, cosine, sine):
    half = value.shape[-1] // 2
    first, second = value[:, :half], value[:, half:]
    return jnp.concatenate(
        [first * cosine - second * sine, second * cosine + first * sine], axis=-1
    )


def place(index, pairs, full, sems, columns=None):
    rows = full.shape[0] // 4
    pitch = pairs[0].shape[0] // 2
    copies = []
    for step in range(4):
        begin = pl.multiple_of((index ^ step) * rows, 16)
        source = pairs[step % 2].at[pl.ds((step // 2) * pitch, rows)]
        if columns is not None:
            source = source.at[:, pl.ds(columns, full.shape[1])]
        copy = pltpu.make_async_copy(source, full.at[pl.ds(begin, rows)], sems.at[step])
        copy.start()
        copies.append(copy)
    return copies


def finish(copies):
    for copy in copies:
        copy.wait()


def kv_kernel(
    info, hidden, cosine, sine,
    b0, b1,
    normed_out, key_raw_out, kv_out, gains_out,
    both_full, gain_parts, sems,
):
    index = info[0]
    copies = place(index, (b0, b1), both_full, sems.at[0])
    model = hidden.shape[1]
    rows = model // 4
    width = key_raw_out.shape[1]
    piece = width // 4
    gain_copies = []
    for step in range(4):
        begin = pl.multiple_of((index ^ step) * gain_pad, gain_pad)
        source = (b0, b1)[step % 2].at[pl.ds((step // 2) * (rows + gain_pad) + rows, gain_pad)]
        copy = pltpu.make_async_copy(
            source, gain_parts.at[pl.ds(begin, gain_pad)], sems.at[1, step]
        )
        copy.start()
        gain_copies.append(copy)
    hat, _ = unit(hidden[...].astype(f32))
    finish(gain_copies)
    span = 2 * lanes
    line = lax.broadcasted_iota(jnp.int32, (span, model), 0)
    column = lax.broadcasted_iota(jnp.int32, (span, model), 1)
    wide_gain = jnp.zeros((gain_pad, model), f32)
    head_gain = jnp.zeros((gain_pad, model), f32)
    for owner in range(4):
        values = gain_parts[owner * gain_pad : (owner + 1) * gain_pad, :span]
        spots = (column == line + owner * rows) & (line < rows)
        wide_gain += nn(values, spots.astype(f32).astype(bf16))
        spots = (column == line + owner * piece) & (line < piece)
        head_gain += nn(values, spots.astype(f32).astype(bf16))
    which = lax.broadcasted_iota(jnp.int32, (gain_pad, model), 0)
    gains = jnp.where(which < 4, wide_gain, head_gain)
    gains_out[...] = gains
    normed = (hat * (1.0 + gains[0:1, :])).astype(bf16)
    normed_out[...] = normed
    finish(copies)
    raw = nn(normed, both_full[:, :width])
    key_raw_out[...] = raw
    hat, _ = unit(raw)
    scale = 1.0 + gains[5:6, :width]
    kv_out[:, :width] = spin(hat * scale, cosine[...], sine[...]).astype(bf16)
    kv_out[:, width:] = nn(normed, both_full[:, width:]).astype(bf16)


def query_kernel(
    info, normed, gains, cosine, sine, q0, q1,
    raw_out, query_out, query_full, sems,
):
    finish(place(info[0], (q0, q1), query_full, sems))
    head_dim = 2 * cosine.shape[1]
    for start in range(0, query_full.shape[1], head_dim):
        part = slice(start, start + head_dim)
        raw = nn(normed[...], query_full[:, part])
        raw_out[:, part] = raw
        hat, _ = unit(raw)
        turned = spin(hat * (1.0 + gains[4:5, :head_dim]), cosine[...], sine[...])
        query_out[:, part] = (turned * head_dim ** (-0.5)).astype(bf16)


def attend_kernel(first, count, info, queries, places, *refs):
    chunks = refs[:count]
    refs = refs[count:]
    if not first:
        weighted_in, total_in = refs[:2]
        refs = refs[2:]
    weighted, total = refs
    tokens = queries.shape[0]
    head_dim = chunks[0].shape[1] // 2
    heads = queries.shape[1] // head_dim
    if first:
        weighted[...] = jnp.zeros_like(weighted)
        total[...] = jnp.zeros_like(total)
    else:
        weighted[...] = weighted_in[...]
        total[...] = total_in[...]
    first_row = info[1]
    for number, chunk in enumerate(chunks):
        base = info[2 + number]

        @pl.loop(0, chunk.shape[0] // tokens)
        def _(step):
            start = base + step * tokens

            @pl.when((start >= 0) & (start <= first_row))
            def _():
                local = pl.ds(pl.multiple_of(step * tokens, tokens), tokens)
                row = first_row + lax.broadcasted_iota(jnp.int32, (tokens, tokens), 0)
                col = start + lax.broadcasted_iota(jnp.int32, (tokens, tokens), 1)
                allowed = (col <= row) & (col >= row - places[...])
                keys = chunk[local, :head_dim]
                values = chunk[local, head_dim:]
                for head in range(heads):
                    part = slice(head * head_dim, (head + 1) * head_dim)
                    scores = nt(queries[:, part], keys)
                    expo = jnp.where(allowed, jnp.exp(scores), 0.0)
                    spot = slice(head * lanes, (head + 1) * lanes)
                    total[:, spot] += jnp.sum(expo, axis=1, keepdims=True)
                    weighted[:, part] += nn(expo.astype(bf16), values)


def mix_kernel(
    info, weighted, total, hidden, gains,
    o0, o1, g0, g1,
    attended_out, mixed_out, projected_out, after_out, normed_out, gate_out, up_out, act_out,
    output_full, gate_full, up_full, sems,
):
    index = info[0]
    feed = gate_full.shape[1]
    output_copies = place(index, (o0, o1), output_full, sems.at[0])
    gate_copies = place(index, (g0, g1), gate_full, sems.at[1], 0)
    up_copies = place(index, (g0, g1), up_full, sems.at[2], feed)
    heads = total.shape[1] // lanes
    head_dim = weighted.shape[1] // heads
    for head in range(heads):
        part = slice(head * head_dim, (head + 1) * head_dim)
        ratio = weighted[:, part] / total[:, head * lanes : head * lanes + 1]
        attended_out[:, part] = ratio
        mixed_out[:, part] = ratio.astype(bf16)
    finish(output_copies)
    projected = nn(mixed_out[...], output_full[...])
    projected_out[...] = projected
    hat, _ = unit(projected)
    after = hidden[...].astype(f32) + hat * (1.0 + gains[1:2, :])
    after_out[...] = after
    hat, _ = unit(after)
    normed_out[...] = (hat * (1.0 + gains[2:3, :])).astype(bf16)
    finish(gate_copies)
    finish(up_copies)
    step_width = 512

    @pl.loop(0, gate_full.shape[1] // step_width)
    def _(step):
        part = pl.ds(pl.multiple_of(step * step_width, step_width), step_width)
        gate = nn(normed_out[...], gate_full[:, part])
        up = nn(normed_out[...], up_full[:, part])
        gate_out[:, part] = gate
        up_out[:, part] = up
        inner = 0.7978845608028654 * (gate + 0.044715 * gate * gate * gate)
        act_out[:, part] = (0.5 * gate * (1.0 + jnp.tanh(inner)) * up).astype(bf16)


def store_columns(keep, send, slot, base, rows, block):
    target = keep if slot < 2 else send
    for number in range(block.shape[1] // lanes):
        target[slot % 2, base + number * rows : base + (number + 1) * rows, :] = block[
            :, number * lanes : (number + 1) * lanes
        ].astype(bf16)


def feed_kernel(
    info, act, gate, up, normed, after, cotangent, gains,
    d0, d1,
    hidden_out, d_gate, d_up, gain_grad, keep, send,
    down_full, d_down, turned, sems,
):
    index = info[0]
    finish(place(index, (d0, d1), down_full, sems))
    down = nn(act[...], down_full[...])
    hat, inverse = unit(down)
    scale = 1.0 + gains[3:4, :]
    hidden_out[...] = (after[...] + hat * scale).astype(bf16)
    grad = cotangent[...].astype(f32)
    gain_grad[...] = jnp.sum(grad * hat, axis=0, keepdims=True)
    d_down[...] = unit_back(hat, inverse, grad * scale).astype(bf16)
    turned[...] = normed[...].astype(f32).T.astype(bf16)
    step_width = 512

    @pl.loop(0, down_full.shape[0] // step_width)
    def _(step):
        part = pl.ds(pl.multiple_of(step * step_width, step_width), step_width)
        d_act = nt(d_down[...], down_full[part, :])
        x = gate[:, part]
        curve = jnp.tanh(0.7978845608028654 * (x + 0.044715 * x * x * x))
        slope = 0.5 * (1.0 + curve) + 0.5 * x * (1.0 - curve * curve) * (
            0.7978845608028654 * (1.0 + 3.0 * 0.044715 * x * x)
        )
        d_gate[:, part] = (d_act * up[:, part] * slope).astype(bf16)
        d_up[:, part] = (d_act * (0.5 * x * (1.0 + curve))).astype(bf16)

    model = normed.shape[1]
    rows = model // 4
    wide = gate.shape[1]
    down_rows = wide // 4
    part_rows = (wide // lanes) * rows
    for slot, step in enumerate(order):
        target = keep if slot < 2 else send
        owner = index ^ step
        lhs = turned[pl.ds(pl.multiple_of(owner * rows, 16), rows), :]
        for base, source in ((0, d_gate), (part_rows, d_up)):

            @pl.loop(0, wide // step_width)
            def _(move):
                part = pl.ds(pl.multiple_of(move * step_width, step_width), step_width)
                block = nn(lhs, source[:, part]).astype(bf16)
                for number in range(step_width // lanes):
                    begin = base + (move * (step_width // lanes) + number) * rows
                    target[slot % 2, pl.ds(pl.multiple_of(begin, 16), rows), :] = block[
                        :, number * lanes : (number + 1) * lanes
                    ]

        left = act[:, pl.ds(pl.multiple_of(owner * down_rows, lanes), down_rows)]
        store_columns(keep, send, slot, 2 * part_rows, down_rows, tn(left, d_down[...]))


def feed_back_kernel(
    info, d_gate, d_up, after, projected, attended, total, cotangent, gains,
    g0, g1, o0, o1,
    d_after_out, d_projected_out, d_mixed_out, rows_out, feed_grad, mix_grad,
    gate_full, up_full, output_full, total_grad, sems,
):
    index = info[0]
    gate_copies = place(index, (g0, g1), gate_full, sems.at[0], 0)
    up_copies = place(index, (g0, g1), up_full, sems.at[1], gate_full.shape[1])
    output_copies = place(index, (o0, o1), output_full, sems.at[2])
    finish(gate_copies)
    total_grad[...] = nt(d_gate[...], gate_full[...])
    finish(up_copies)
    grad = total_grad[...] + nt(d_up[...], up_full[...])
    hat, inverse = unit(after[...])
    feed_grad[...] = jnp.sum(grad * hat, axis=0, keepdims=True)
    d_after = cotangent[...].astype(f32) + unit_back(hat, inverse, grad * (1.0 + gains[2:3, :]))
    d_after_out[...] = d_after
    hat, inverse = unit(projected[...])
    mix_grad[...] = jnp.sum(d_after * hat, axis=0, keepdims=True)
    d_projected = unit_back(hat, inverse, d_after * (1.0 + gains[1:2, :])).astype(bf16)
    d_projected_out[...] = d_projected
    finish(output_copies)
    d_mixed = nt(d_projected, output_full[...]).astype(bf16)
    d_mixed_out[...] = d_mixed
    heads = total.shape[1] // lanes
    head_dim = attended.shape[1] // heads
    tokens = attended.shape[0]
    lane = lax.broadcasted_iota(jnp.int32, (tokens, lanes), 1)
    table = jnp.zeros((tokens, lanes), f32)
    for head in range(heads):
        part = slice(head * head_dim, (head + 1) * head_dim)
        delta = jnp.sum(d_mixed[:, part].astype(f32) * attended[:, part], axis=1, keepdims=True)
        table = jnp.where(lane == head, delta, table)
        share = 1.0 / total[:, head * lanes : (head + 1) * lanes]
        table = jnp.where(lane == heads + head, share, table)
    rows_out[...] = table.T[: rows_out.shape[0], :]


def attend_back_kernel(first, count, info, queries, d_mixed, table, places, *refs):
    chunks = refs[:count]
    refs = refs[count:]
    if not first:
        query_in = refs[0]
        refs = refs[1:]
    query_grads = refs[0]
    chunk_grads = refs[1 : 1 + count]
    key_sum, value_sum = refs[1 + count :]
    tokens = queries.shape[0]
    head_dim = chunks[0].shape[1] // 2
    heads = queries.shape[1] // head_dim
    if first:
        query_grads[...] = jnp.zeros_like(query_grads)
    else:
        query_grads[...] = query_in[...]
    first_row = info[1]
    for number, (chunk, chunk_grad) in enumerate(zip(chunks, chunk_grads)):
        base = info[2 + number]
        chunk_grad[...] = jnp.zeros_like(chunk_grad)

        @pl.loop(0, chunk.shape[0] // tokens)
        def _(step):
            start = base + step * tokens

            @pl.when((start >= 0) & (start <= first_row))
            def _():
                local = pl.ds(pl.multiple_of(step * tokens, tokens), tokens)
                row = first_row + lax.broadcasted_iota(jnp.int32, (tokens, tokens), 1)
                col = start + lax.broadcasted_iota(jnp.int32, (tokens, tokens), 0)
                allowed = (col <= row) & (col >= row - places[...])
                keys = chunk[local, :head_dim]
                values = chunk[local, head_dim:]
                for head in range(heads):
                    part = slice(head * head_dim, (head + 1) * head_dim)
                    query = queries[:, part]
                    grad = d_mixed[:, part]
                    expo = jnp.where(allowed, jnp.exp(nt(keys, query)), 0.0)
                    probs = expo * table[heads + head : heads + head + 1, :]
                    back = nt(values, grad) - table[head : head + 1, :]
                    d_scores = (probs * back).astype(bf16)
                    d_value = nn(probs.astype(bf16), grad)
                    d_key = nn(d_scores, query)
                    if head == 0:
                        key_sum[...] = d_key
                        value_sum[...] = d_value
                    else:
                        key_sum[...] += d_key
                        value_sum[...] += d_value
                    query_grads[:, part] += tn(d_scores, keys)
                chunk_grad[local, :head_dim] = key_sum[...].astype(bf16)
                chunk_grad[local, head_dim:] = value_sum[...].astype(bf16)


def unspin(value, cosine, sine):
    half = value.shape[-1] // 2
    first, second = value[:, :half], value[:, half:]
    return jnp.concatenate(
        [first * cosine + second * sine, second * cosine - first * sine], axis=-1
    )


def query_back_kernel(
    info, query_grads, raw, cosine, sine, gains, normed, mixed, d_projected,
    q0, q1,
    d_normed_out, gain_grad, keep, send,
    query_full, d_raw, turned, sems,
):
    index = info[0]
    copies = place(index, (q0, q1), query_full, sems)
    head_dim = 2 * cosine.shape[1]
    wide = raw.shape[1]
    scale = 1.0 + gains[4:5, :head_dim]
    gain_sum = jnp.zeros((1, head_dim), f32)
    for start in range(0, wide, head_dim):
        part = slice(start, start + head_dim)
        hat, inverse = unit(raw[:, part])
        grad = unspin(query_grads[:, part] * head_dim ** (-0.5), cosine[...], sine[...])
        gain_sum += jnp.sum(grad * hat, axis=0, keepdims=True)
        d_raw[:, part] = unit_back(hat, inverse, grad * scale).astype(bf16)
    gain_grad[...] = gain_sum
    turned[...] = normed[...].astype(f32).T.astype(bf16)
    rows = normed.shape[1] // 4
    mixed_rows = mixed.shape[1] // 4
    for slot, step in enumerate(order):
        owner = index ^ step
        lhs = turned[pl.ds(pl.multiple_of(owner * rows, 16), rows), :]
        store_columns(keep, send, slot, 0, rows, nn(lhs, d_raw[...]))
        left = mixed[:, pl.ds(pl.multiple_of(owner * mixed_rows, lanes), mixed_rows)]
        store_columns(
            keep, send, slot, (wide // lanes) * rows, mixed_rows, tn(left, d_projected[...])
        )
    finish(copies)
    d_normed_out[...] = nt(d_raw[...], query_full[...])


def key_back_kernel(
    count, info, cosine, sine, gains, raw, normed, hidden, d_after, d_normed_query,
    mix_grad, feed_grad, final_grad, query_grad, b0, b1, *refs,
):
    parts = refs[:count]
    (
        input_grad, keep, send,
        both_full, d_both, turned, gain_grads, sems,
    ) = refs[count:]
    index = info[0]
    copies = place(index, (b0, b1), both_full, sems)
    width = raw.shape[1]
    both = parts[0][...].astype(f32)
    for piece in parts[1:]:
        both = both + piece[...].astype(f32)
    hat, inverse = unit(raw[...])
    grad = unspin(both[:, :width], cosine[...], sine[...])
    gain_grads[...] = jnp.zeros_like(gain_grads)
    gain_grads[5:6, :width] = jnp.sum(grad * hat, axis=0, keepdims=True)
    d_both[:, :width] = unit_back(hat, inverse, grad * (1.0 + gains[5:6, :width])).astype(bf16)
    d_both[:, width:] = both[:, width:].astype(bf16)
    turned[...] = normed[...].astype(f32).T.astype(bf16)
    rows = normed.shape[1] // 4
    for slot, step in enumerate(order):
        owner = index ^ step
        lhs = turned[pl.ds(pl.multiple_of(owner * rows, 16), rows), :]
        store_columns(keep, send, slot, 0, rows, nn(lhs, d_both[...]))
    finish(copies)
    d_normed = d_normed_query[...] + nt(d_both[...], both_full[...])
    hat, inverse = unit(hidden[...].astype(f32))
    gain_grads[0:1, :] = jnp.sum(d_normed * hat, axis=0, keepdims=True)
    gain_grads[1:2, :] = mix_grad[...]
    gain_grads[2:3, :] = feed_grad[...]
    gain_grads[3:4, :] = final_grad[...]
    gain_grads[4:5, :width] = query_grad[...]
    input_grad[...] = d_after[...] + unit_back(hat, inverse, d_normed * (1.0 + gains[0:1, :]))
    model = normed.shape[1]
    piece = width // 4
    span = 2 * lanes
    line = lax.broadcasted_iota(jnp.int32, (model, span), 0)
    column = lax.broadcasted_iota(jnp.int32, (model, span), 1)
    values = gain_grads[...].astype(bf16)
    base = (2 * width // lanes) * rows
    for slot, step in enumerate(order):
        target = keep if slot < 2 else send
        owner = index ^ step
        spots = (line == column + owner * rows) & (column < rows)
        wide_part = nn(values, spots.astype(f32).astype(bf16)).astype(bf16)
        spots = (line == column + owner * piece) & (column < piece)
        head_part = nn(values, spots.astype(f32).astype(bf16)).astype(bf16)
        begin = base
        for part in (wide_part[:, :lanes], wide_part[:, lanes:], head_part[:, :lanes]):
            target[slot % 2, begin : begin + gain_pad, :] = part
            begin += gain_pad
        target[slot % 2, begin:, :] = jnp.zeros((target.shape[1] - begin, lanes), bf16)


def unpack_kernel(shapes, count, *refs):
    packs, outs = refs[:count], refs[count:]
    number, base = 0, 0
    for out, (rows, width) in zip(outs, shapes):
        for start in range(0, width, lanes):
            if base == packs[number].shape[0]:
                number, base = number + 1, 0
            out[:, start : start + lanes] = packs[number][base : base + rows, :].astype(f32)
            base += rows


def flip(value, axis, bit):
    size = lax.axis_size(axis)
    return lax.ppermute(value, axis, [(i, i ^ bit) for i in range(size)])


def pair_up(shard, far):
    both = jnp.concatenate([shard, far], axis=0)
    return both, flip(both, "fsdp", 1)


def add_low(*values):
    total = values[0].astype(f32)
    for value in values[1:]:
        total = total + value.astype(f32)
    return total.astype(bf16)


def take_half(value, which):
    axis = value.ndim - 2
    half = value.shape[axis] // 2
    return lax.dynamic_slice_in_dim(value, which * half, half, axis)


def ctx_bits():
    return [1 << i for i in range(lax.axis_size("ctx").bit_length() - 1)]


def scatter_step(value, bit):
    mine = (lax.axis_index("ctx") // bit) % 2
    sent = flip(take_half(value, 1 - mine), "ctx", bit)
    return add_low(take_half(value, mine), sent)


def gather_step(value, bit):
    mine = (lax.axis_index("ctx") // bit) % 2
    other = flip(value, "ctx", bit)
    low = jnp.where(mine == 0, value, other)
    high = jnp.where(mine == 0, other, value)
    return jnp.concatenate([low, high], axis=0)


def send_on(value, shift, groups):
    return lax.ppermute(value, "ctx", [(i, i + shift) for i in range(groups - shift)])


def send_back(value, shift, groups):
    return lax.ppermute(value, "ctx", [(i + shift, i) for i in range(groups - shift)])


def on_device(
    hidden_in, positions, query_weight, key_weight, value_weight, output_weight, gate_weight,
    up_weight, down_weight, input_gain, mixer_gain, feed_gain, final_gain, query_gain, key_gain,
    out_grad,
):
    tokens = hidden_in.shape[1]
    model = hidden_in.shape[2]
    rows = key_weight.shape[0]
    head_dim = key_weight.shape[1]
    wide = query_weight.shape[1]
    heads = wide // head_dim
    feed = gate_weight.shape[1]
    mixed_rows = output_weight.shape[0]
    down_rows = down_weight.shape[0]
    me = lax.axis_index("fsdp")
    ctx = lax.axis_index("ctx")
    groups = lax.axis_size("ctx")
    first_row = ctx * tokens

    gains = jnp.zeros((gain_pad, 2 * head_dim), bf16)
    shards = (input_gain, mixer_gain, feed_gain, final_gain, query_gain, key_gain)
    for number, gain in enumerate(shards):
        gains = gains + jnp.pad(
            gain[None], ((number, gain_pad - 1 - number), (0, 2 * head_dim - gain.shape[0]))
        )
    both_shard = jnp.concatenate(
        [jnp.concatenate([key_weight, value_weight], axis=1), gains], axis=0
    )
    far_both = flip(both_shard, "fsdp", 2)
    far_query = flip(query_weight, "fsdp", 2)
    far_both, output_weight = tie(far_both, output_weight)
    far_output = flip(output_weight, "fsdp", 2)
    both_blocks = pair_up(both_shard, far_both)
    feed_pair = jnp.concatenate([gate_weight, up_weight], axis=1)

    hidden = hidden_in[0]
    cotangent = out_grad[0]
    places = positions[0]
    place_col = places[:, None]
    place_row = places[None, :]
    half = head_dim // 2
    freqs = rope_base ** (-(jnp.arange(half, dtype=f32) * 2.0) / head_dim)
    angles = places.astype(f32)[:, None] * freqs[None, :]
    cosine, sine = jnp.cos(angles), jnp.sin(angles)

    def facts(*starts):
        return jnp.stack([me, first_row, *starts]).astype(jnp.int32)

    info = facts()
    sem = pltpu.SemaphoreType.DMA
    token_flops = 2 * tokens * model

    normed, key_raw, kv, gains = call(
        kv_kernel,
        (info, hidden, cosine, sine, *both_blocks),
        [SMEM] + [VMEM] * 3 + [ANY] * 2,
        [
            ((tokens, model), bf16),
            ((tokens, head_dim), f32),
            ((tokens, 2 * head_dim), bf16),
            ((gain_pad, model), f32),
        ],
        [
            pltpu.VMEM((model, 2 * head_dim), bf16),
            pltpu.VMEM((4 * gain_pad, 2 * head_dim), bf16),
            sem((2, 4)),
        ],
        flops=token_flops * 2 * head_dim,
        name="key_value",
    )
    normed, far_query = tie(normed, far_query)

    ring = groups == 8
    if ring:
        side = ctx % 2
        stage = ctx // 2
        moved = [kv, send_on(kv, 2, groups)]
        others = [flip(kv, "ctx", 1)]
        moved[1], far_output, feed_pair = tie(moved[1], far_output, feed_pair)
        moved.append(send_on(moved[1], 2, groups))
        others.append(flip(moved[1], "ctx", 1))
    else:
        gathered = lax.all_gather(kv, "ctx", axis=0, tiled=True)
    query_blocks = pair_up(query_weight, far_query)
    query_raw, queries = call(
        query_kernel,
        (info, normed, gains, cosine, sine, *query_blocks),
        [SMEM] + [VMEM] * 4 + [ANY] * 2,
        [((tokens, wide), f32), ((tokens, wide), bf16)],
        [pltpu.VMEM((model, wide), bf16), sem((4,))],
        flops=token_flops * wide,
        name="query",
    )

    far_feed = flip(feed_pair, "fsdp", 2)
    if ring:
        queries, moved[2], others[1] = tie(queries, moved[2], others[1])
        moved.append(send_on(moved[2], 2, groups))
        others.append(flip(moved[2], "ctx", 1))

    state = ()
    chunk_flops = 4 * tokens * tokens * wide
    sources = []
    for number in range(groups // 2 if ring else 1):
        if ring:
            if number == 1:
                moved[3], total, far_output = tie(moved[3], state[1], far_output)
                state = (state[0], total)
                others.append(flip(moved[3], "ctx", 1))
                output_blocks = pair_up(output_weight, far_output)
            if number == 2:
                total, others[2] = tie(state[1], others[2])
                state = (state[0], total)
            if number == 3:
                far_feed, down_weight, total, output_blocks, others[3] = tie(
                    far_feed, down_weight, state[1], output_blocks, others[3]
                )
                state = (state[0], total)
                feed_blocks = pair_up(feed_pair, far_feed)
                far_down = flip(down_weight, "fsdp", 2)
            arrays = (moved[number], others[number])
            base = (stage - number) * 2
            starts = ((base + side) * tokens, (base + 1 - side) * tokens)
        else:
            arrays, starts = (gathered,), (jnp.int32(0),)
        sources.append((arrays, starts))
        first = number == 0
        count = len(arrays)

        def attend(*args, first=first, count=count):
            attend_kernel(first, count, *args)

        state = call(
            attend,
            (facts(*starts), queries, place_col, *arrays, *state),
            [SMEM] + [VMEM] * (2 + count + len(state)),
            [((tokens, wide), f32), ((tokens, heads * lanes), f32)],
            flops=chunk_flops * 2,
            limit=vmem_bytes if ring else 3 * vmem_bytes,
            name="attend",
        )
    weighted, total = state
    if not ring:
        output_blocks = pair_up(output_weight, far_output)
        feed_blocks = pair_up(feed_pair, far_feed)
        far_down = flip(down_weight, "fsdp", 2)

    attended, mixed, projected, after, normed_feed, gate_value, up_value, activated = call(
        mix_kernel,
        (
            info, weighted, total, hidden, gains,
            *output_blocks, *feed_blocks,
        ),
        [SMEM] + [VMEM] * 4 + [ANY] * 4,
        [
            ((tokens, wide), f32),
            ((tokens, wide), bf16),
            ((tokens, model), f32),
            ((tokens, model), f32),
            ((tokens, model), bf16),
            ((tokens, feed), f32),
            ((tokens, feed), f32),
            ((tokens, feed), bf16),
        ],
        [
            pltpu.VMEM((wide, model), bf16),
            pltpu.VMEM((model, feed), bf16),
            pltpu.VMEM((model, feed), bf16),
            sem((3, 4)),
        ],
        flops=token_flops * (wide + 2 * feed),
        name="mix",
    )
    far_down, mixed = tie(far_down, mixed)
    down_blocks = pair_up(down_weight, far_down)
    feed_rows = 2 * (feed // lanes) * rows + (model // lanes) * down_rows
    hidden_out, d_gate, d_up, grad_final, feed_keep, feed_send = call(
        feed_kernel,
        (
            info, activated, gate_value, up_value, normed_feed, after, cotangent, gains,
            *down_blocks,
        ),
        [SMEM] + [VMEM] * 7 + [ANY] * 2,
        [
            ((tokens, model), bf16),
            ((tokens, feed), bf16),
            ((tokens, feed), bf16),
            ((1, model), f32),
            ((2, feed_rows, lanes), bf16),
            ((2, feed_rows, lanes), bf16),
        ],
        [
            pltpu.VMEM((feed, model), bf16),
            pltpu.VMEM((tokens, model), bf16),
            pltpu.VMEM((model, tokens), bf16),
            sem((4,)),
        ],
        flops=token_flops * 5 * feed,
        name="feed",
    )
    feed_near = flip(feed_send, "fsdp", 1)

    d_after, d_projected, d_mixed, table, grad_feed_gain, grad_mix_gain = call(
        feed_back_kernel,
        (
            info, d_gate, d_up, after, projected, attended, total, cotangent, gains,
            *feed_blocks, *output_blocks,
        ),
        [SMEM] + [VMEM] * 8 + [ANY] * 4,
        [
            ((tokens, model), f32),
            ((tokens, model), bf16),
            ((tokens, wide), bf16),
            ((2 * heads, tokens), f32),
            ((1, model), f32),
            ((1, model), f32),
        ],
        [
            pltpu.VMEM((model, feed), bf16),
            pltpu.VMEM((model, feed), bf16),
            pltpu.VMEM((wide, model), bf16),
            pltpu.VMEM((tokens, model), f32),
            sem((3, 4)),
        ],
        flops=token_flops * (2 * feed + wide),
        name="feed_back",
    )

    feed_near, d_mixed = tie(feed_near, d_mixed)
    gate_rows = (feed // lanes) * rows
    half_rows = feed_rows // 2
    left_sum = add_low(feed_keep[1, :half_rows], feed_near[1, :half_rows])
    right_sum = add_low(feed_keep[:, half_rows:], feed_near[:, half_rows:])
    d_mixed, left_sum, right_sum = tie(d_mixed, left_sum, right_sum)
    left_far = flip(left_sum, "fsdp", 2)
    bits = ctx_bits()
    steps = len(bits)
    turned = [bits[1], bits[0], *bits[2:]]
    right_sum = scatter_step(right_sum, turned[0])

    query_grads = ()
    arrived = []
    waiting = None
    last = len(sources) - 1
    for number, (arrays, starts) in enumerate(reversed(sources)):
        first = number == 0
        count = len(arrays)

        def attend_back(*args, first=first, count=count):
            attend_back_kernel(first, count, *args)

        results = call(
            attend_back,
            (facts(*starts), queries, d_mixed, table, place_row, *arrays, *query_grads),
            [SMEM] + [VMEM] * (4 + count + len(query_grads)),
            [((tokens, wide), f32)] + [(a.shape, bf16) for a in arrays],
            [pltpu.VMEM((tokens, head_dim), f32), pltpu.VMEM((tokens, head_dim), f32)],
            flops=chunk_flops * 5,
            limit=vmem_bytes if ring else 3 * vmem_bytes,
            name="attend_back",
        )
        query_grads = results[:1]
        if not ring:
            arrived.append(
                lax.psum_scatter(results[1], "ctx", scatter_dimension=0, tiled=True)
            )
            continue
        shift = last - number
        own, other = results[1:]
        if waiting is not None:
            crossed, held, *arrived = tie(waiting[1], query_grads[0], *arrived)
            if number == max(last - 2, 1):
                held, right_sum = tie(held, right_sum)
                right_far = flip(right_sum[1], "fsdp", 2)
            query_grads = (held,)
            arrived = [send_back(add_low(waiting[0], crossed, *arrived), 2, groups)]
        waiting = (own, flip(other, "ctx", 1))
    if ring:
        arrived += list(waiting)

    held, left_far = tie(query_grads[0], left_far)
    query_grads = (held,)
    left = add_low(feed_keep[0, :half_rows], feed_near[0, :half_rows], left_far)
    left = scatter_step(left, bits[0])
    if not ring:
        right_far = flip(right_sum[1], "fsdp", 2)
    query_rows = (wide // lanes) * rows
    output_rows = (model // lanes) * mixed_rows
    d_normed_query, grad_query_gain, query_keep, query_send = call(
        query_back_kernel,
        (
            info, query_grads[0], query_raw, cosine, sine, gains, normed, mixed, d_projected,
            *query_blocks,
        ),
        [SMEM] + [VMEM] * 8 + [ANY] * 2,
        [
            ((tokens, model), f32),
            ((1, head_dim), f32),
            ((2, query_rows + output_rows, lanes), bf16),
            ((2, query_rows + output_rows, lanes), bf16),
        ],
        [
            pltpu.VMEM((model, wide), bf16),
            pltpu.VMEM((tokens, wide), bf16),
            pltpu.VMEM((model, tokens), bf16),
            sem((4,)),
        ],
        flops=token_flops * 3 * wide,
        name="query_back",
    )
    arrived_count = len(arrived)
    d_normed_query, right_far, *arrived = tie(d_normed_query, right_far, *arrived)
    query_near = flip(query_send, "fsdp", 1)
    d_after, left, query_near = tie(d_after, left, query_near)
    query_far = flip(add_low(query_keep[1], query_near[1]), "fsdp", 2)
    both_rows = (2 * head_dim // lanes) * rows + lanes

    def key_back(*args):
        key_back_kernel(arrived_count, *args)

    grad_input, both_keep, both_send = call(
        key_back,
        (
            info, cosine, sine, gains, key_raw, normed, hidden, d_after,
            d_normed_query, grad_mix_gain, grad_feed_gain, grad_final, grad_query_gain,
            *both_blocks, *arrived,
        ),
        [SMEM] + [VMEM] * 12 + [ANY] * 2 + [VMEM] * arrived_count,
        [
            ((tokens, model), f32),
            ((2, both_rows, lanes), bf16),
            ((2, both_rows, lanes), bf16),
        ],
        [
            pltpu.VMEM((model, 2 * head_dim), bf16),
            pltpu.VMEM((tokens, 2 * head_dim), bf16),
            pltpu.VMEM((model, tokens), bf16),
            pltpu.VMEM((gain_pad, model), f32),
            sem((4,)),
        ],
        flops=token_flops * 4 * head_dim,
        name="key_back",
    )
    both_near = flip(both_send, "fsdp", 1)

    right = add_low(right_sum[0], right_far)
    query_part = both_part = None
    for number in range(1, 2 * steps + 2):
        if number < steps:
            left = scatter_step(left, bits[number])
            right = scatter_step(right, turned[number])
        elif number < 2 * steps:
            left = gather_step(left, bits[2 * steps - 1 - number])
            right = gather_step(right, turned[2 * steps - 1 - number])
        if number == 1:
            both_far = flip(add_low(both_keep[1], both_near[1]), "fsdp", 2)
            left, right, query_far, both_near = tie(left, right, query_far, both_near)
            query_part = add_low(query_keep[0], query_near[0], query_far)
            continue
        now = number - 2
        if now < steps:
            query_part = scatter_step(query_part, bits[now])
        elif now < 2 * steps:
            query_part = gather_step(query_part, bits[2 * steps - 1 - now])
        if number == 2:
            left, right, query_part, both_far = tie(left, right, query_part, both_far)
            both_part = add_low(both_keep[0], both_near[0], both_far)
            both_part = scatter_step(both_part, bits[0])
            continue
        if number - 2 < steps:
            both_part = add_low(both_part, flip(both_part, "ctx", bits[number - 2]))
        elif number - 2 == steps:
            both_part = gather_step(both_part, bits[0])
        left, right, query_part, both_part = tie(left, right, query_part, both_part)

    def unpack(packs, shapes):
        def kernel(*args):
            unpack_kernel(shapes, len(packs), *args)

        specs = [VMEM] * len(packs)
        return call(kernel, packs, specs, [(s, f32) for s in shapes], name="unpack")

    grad_gate, grad_up, grad_down = unpack(
        (left, right), [gate_weight.shape, up_weight.shape, down_weight.shape]
    )
    grad_query, grad_output = unpack((query_part,), [query_weight.shape, output_weight.shape])
    grad_key, grad_value, wide_gains, head_gains = unpack(
        (both_part,),
        [key_weight.shape, value_weight.shape, (gain_pad, 2 * lanes), (gain_pad, lanes)],
    )
    gain_shards = [wide_gains[i, :rows] for i in range(4)]
    gain_shards += [head_gains[i, : query_gain.shape[0]] for i in (4, 5)]
    return (
        hidden_out[None],
        grad_input[None],
        grad_query,
        grad_key,
        grad_value,
        grad_output,
        grad_gate,
        grad_up,
        grad_down,
        *gain_shards,
    )


def solution(mesh):
    token = P("fsdp", "ctx", None)
    weight = P("fsdp", None)
    gain = P("fsdp")
    return jax.shard_map(
        on_device,
        mesh=mesh,
        in_specs=(token, P("fsdp", "ctx")) + (weight,) * 7 + (gain,) * 6 + (token,),
        out_specs=(token, token) + (weight,) * 7 + (gain,) * 6,
        check_vma=False,
    )
```

```python
import jax
import jax.numpy as jnp
from jax import lax
from jax.experimental import pallas as pl
from jax.experimental.pallas import tpu as pltpu
from jax.sharding import PartitionSpec as P

eps = 1e-06
rope_base = 1000000.0
lanes = 128
order = (0, 2, 1, 3)
vmem_bytes = 8 * 1024 * 1024
large_bytes = 12 * 1024 * 1024
gain_pad = 16
f32 = jnp.float32
bf16 = jnp.bfloat16

ANY = pl.BlockSpec(memory_space=pl.ANY)
SMEM = pl.BlockSpec(memory_space=pltpu.SMEM)
VMEM = pl.BlockSpec(memory_space=pltpu.VMEM)


def tie(*values):
    return lax.optimization_barrier(values)


def call(kernel, inputs, specs, outs, scratch=(), flops=0, limit=vmem_bytes, name=None):
    return pl.pallas_call(
        kernel,
        out_shape=tuple(jax.ShapeDtypeStruct(s, d) for s, d in outs),
        in_specs=list(specs),
        out_specs=tuple(VMEM for _ in outs),
        scratch_shapes=list(scratch),
        compiler_params=pltpu.CompilerParams(vmem_limit_bytes=limit),
        cost_estimate=pl.CostEstimate(flops=1, bytes_accessed=1, transcendentals=0),
        name=name,
    )(*inputs)


def nn(left, right):
    return lax.dot_general(left, right, (((1,), (0,)), ((), ())), preferred_element_type=f32)


def nt(left, right):
    return lax.dot_general(left, right, (((1,), (1,)), ((), ())), preferred_element_type=f32)


def tn(left, right):
    return lax.dot_general(left, right, (((0,), (0,)), ((), ())), preferred_element_type=f32)


def unit(value):
    inverse = lax.rsqrt(jnp.mean(value * value, axis=-1, keepdims=True) + eps)
    return value * inverse, inverse


def unit_back(hat, inverse, grad_hat):
    return inverse * (grad_hat - hat * jnp.mean(grad_hat * hat, axis=-1, keepdims=True))


def spin(value, cosine, sine):
    half = value.shape[-1] // 2
    first, second = value[:, :half], value[:, half:]
    return jnp.concatenate(
        [first * cosine - second * sine, second * cosine + first * sine], axis=-1
    )


def place(index, pairs, full, sems, columns=None):
    rows = full.shape[0] // 4
    pitch = pairs[0].shape[0] // 2
    copies = []
    for step in range(4):
        begin = pl.multiple_of((index ^ step) * rows, 16)
        source = pairs[step % 2].at[pl.ds((step // 2) * pitch, rows)]
        if columns is not None:
            source = source.at[:, pl.ds(columns, full.shape[1])]
        copy = pltpu.make_async_copy(source, full.at[pl.ds(begin, rows)], sems.at[step])
        copy.start()
        copies.append(copy)
    return copies


def finish(copies):
    for copy in copies:
        copy.wait()


def kv_kernel(
    info, hidden, cosine, sine,
    b0, b1,
    normed_out, key_raw_out, kv_out, gains_out,
    both_full, gain_parts, sems,
):
    index = info[0]
    copies = place(index, (b0, b1), both_full, sems.at[0])
    model = hidden.shape[1]
    rows = model // 4
    width = key_raw_out.shape[1]
    piece = width // 4
    gain_copies = []
    for step in range(4):
        begin = pl.multiple_of((index ^ step) * gain_pad, gain_pad)
        source = (b0, b1)[step % 2].at[pl.ds((step // 2) * (rows + gain_pad) + rows, gain_pad)]
        copy = pltpu.make_async_copy(
            source, gain_parts.at[pl.ds(begin, gain_pad)], sems.at[1, step]
        )
        copy.start()
        gain_copies.append(copy)
    hat, _ = unit(hidden[...].astype(f32))
    finish(gain_copies)
    span = 2 * lanes
    line = lax.broadcasted_iota(jnp.int32, (span, model), 0)
    column = lax.broadcasted_iota(jnp.int32, (span, model), 1)
    wide_gain = jnp.zeros((gain_pad, model), f32)
    head_gain = jnp.zeros((gain_pad, model), f32)
    for owner in range(4):
        values = gain_parts[owner * gain_pad : (owner + 1) * gain_pad, :span]
        spots = (column == line + owner * rows) & (line < rows)
        wide_gain += nn(values, spots.astype(f32).astype(bf16))
        spots = (column == line + owner * piece) & (line < piece)
        head_gain += nn(values, spots.astype(f32).astype(bf16))
    which = lax.broadcasted_iota(jnp.int32, (gain_pad, model), 0)
    gains = jnp.where(which < 4, wide_gain, head_gain)
    gains_out[...] = gains
    normed = (hat * (1.0 + gains[0:1, :])).astype(bf16)
    normed_out[...] = normed
    finish(copies)
    raw = nn(normed, both_full[:, :width])
    key_raw_out[...] = raw
    hat, _ = unit(raw)
    scale = 1.0 + gains[5:6, :width]
    kv_out[:, :width] = spin(hat * scale, cosine[...], sine[...]).astype(bf16)
    kv_out[:, width:] = nn(normed, both_full[:, width:]).astype(bf16)


def query_kernel(
    info, normed, gains, cosine, sine, q0, q1,
    raw_out, query_out, query_full, sems,
):
    finish(place(info[0], (q0, q1), query_full, sems))
    head_dim = 2 * cosine.shape[1]
    for start in range(0, query_full.shape[1], head_dim):
        part = slice(start, start + head_dim)
        raw = nn(normed[...], query_full[:, part])
        raw_out[:, part] = raw
        hat, _ = unit(raw)
        turned = spin(hat * (1.0 + gains[4:5, :head_dim]), cosine[...], sine[...])
        query_out[:, part] = (turned * head_dim ** (-0.5)).astype(bf16)


def attend_kernel(first, count, info, queries, places, *refs):
    chunks = refs[:count]
    refs = refs[count:]
    if not first:
        weighted_in, total_in = refs[:2]
        refs = refs[2:]
    weighted, total = refs
    tokens = queries.shape[0]
    head_dim = chunks[0].shape[1] // 2
    heads = queries.shape[1] // head_dim
    if first:
        weighted[...] = jnp.zeros_like(weighted)
        total[...] = jnp.zeros_like(total)
    else:
        weighted[...] = weighted_in[...]
        total[...] = total_in[...]
    first_row = info[1]
    for number, chunk in enumerate(chunks):
        base = info[2 + number]

        @pl.loop(0, chunk.shape[0] // tokens)
        def _(step):
            start = base + step * tokens

            @pl.when((start >= 0) & (start <= first_row))
            def _():
                local = pl.ds(pl.multiple_of(step * tokens, tokens), tokens)
                row = first_row + lax.broadcasted_iota(jnp.int32, (tokens, tokens), 0)
                col = start + lax.broadcasted_iota(jnp.int32, (tokens, tokens), 1)
                allowed = (col <= row) & (col >= row - places[...])
                keys = chunk[local, :head_dim]
                values = chunk[local, head_dim:]
                for head in range(heads):
                    part = slice(head * head_dim, (head + 1) * head_dim)
                    scores = nt(queries[:, part], keys)
                    expo = jnp.where(allowed, jnp.exp(scores), 0.0)
                    spot = slice(head * lanes, (head + 1) * lanes)
                    total[:, spot] += jnp.sum(expo, axis=1, keepdims=True)
                    weighted[:, part] += nn(expo.astype(bf16), values)


def mix_kernel(
    info, weighted, total, hidden, gains,
    o0, o1, g0, g1,
    attended_out, mixed_out, projected_out, after_out, normed_out, gate_out, up_out, act_out,
    output_full, gate_full, up_full, sems,
):
    index = info[0]
    feed = gate_full.shape[1]
    output_copies = place(index, (o0, o1), output_full, sems.at[0])
    gate_copies = place(index, (g0, g1), gate_full, sems.at[1], 0)
    up_copies = place(index, (g0, g1), up_full, sems.at[2], feed)
    heads = total.shape[1] // lanes
    head_dim = weighted.shape[1] // heads
    for head in range(heads):
        part = slice(head * head_dim, (head + 1) * head_dim)
        ratio = weighted[:, part] / total[:, head * lanes : head * lanes + 1]
        attended_out[:, part] = ratio
        mixed_out[:, part] = ratio.astype(bf16)
    finish(output_copies)
    projected = nn(mixed_out[...], output_full[...])
    projected_out[...] = projected
    hat, _ = unit(projected)
    after = hidden[...].astype(f32) + hat * (1.0 + gains[1:2, :])
    after_out[...] = after
    hat, _ = unit(after)
    normed_out[...] = (hat * (1.0 + gains[2:3, :])).astype(bf16)
    finish(gate_copies)
    finish(up_copies)
    step_width = 512

    @pl.loop(0, gate_full.shape[1] // step_width)
    def _(step):
        part = pl.ds(pl.multiple_of(step * step_width, step_width), step_width)
        gate = nn(normed_out[...], gate_full[:, part])
        up = nn(normed_out[...], up_full[:, part])
        gate_out[:, part] = gate
        up_out[:, part] = up
        inner = 0.7978845608028654 * (gate + 0.044715 * gate * gate * gate)
        act_out[:, part] = (0.5 * gate * (1.0 + jnp.tanh(inner)) * up).astype(bf16)


def store_columns(keep, send, slot, base, rows, block):
    target = keep if slot < 2 else send
    for number in range(block.shape[1] // lanes):
        target[slot % 2, base + number * rows : base + (number + 1) * rows, :] = block[
            :, number * lanes : (number + 1) * lanes
        ].astype(bf16)


def feed_kernel(
    info, act, gate, up, normed, after, cotangent, gains,
    d0, d1,
    hidden_out, d_gate, d_up, gain_grad, keep, send,
    down_full, d_down, turned, sems,
):
    index = info[0]
    finish(place(index, (d0, d1), down_full, sems))
    down = nn(act[...], down_full[...])
    hat, inverse = unit(down)
    scale = 1.0 + gains[3:4, :]
    hidden_out[...] = (after[...] + hat * scale).astype(bf16)
    grad = cotangent[...].astype(f32)
    gain_grad[...] = jnp.sum(grad * hat, axis=0, keepdims=True)
    d_down[...] = unit_back(hat, inverse, grad * scale).astype(bf16)
    turned[...] = normed[...].astype(f32).T.astype(bf16)
    step_width = 512

    @pl.loop(0, down_full.shape[0] // step_width)
    def _(step):
        part = pl.ds(pl.multiple_of(step * step_width, step_width), step_width)
        d_act = nt(d_down[...], down_full[part, :])
        x = gate[:, part]
        curve = jnp.tanh(0.7978845608028654 * (x + 0.044715 * x * x * x))
        slope = 0.5 * (1.0 + curve) + 0.5 * x * (1.0 - curve * curve) * (
            0.7978845608028654 * (1.0 + 3.0 * 0.044715 * x * x)
        )
        d_gate[:, part] = (d_act * up[:, part] * slope).astype(bf16)
        d_up[:, part] = (d_act * (0.5 * x * (1.0 + curve))).astype(bf16)

    model = normed.shape[1]
    rows = model // 4
    wide = gate.shape[1]
    down_rows = wide // 4
    part_rows = (wide // lanes) * rows
    for slot, step in enumerate(order):
        target = keep if slot < 2 else send
        owner = index ^ step
        lhs = turned[pl.ds(pl.multiple_of(owner * rows, 16), rows), :]
        for base, source in ((0, d_gate), (part_rows, d_up)):

            @pl.loop(0, wide // step_width)
            def _(move):
                part = pl.ds(pl.multiple_of(move * step_width, step_width), step_width)
                block = nn(lhs, source[:, part]).astype(bf16)
                for number in range(step_width // lanes):
                    begin = base + (move * (step_width // lanes) + number) * rows
                    target[slot % 2, pl.ds(pl.multiple_of(begin, 16), rows), :] = block[
                        :, number * lanes : (number + 1) * lanes
                    ]

        left = act[:, pl.ds(pl.multiple_of(owner * down_rows, lanes), down_rows)]
        store_columns(keep, send, slot, 2 * part_rows, down_rows, tn(left, d_down[...]))


def feed_back_kernel(
    info, d_gate, d_up, after, projected, attended, total, cotangent, gains,
    g0, g1, o0, o1,
    d_after_out, d_projected_out, d_mixed_out, rows_out, feed_grad, mix_grad,
    gate_full, up_full, output_full, total_grad, sems,
):
    index = info[0]
    gate_copies = place(index, (g0, g1), gate_full, sems.at[0], 0)
    up_copies = place(index, (g0, g1), up_full, sems.at[1], gate_full.shape[1])
    output_copies = place(index, (o0, o1), output_full, sems.at[2])
    finish(gate_copies)
    total_grad[...] = nt(d_gate[...], gate_full[...])
    finish(up_copies)
    grad = total_grad[...] + nt(d_up[...], up_full[...])
    hat, inverse = unit(after[...])
    feed_grad[...] = jnp.sum(grad * hat, axis=0, keepdims=True)
    d_after = cotangent[...].astype(f32) + unit_back(hat, inverse, grad * (1.0 + gains[2:3, :]))
    d_after_out[...] = d_after
    hat, inverse = unit(projected[...])
    mix_grad[...] = jnp.sum(d_after * hat, axis=0, keepdims=True)
    d_projected = unit_back(hat, inverse, d_after * (1.0 + gains[1:2, :])).astype(bf16)
    d_projected_out[...] = d_projected
    finish(output_copies)
    d_mixed = nt(d_projected, output_full[...]).astype(bf16)
    d_mixed_out[...] = d_mixed
    heads = total.shape[1] // lanes
    head_dim = attended.shape[1] // heads
    tokens = attended.shape[0]
    lane = lax.broadcasted_iota(jnp.int32, (tokens, lanes), 1)
    table = jnp.zeros((tokens, lanes), f32)
    for head in range(heads):
        part = slice(head * head_dim, (head + 1) * head_dim)
        delta = jnp.sum(d_mixed[:, part].astype(f32) * attended[:, part], axis=1, keepdims=True)
        table = jnp.where(lane == head, delta, table)
        share = 1.0 / total[:, head * lanes : (head + 1) * lanes]
        table = jnp.where(lane == heads + head, share, table)
    rows_out[...] = table.T[: rows_out.shape[0], :]


def attend_back_kernel(first, count, info, queries, d_mixed, table, places, *refs):
    chunks = refs[:count]
    refs = refs[count:]
    if not first:
        query_in = refs[0]
        refs = refs[1:]
    query_grads = refs[0]
    chunk_grads = refs[1 : 1 + count]
    key_sum, value_sum = refs[1 + count :]
    tokens = queries.shape[0]
    head_dim = chunks[0].shape[1] // 2
    heads = queries.shape[1] // head_dim
    if first:
        query_grads[...] = jnp.zeros_like(query_grads)
    else:
        query_grads[...] = query_in[...]
    first_row = info[1]
    for number, (chunk, chunk_grad) in enumerate(zip(chunks, chunk_grads)):
        base = info[2 + number]
        chunk_grad[...] = jnp.zeros_like(chunk_grad)

        @pl.loop(0, chunk.shape[0] // tokens)
        def _(step):
            start = base + step * tokens

            @pl.when((start >= 0) & (start <= first_row))
            def _():
                local = pl.ds(pl.multiple_of(step * tokens, tokens), tokens)
                row = first_row + lax.broadcasted_iota(jnp.int32, (tokens, tokens), 1)
                col = start + lax.broadcasted_iota(jnp.int32, (tokens, tokens), 0)
                allowed = (col <= row) & (col >= row - places[...])
                keys = chunk[local, :head_dim]
                values = chunk[local, head_dim:]
                for head in range(heads):
                    part = slice(head * head_dim, (head + 1) * head_dim)
                    query = queries[:, part]
                    grad = d_mixed[:, part]
                    expo = jnp.where(allowed, jnp.exp(nt(keys, query)), 0.0)
                    probs = expo * table[heads + head : heads + head + 1, :]
                    back = nt(values, grad) - table[head : head + 1, :]
                    d_scores = (probs * back).astype(bf16)
                    d_value = nn(probs.astype(bf16), grad)
                    d_key = nn(d_scores, query)
                    if head == 0:
                        key_sum[...] = d_key
                        value_sum[...] = d_value
                    else:
                        key_sum[...] += d_key
                        value_sum[...] += d_value
                    query_grads[:, part] += tn(d_scores, keys)
                chunk_grad[local, :head_dim] = key_sum[...].astype(bf16)
                chunk_grad[local, head_dim:] = value_sum[...].astype(bf16)


def unspin(value, cosine, sine):
    half = value.shape[-1] // 2
    first, second = value[:, :half], value[:, half:]
    return jnp.concatenate(
        [first * cosine + second * sine, second * cosine - first * sine], axis=-1
    )


def query_back_kernel(
    info, query_grads, raw, cosine, sine, gains, normed, mixed, d_projected,
    q0, q1,
    d_normed_out, gain_grad, keep, send,
    query_full, d_raw, turned, sems,
):
    index = info[0]
    copies = place(index, (q0, q1), query_full, sems)
    head_dim = 2 * cosine.shape[1]
    wide = raw.shape[1]
    scale = 1.0 + gains[4:5, :head_dim]
    gain_sum = jnp.zeros((1, head_dim), f32)
    for start in range(0, wide, head_dim):
        part = slice(start, start + head_dim)
        hat, inverse = unit(raw[:, part])
        grad = unspin(query_grads[:, part] * head_dim ** (-0.5), cosine[...], sine[...])
        gain_sum += jnp.sum(grad * hat, axis=0, keepdims=True)
        d_raw[:, part] = unit_back(hat, inverse, grad * scale).astype(bf16)
    gain_grad[...] = gain_sum
    turned[...] = normed[...].astype(f32).T.astype(bf16)
    rows = normed.shape[1] // 4
    mixed_rows = mixed.shape[1] // 4
    for slot, step in enumerate(order):
        owner = index ^ step
        lhs = turned[pl.ds(pl.multiple_of(owner * rows, 16), rows), :]
        store_columns(keep, send, slot, 0, rows, nn(lhs, d_raw[...]))
        left = mixed[:, pl.ds(pl.multiple_of(owner * mixed_rows, lanes), mixed_rows)]
        store_columns(
            keep, send, slot, (wide // lanes) * rows, mixed_rows, tn(left, d_projected[...])
        )
    finish(copies)
    d_normed_out[...] = nt(d_raw[...], query_full[...])


def key_back_kernel(
    count, info, cosine, sine, gains, raw, normed, hidden, d_after, d_normed_query,
    mix_grad, feed_grad, final_grad, query_grad, keep_in, send_in, b0, b1, *refs,
):
    parts = refs[:count]
    (
        input_grad, keep, send,
        both_full, d_both, turned, gain_grads, sems,
    ) = refs[count:]
    index = info[0]
    copies = place(index, (b0, b1), both_full, sems)
    width = raw.shape[1]
    both = parts[0][...].astype(f32)
    for piece in parts[1:]:
        both = both + piece[...].astype(f32)
    hat, inverse = unit(raw[...])
    grad = unspin(both[:, :width], cosine[...], sine[...])
    gain_grads[...] = jnp.zeros_like(gain_grads)
    gain_grads[5:6, :width] = jnp.sum(grad * hat, axis=0, keepdims=True)
    d_both[:, :width] = unit_back(hat, inverse, grad * (1.0 + gains[5:6, :width])).astype(bf16)
    d_both[:, width:] = both[:, width:].astype(bf16)
    turned[...] = normed[...].astype(f32).T.astype(bf16)
    rows = normed.shape[1] // 4
    base = keep_in.shape[1]
    keep[:, :base, :] = keep_in[...]
    send[:, :base, :] = send_in[...]
    for slot, step in enumerate(order):
        owner = index ^ step
        lhs = turned[pl.ds(pl.multiple_of(owner * rows, 16), rows), :]
        store_columns(keep, send, slot, base, rows, nn(lhs, d_both[...]))
    finish(copies)
    d_normed = d_normed_query[...] + nt(d_both[...], both_full[...])
    hat, inverse = unit(hidden[...].astype(f32))
    gain_grads[0:1, :] = jnp.sum(d_normed * hat, axis=0, keepdims=True)
    gain_grads[1:2, :] = mix_grad[...]
    gain_grads[2:3, :] = feed_grad[...]
    gain_grads[3:4, :] = final_grad[...]
    gain_grads[4:5, :width] = query_grad[...]
    input_grad[...] = d_after[...] + unit_back(hat, inverse, d_normed * (1.0 + gains[0:1, :]))
    model = normed.shape[1]
    piece = width // 4
    span = 2 * lanes
    line = lax.broadcasted_iota(jnp.int32, (model, span), 0)
    column = lax.broadcasted_iota(jnp.int32, (model, span), 1)
    values = gain_grads[...].astype(bf16)
    base += (2 * width // lanes) * rows
    for slot, step in enumerate(order):
        target = keep if slot < 2 else send
        owner = index ^ step
        spots = (line == column + owner * rows) & (column < rows)
        wide_part = nn(values, spots.astype(f32).astype(bf16)).astype(bf16)
        spots = (line == column + owner * piece) & (column < piece)
        head_part = nn(values, spots.astype(f32).astype(bf16)).astype(bf16)
        begin = base
        for part in (wide_part[:, :lanes], wide_part[:, lanes:], head_part[:, :lanes]):
            target[slot % 2, begin : begin + gain_pad, :] = part
            begin += gain_pad
        target[slot % 2, begin:, :] = jnp.zeros((target.shape[1] - begin, lanes), bf16)


def unpack_kernel(shapes, count, *refs):
    packs, outs = refs[:count], refs[count:]
    number, base = 0, 0
    for out, (rows, width) in zip(outs, shapes):
        for start in range(0, width, lanes):
            if base == packs[number].shape[0]:
                number, base = number + 1, 0
            out[:, start : start + lanes] = packs[number][base : base + rows, :].astype(f32)
            base += rows


def flip(value, axis, bit):
    size = lax.axis_size(axis)
    return lax.ppermute(value, axis, [(i, i ^ bit) for i in range(size)])


def pair_up(shard, far):
    both = jnp.concatenate([shard, far], axis=0)
    return both, flip(both, "fsdp", 1)


def add_low(*values):
    total = values[0].astype(f32)
    for value in values[1:]:
        total = total + value.astype(f32)
    return total.astype(bf16)


def take_half(value, which):
    axis = value.ndim - 2
    half = value.shape[axis] // 2
    return lax.dynamic_slice_in_dim(value, which * half, half, axis)


def ctx_bits():
    return [1 << i for i in range(lax.axis_size("ctx").bit_length() - 1)]


def scatter_step(value, bit):
    mine = (lax.axis_index("ctx") // bit) % 2
    sent = flip(take_half(value, 1 - mine), "ctx", bit)
    return add_low(take_half(value, mine), sent)


def gather_step(value, bit):
    mine = (lax.axis_index("ctx") // bit) % 2
    other = flip(value, "ctx", bit)
    low = jnp.where(mine == 0, value, other)
    high = jnp.where(mine == 0, other, value)
    return jnp.concatenate([low, high], axis=0)


def send_on(value, shift, groups):
    return lax.ppermute(value, "ctx", [(i, i + shift) for i in range(groups - shift)])


def send_back(value, shift, groups):
    return lax.ppermute(value, "ctx", [(i + shift, i) for i in range(groups - shift)])


def on_device(
    hidden_in, positions, query_weight, key_weight, value_weight, output_weight, gate_weight,
    up_weight, down_weight, input_gain, mixer_gain, feed_gain, final_gain, query_gain, key_gain,
    out_grad,
):
    tokens = hidden_in.shape[1]
    model = hidden_in.shape[2]
    rows = key_weight.shape[0]
    head_dim = key_weight.shape[1]
    wide = query_weight.shape[1]
    heads = wide // head_dim
    feed = gate_weight.shape[1]
    mixed_rows = output_weight.shape[0]
    down_rows = down_weight.shape[0]
    me = lax.axis_index("fsdp")
    ctx = lax.axis_index("ctx")
    groups = lax.axis_size("ctx")
    first_row = ctx * tokens

    gains = jnp.zeros((gain_pad, 2 * head_dim), bf16)
    shards = (input_gain, mixer_gain, feed_gain, final_gain, query_gain, key_gain)
    for number, gain in enumerate(shards):
        gains = gains + jnp.pad(
            gain[None], ((number, gain_pad - 1 - number), (0, 2 * head_dim - gain.shape[0]))
        )
    both_shard = jnp.concatenate(
        [jnp.concatenate([key_weight, value_weight], axis=1), gains], axis=0
    )
    far_both = flip(both_shard, "fsdp", 2)
    far_query = flip(query_weight, "fsdp", 2)
    far_both, output_weight = tie(far_both, output_weight)
    far_output = flip(output_weight, "fsdp", 2)
    both_blocks = pair_up(both_shard, far_both)
    feed_pair = jnp.concatenate([gate_weight, up_weight], axis=1)

    hidden = hidden_in[0]
    cotangent = out_grad[0]
    places = positions[0]
    place_col = places[:, None]
    place_row = places[None, :]
    half = head_dim // 2
    freqs = rope_base ** (-(jnp.arange(half, dtype=f32) * 2.0) / head_dim)
    angles = places.astype(f32)[:, None] * freqs[None, :]
    cosine, sine = jnp.cos(angles), jnp.sin(angles)

    def facts(*starts):
        return jnp.stack([me, first_row, *starts]).astype(jnp.int32)

    info = facts()
    sem = pltpu.SemaphoreType.DMA
    token_flops = 2 * tokens * model

    normed, key_raw, kv, gains = call(
        kv_kernel,
        (info, hidden, cosine, sine, *both_blocks),
        [SMEM] + [VMEM] * 3 + [ANY] * 2,
        [
            ((tokens, model), bf16),
            ((tokens, head_dim), f32),
            ((tokens, 2 * head_dim), bf16),
            ((gain_pad, model), f32),
        ],
        [
            pltpu.VMEM((model, 2 * head_dim), bf16),
            pltpu.VMEM((4 * gain_pad, 2 * head_dim), bf16),
            sem((2, 4)),
        ],
        flops=token_flops * 2 * head_dim,
        name="key_value",
    )
    normed, far_query = tie(normed, far_query)

    ring = groups == 8
    if ring:
        side = ctx % 2
        stage = ctx // 2
        moved = [kv, send_on(kv, 2, groups)]
        others = [flip(kv, "ctx", 1)]
        moved[1], far_output, feed_pair = tie(moved[1], far_output, feed_pair)
        moved.append(send_on(moved[1], 2, groups))
        others.append(flip(moved[1], "ctx", 1))
    else:
        gathered = lax.all_gather(kv, "ctx", axis=0, tiled=True)
    query_blocks = pair_up(query_weight, far_query)
    query_raw, queries = call(
        query_kernel,
        (info, normed, gains, cosine, sine, *query_blocks),
        [SMEM] + [VMEM] * 4 + [ANY] * 2,
        [((tokens, wide), f32), ((tokens, wide), bf16)],
        [pltpu.VMEM((model, wide), bf16), sem((4,))],
        flops=token_flops * wide,
        name="query",
    )

    far_feed = flip(feed_pair, "fsdp", 2)
    if ring:
        queries, moved[2], others[1] = tie(queries, moved[2], others[1])
        moved.append(send_on(moved[2], 2, groups))
        others.append(flip(moved[2], "ctx", 1))

    state = ()
    chunk_flops = 4 * tokens * tokens * wide
    sources = []
    for number in range(groups // 2 if ring else 1):
        if ring:
            if number == 1:
                moved[3], total, far_output = tie(moved[3], state[1], far_output)
                state = (state[0], total)
                others.append(flip(moved[3], "ctx", 1))
                output_blocks = pair_up(output_weight, far_output)
            if number == 2:
                total, others[2] = tie(state[1], others[2])
                state = (state[0], total)
            if number == 3:
                far_feed, down_weight, total, output_blocks, others[3] = tie(
                    far_feed, down_weight, state[1], output_blocks, others[3]
                )
                state = (state[0], total)
                feed_blocks = pair_up(feed_pair, far_feed)
                far_down = flip(down_weight, "fsdp", 2)
            arrays = (moved[number], others[number])
            base = (stage - number) * 2
            starts = ((base + side) * tokens, (base + 1 - side) * tokens)
        else:
            arrays, starts = (gathered,), (jnp.int32(0),)
        sources.append((arrays, starts))
        first = number == 0
        count = len(arrays)

        def attend(*args, first=first, count=count):
            attend_kernel(first, count, *args)

        state = call(
            attend,
            (facts(*starts), queries, place_col, *arrays, *state),
            [SMEM] + [VMEM] * (2 + count + len(state)),
            [((tokens, wide), f32), ((tokens, heads * lanes), f32)],
            flops=chunk_flops * 2,
            limit=vmem_bytes if ring else 48 * 1024 * 1024,
            name="attend",
        )
    weighted, total = state
    if not ring:
        output_blocks = pair_up(output_weight, far_output)
        feed_blocks = pair_up(feed_pair, far_feed)
        far_down = flip(down_weight, "fsdp", 2)

    attended, mixed, projected, after, normed_feed, gate_value, up_value, activated = call(
        mix_kernel,
        (
            info, weighted, total, hidden, gains,
            *output_blocks, *feed_blocks,
        ),
        [SMEM] + [VMEM] * 4 + [ANY] * 4,
        [
            ((tokens, wide), f32),
            ((tokens, wide), bf16),
            ((tokens, model), f32),
            ((tokens, model), f32),
            ((tokens, model), bf16),
            ((tokens, feed), f32),
            ((tokens, feed), f32),
            ((tokens, feed), bf16),
        ],
        [
            pltpu.VMEM((wide, model), bf16),
            pltpu.VMEM((model, feed), bf16),
            pltpu.VMEM((model, feed), bf16),
            sem((3, 4)),
        ],
        flops=token_flops * (wide + 2 * feed),
        limit=large_bytes,
        name="mix",
    )
    far_down, mixed = tie(far_down, mixed)
    down_blocks = pair_up(down_weight, far_down)
    feed_rows = 2 * (feed // lanes) * rows + (model // lanes) * down_rows
    hidden_out, d_gate, d_up, grad_final, feed_keep, feed_send = call(
        feed_kernel,
        (
            info, activated, gate_value, up_value, normed_feed, after, cotangent, gains,
            *down_blocks,
        ),
        [SMEM] + [VMEM] * 7 + [ANY] * 2,
        [
            ((tokens, model), bf16),
            ((tokens, feed), bf16),
            ((tokens, feed), bf16),
            ((1, model), f32),
            ((2, feed_rows, lanes), bf16),
            ((2, feed_rows, lanes), bf16),
        ],
        [
            pltpu.VMEM((feed, model), bf16),
            pltpu.VMEM((tokens, model), bf16),
            pltpu.VMEM((model, tokens), bf16),
            sem((4,)),
        ],
        flops=token_flops * 5 * feed,
        limit=large_bytes,
        name="feed",
    )
    feed_near = flip(feed_send, "fsdp", 1)

    d_after, d_projected, d_mixed, table, grad_feed_gain, grad_mix_gain = call(
        feed_back_kernel,
        (
            info, d_gate, d_up, after, projected, attended, total, cotangent, gains,
            *feed_blocks, *output_blocks,
        ),
        [SMEM] + [VMEM] * 8 + [ANY] * 4,
        [
            ((tokens, model), f32),
            ((tokens, model), bf16),
            ((tokens, wide), bf16),
            ((2 * heads, tokens), f32),
            ((1, model), f32),
            ((1, model), f32),
        ],
        [
            pltpu.VMEM((model, feed), bf16),
            pltpu.VMEM((model, feed), bf16),
            pltpu.VMEM((wide, model), bf16),
            pltpu.VMEM((tokens, model), f32),
            sem((3, 4)),
        ],
        flops=token_flops * (2 * feed + wide),
        limit=large_bytes,
        name="feed_back",
    )

    feed_near, d_mixed = tie(feed_near, d_mixed)
    gate_rows = (feed // lanes) * rows
    half_rows = feed_rows // 2
    feed_sum = add_low(feed_keep[1], feed_near[1])
    d_mixed, feed_sum = tie(d_mixed, feed_sum)
    feed_far = flip(feed_sum, "fsdp", 2)
    bits = ctx_bits()
    steps = len(bits)
    turned = [bits[1], bits[0], *bits[2:]]

    query_grads = ()
    arrived = []
    waiting = None
    last = len(sources) - 1
    for number, (arrays, starts) in enumerate(reversed(sources)):
        first = number == 0
        count = len(arrays)

        def attend_back(*args, first=first, count=count):
            attend_back_kernel(first, count, *args)

        results = call(
            attend_back,
            (facts(*starts), queries, d_mixed, table, place_row, *arrays, *query_grads),
            [SMEM] + [VMEM] * (4 + count + len(query_grads)),
            [((tokens, wide), f32)] + [(a.shape, bf16) for a in arrays],
            [pltpu.VMEM((tokens, head_dim), f32), pltpu.VMEM((tokens, head_dim), f32)],
            flops=chunk_flops * 5,
            limit=vmem_bytes if ring else 48 * 1024 * 1024,
            name="attend_back",
        )
        query_grads = results[:1]
        if not ring:
            arrived.append(
                lax.psum_scatter(results[1], "ctx", scatter_dimension=0, tiled=True)
            )
            continue
        shift = last - number
        own, other = results[1:]
        if waiting is not None:
            crossed, held, *arrived = tie(waiting[1], query_grads[0], *arrived)
            query_grads = (held,)
            arrived = [send_back(add_low(waiting[0], crossed, *arrived), 2, groups)]
        waiting = (own, flip(other, "ctx", 1))
    if ring:
        arrived += list(waiting)

    query_rows = (wide // lanes) * rows
    output_rows = (model // lanes) * mixed_rows
    both_rows = (2 * head_dim // lanes) * rows + lanes
    pack_rows = query_rows + output_rows + both_rows
    d_normed_query, grad_query_gain, query_keep, query_send = call(
        query_back_kernel,
        (
            info, query_grads[0], query_raw, cosine, sine, gains, normed, mixed, d_projected,
            *query_blocks,
        ),
        [SMEM] + [VMEM] * 8 + [ANY] * 2,
        [
            ((tokens, model), f32),
            ((1, head_dim), f32),
            ((2, query_rows + output_rows, lanes), bf16),
            ((2, query_rows + output_rows, lanes), bf16),
        ],
        [
            pltpu.VMEM((model, wide), bf16),
            pltpu.VMEM((tokens, wide), bf16),
            pltpu.VMEM((model, tokens), bf16),
            sem((4,)),
        ],
        flops=token_flops * 3 * wide,
        name="query_back",
    )
    arrived_count = len(arrived)

    def key_back(*args):
        key_back_kernel(arrived_count, *args)

    grad_input, pack_keep, pack_send = call(
        key_back,
        (
            info, cosine, sine, gains, key_raw, normed, hidden, d_after,
            d_normed_query, grad_mix_gain, grad_feed_gain, grad_final, grad_query_gain,
            query_keep, query_send, *both_blocks, *arrived,
        ),
        [SMEM] + [VMEM] * 14 + [ANY] * 2 + [VMEM] * arrived_count,
        [
            ((tokens, model), f32),
            ((2, pack_rows, lanes), bf16),
            ((2, pack_rows, lanes), bf16),
        ],
        [
            pltpu.VMEM((model, 2 * head_dim), bf16),
            pltpu.VMEM((tokens, 2 * head_dim), bf16),
            pltpu.VMEM((model, tokens), bf16),
            pltpu.VMEM((gain_pad, model), f32),
            sem((4,)),
        ],
        flops=token_flops * 4 * head_dim,
        name="key_back",
    )
    pack_send, feed_far = tie(pack_send, feed_far)
    pack_near = flip(pack_send, "fsdp", 1)

    left = add_low(feed_keep[0, :half_rows], feed_near[0, :half_rows], feed_far[:half_rows])
    right = add_low(feed_keep[0, half_rows:], feed_near[0, half_rows:], feed_far[half_rows:])
    pack = None
    for number in range(2 * steps + 2):
        if number < steps:
            left = scatter_step(left, bits[number])
            right = scatter_step(right, turned[number])
        elif number < 2 * steps:
            left = gather_step(left, bits[2 * steps - 1 - number])
            right = gather_step(right, turned[2 * steps - 1 - number])
        if number == 0:
            pack_far = flip(add_low(pack_keep[1], pack_near[1]), "fsdp", 2)
            left, right = tie(left, right)
        elif number == 1:
            left, right, pack_far = tie(left, right, pack_far)
            pack = add_low(pack_keep[0], pack_near[0], pack_far)
        else:
            now = number - 2
            if now < steps:
                pack = scatter_step(pack, bits[now])
            else:
                pack = gather_step(pack, bits[2 * steps - 1 - now])
            left, right, pack = tie(left, right, pack)

    def unpack(packs, shapes):
        def kernel(*args):
            unpack_kernel(shapes, len(packs), *args)

        specs = [VMEM] * len(packs)
        return call(kernel, packs, specs, [(s, f32) for s in shapes], name="unpack")

    grad_gate, grad_up, grad_down = unpack(
        (left, right), [gate_weight.shape, up_weight.shape, down_weight.shape]
    )
    grad_query, grad_output, grad_key, grad_value, wide_gains, head_gains = unpack(
        (pack,),
        [
            query_weight.shape,
            output_weight.shape,
            key_weight.shape,
            value_weight.shape,
            (gain_pad, 2 * lanes),
            (gain_pad, lanes),
        ],
    )
    gain_shards = [wide_gains[i, :rows] for i in range(4)]
    gain_shards += [head_gains[i, : query_gain.shape[0]] for i in (4, 5)]
    return (
        hidden_out[None],
        grad_input[None],
        grad_query,
        grad_key,
        grad_value,
        grad_output,
        grad_gate,
        grad_up,
        grad_down,
        *gain_shards,
    )


def solution(mesh):
    token = P("fsdp", "ctx", None)
    weight = P("fsdp", None)
    gain = P("fsdp")
    return jax.shard_map(
        on_device,
        mesh=mesh,
        in_specs=(token, P("fsdp", "ctx")) + (weight,) * 7 + (gain,) * 6 + (token,),
        out_specs=(token, token) + (weight,) * 7 + (gain,) * 6,
        check_vma=False,
    )
```

```python
import jax
import jax.numpy as jnp
from jax import lax
from jax.experimental import pallas as pl
from jax.experimental.pallas import tpu as pltpu
from jax.sharding import PartitionSpec as P

eps = 1e-06
rope_base = 1000000.0
lanes = 128
order = (0, 2, 1, 3)
vmem_bytes = 8 * 1024 * 1024
large_bytes = 12 * 1024 * 1024
gain_pad = 16
f32 = jnp.float32
bf16 = jnp.bfloat16

ANY = pl.BlockSpec(memory_space=pl.ANY)
SMEM = pl.BlockSpec(memory_space=pltpu.SMEM)
VMEM = pl.BlockSpec(memory_space=pltpu.VMEM)


def tie(*values):
    return lax.optimization_barrier(values)


def call(kernel, inputs, specs, outs, scratch=(), flops=0, limit=vmem_bytes, name=None):
    return pl.pallas_call(
        kernel,
        out_shape=tuple(jax.ShapeDtypeStruct(s, d) for s, d in outs),
        in_specs=list(specs),
        out_specs=tuple(VMEM for _ in outs),
        scratch_shapes=list(scratch),
        compiler_params=pltpu.CompilerParams(vmem_limit_bytes=limit),
        cost_estimate=pl.CostEstimate(flops=1, bytes_accessed=1, transcendentals=0),
        name=name,
    )(*inputs)


def nn(left, right):
    return lax.dot_general(left, right, (((1,), (0,)), ((), ())), preferred_element_type=f32)


def nt(left, right):
    return lax.dot_general(left, right, (((1,), (1,)), ((), ())), preferred_element_type=f32)


def tn(left, right):
    return lax.dot_general(left, right, (((0,), (0,)), ((), ())), preferred_element_type=f32)


def unit(value):
    inverse = lax.rsqrt(jnp.mean(value * value, axis=-1, keepdims=True) + eps)
    return value * inverse, inverse


def unit_back(hat, inverse, grad_hat):
    return inverse * (grad_hat - hat * jnp.mean(grad_hat * hat, axis=-1, keepdims=True))


def spin(value, cosine, sine):
    half = value.shape[-1] // 2
    first, second = value[:, :half], value[:, half:]
    return jnp.concatenate(
        [first * cosine - second * sine, second * cosine + first * sine], axis=-1
    )


def place(index, pairs, full, sems, columns=None):
    rows = full.shape[0] // 4
    pitch = pairs[0].shape[0] // 2
    copies = []
    for step in range(4):
        begin = pl.multiple_of((index ^ step) * rows, 16)
        source = pairs[step % 2].at[pl.ds((step // 2) * pitch, rows)]
        if columns is not None:
            source = source.at[:, pl.ds(columns, full.shape[1])]
        copy = pltpu.make_async_copy(source, full.at[pl.ds(begin, rows)], sems.at[step])
        copy.start()
        copies.append(copy)
    return copies


def finish(copies):
    for copy in copies:
        copy.wait()


def kv_kernel(
    info, hidden, cosine, sine,
    b0, b1,
    normed_out, key_raw_out, kv_out, gains_out,
    both_full, gain_parts, sems,
):
    index = info[0]
    copies = place(index, (b0, b1), both_full, sems.at[0])
    model = hidden.shape[1]
    rows = model // 4
    width = key_raw_out.shape[1]
    piece = width // 4
    gain_copies = []
    for step in range(4):
        begin = pl.multiple_of((index ^ step) * gain_pad, gain_pad)
        source = (b0, b1)[step % 2].at[pl.ds((step // 2) * (rows + gain_pad) + rows, gain_pad)]
        copy = pltpu.make_async_copy(
            source, gain_parts.at[pl.ds(begin, gain_pad)], sems.at[1, step]
        )
        copy.start()
        gain_copies.append(copy)
    hat, _ = unit(hidden[...].astype(f32))
    finish(gain_copies)
    span = 2 * lanes
    line = lax.broadcasted_iota(jnp.int32, (span, model), 0)
    column = lax.broadcasted_iota(jnp.int32, (span, model), 1)
    wide_gain = jnp.zeros((gain_pad, model), f32)
    head_gain = jnp.zeros((gain_pad, model), f32)
    for owner in range(4):
        values = gain_parts[owner * gain_pad : (owner + 1) * gain_pad, :span]
        spots = (column == line + owner * rows) & (line < rows)
        wide_gain += nn(values, spots.astype(f32).astype(bf16))
        spots = (column == line + owner * piece) & (line < piece)
        head_gain += nn(values, spots.astype(f32).astype(bf16))
    which = lax.broadcasted_iota(jnp.int32, (gain_pad, model), 0)
    gains = jnp.where(which < 4, wide_gain, head_gain)
    gains_out[...] = gains
    normed = (hat * (1.0 + gains[0:1, :])).astype(bf16)
    normed_out[...] = normed
    finish(copies)
    raw = nn(normed, both_full[:, :width])
    key_raw_out[...] = raw
    hat, _ = unit(raw)
    scale = 1.0 + gains[5:6, :width]
    kv_out[:, :width] = spin(hat * scale, cosine[...], sine[...]).astype(bf16)
    kv_out[:, width:] = nn(normed, both_full[:, width:]).astype(bf16)


def query_kernel(
    info, normed, gains, cosine, sine, q0, q1,
    raw_out, query_out, query_full, sems,
):
    finish(place(info[0], (q0, q1), query_full, sems))
    head_dim = 2 * cosine.shape[1]
    for start in range(0, query_full.shape[1], head_dim):
        part = slice(start, start + head_dim)
        raw = nn(normed[...], query_full[:, part])
        raw_out[:, part] = raw
        hat, _ = unit(raw)
        turned = spin(hat * (1.0 + gains[4:5, :head_dim]), cosine[...], sine[...])
        query_out[:, part] = (turned * head_dim ** (-0.5)).astype(bf16)


def attend_kernel(first, count, info, queries, places, *refs):
    chunks = refs[:count]
    refs = refs[count:]
    if not first:
        weighted_in, total_in = refs[:2]
        refs = refs[2:]
    weighted, total = refs
    tokens = queries.shape[0]
    head_dim = chunks[0].shape[1] // 2
    heads = queries.shape[1] // head_dim
    if first:
        weighted[...] = jnp.zeros_like(weighted)
        total[...] = jnp.zeros_like(total)
    else:
        weighted[...] = weighted_in[...]
        total[...] = total_in[...]
    first_row = info[1]
    for number, chunk in enumerate(chunks):
        base = info[2 + number]

        @pl.loop(0, chunk.shape[0] // tokens)
        def _(step):
            start = base + step * tokens

            @pl.when((start >= 0) & (start <= first_row))
            def _():
                local = pl.ds(pl.multiple_of(step * tokens, tokens), tokens)
                row = first_row + lax.broadcasted_iota(jnp.int32, (tokens, tokens), 0)
                col = start + lax.broadcasted_iota(jnp.int32, (tokens, tokens), 1)
                allowed = (col <= row) & (col >= row - places[...])
                keys = chunk[local, :head_dim]
                values = chunk[local, head_dim:]
                for head in range(heads):
                    part = slice(head * head_dim, (head + 1) * head_dim)
                    scores = nt(queries[:, part], keys)
                    expo = jnp.where(allowed, jnp.exp(scores), 0.0)
                    spot = slice(head * lanes, (head + 1) * lanes)
                    total[:, spot] += jnp.sum(expo, axis=1, keepdims=True)
                    weighted[:, part] += nn(expo.astype(bf16), values)


def mix_kernel(
    info, weighted, total, hidden, gains,
    o0, o1, g0, g1,
    attended_out, mixed_out, projected_out, after_out, normed_out, gate_out, up_out, act_out,
    output_full, gate_full, up_full, sems,
):
    index = info[0]
    feed = gate_full.shape[1]
    output_copies = place(index, (o0, o1), output_full, sems.at[0])
    gate_copies = place(index, (g0, g1), gate_full, sems.at[1], 0)
    up_copies = place(index, (g0, g1), up_full, sems.at[2], feed)
    heads = total.shape[1] // lanes
    head_dim = weighted.shape[1] // heads
    for head in range(heads):
        part = slice(head * head_dim, (head + 1) * head_dim)
        ratio = weighted[:, part] / total[:, head * lanes : head * lanes + 1]
        attended_out[:, part] = ratio
        mixed_out[:, part] = ratio.astype(bf16)
    finish(output_copies)
    projected = nn(mixed_out[...], output_full[...])
    projected_out[...] = projected
    hat, _ = unit(projected)
    after = hidden[...].astype(f32) + hat * (1.0 + gains[1:2, :])
    after_out[...] = after
    hat, _ = unit(after)
    normed_out[...] = (hat * (1.0 + gains[2:3, :])).astype(bf16)
    finish(gate_copies)
    finish(up_copies)
    step_width = 512

    @pl.loop(0, gate_full.shape[1] // step_width)
    def _(step):
        part = pl.ds(pl.multiple_of(step * step_width, step_width), step_width)
        gate = nn(normed_out[...], gate_full[:, part])
        up = nn(normed_out[...], up_full[:, part])
        gate_out[:, part] = gate
        up_out[:, part] = up
        inner = 0.7978845608028654 * (gate + 0.044715 * gate * gate * gate)
        act_out[:, part] = (0.5 * gate * (1.0 + jnp.tanh(inner)) * up).astype(bf16)


def store_columns(keep, send, slot, base, rows, block):
    target = keep if slot < 2 else send
    for number in range(block.shape[1] // lanes):
        target[slot % 2, base + number * rows : base + (number + 1) * rows, :] = block[
            :, number * lanes : (number + 1) * lanes
        ].astype(bf16)


def feed_kernel(
    info, act, gate, up, normed, after, cotangent, gains,
    d0, d1,
    hidden_out, d_gate, d_up, gain_grad, keep, send,
    down_full, d_down, turned, sems,
):
    index = info[0]
    finish(place(index, (d0, d1), down_full, sems))
    down = nn(act[...], down_full[...])
    hat, inverse = unit(down)
    scale = 1.0 + gains[3:4, :]
    hidden_out[...] = (after[...] + hat * scale).astype(bf16)
    grad = cotangent[...].astype(f32)
    gain_grad[...] = jnp.sum(grad * hat, axis=0, keepdims=True)
    d_down[...] = unit_back(hat, inverse, grad * scale).astype(bf16)
    turned[...] = normed[...].astype(f32).T.astype(bf16)
    step_width = 512

    @pl.loop(0, down_full.shape[0] // step_width)
    def _(step):
        part = pl.ds(pl.multiple_of(step * step_width, step_width), step_width)
        d_act = nt(d_down[...], down_full[part, :])
        x = gate[:, part]
        curve = jnp.tanh(0.7978845608028654 * (x + 0.044715 * x * x * x))
        slope = 0.5 * (1.0 + curve) + 0.5 * x * (1.0 - curve * curve) * (
            0.7978845608028654 * (1.0 + 3.0 * 0.044715 * x * x)
        )
        d_gate[:, part] = (d_act * up[:, part] * slope).astype(bf16)
        d_up[:, part] = (d_act * (0.5 * x * (1.0 + curve))).astype(bf16)

    model = normed.shape[1]
    rows = model // 4
    wide = gate.shape[1]
    down_rows = wide // 4
    part_rows = (wide // lanes) * rows
    for slot, step in enumerate(order):
        target = keep if slot < 2 else send
        owner = index ^ step
        lhs = turned[pl.ds(pl.multiple_of(owner * rows, 16), rows), :]
        for base, source in ((0, d_gate), (part_rows, d_up)):

            @pl.loop(0, wide // step_width)
            def _(move):
                part = pl.ds(pl.multiple_of(move * step_width, step_width), step_width)
                block = nn(lhs, source[:, part]).astype(bf16)
                for number in range(step_width // lanes):
                    begin = base + (move * (step_width // lanes) + number) * rows
                    target[slot % 2, pl.ds(pl.multiple_of(begin, 16), rows), :] = block[
                        :, number * lanes : (number + 1) * lanes
                    ]

        left = act[:, pl.ds(pl.multiple_of(owner * down_rows, lanes), down_rows)]
        store_columns(keep, send, slot, 2 * part_rows, down_rows, tn(left, d_down[...]))


def feed_back_kernel(
    info, d_gate, d_up, after, projected, attended, total, cotangent, gains,
    g0, g1, o0, o1,
    d_after_out, d_projected_out, d_mixed_out, rows_out, feed_grad, mix_grad,
    gate_full, up_full, output_full, total_grad, sems,
):
    index = info[0]
    gate_copies = place(index, (g0, g1), gate_full, sems.at[0], 0)
    up_copies = place(index, (g0, g1), up_full, sems.at[1], gate_full.shape[1])
    output_copies = place(index, (o0, o1), output_full, sems.at[2])
    finish(gate_copies)
    total_grad[...] = nt(d_gate[...], gate_full[...])
    finish(up_copies)
    grad = total_grad[...] + nt(d_up[...], up_full[...])
    hat, inverse = unit(after[...])
    feed_grad[...] = jnp.sum(grad * hat, axis=0, keepdims=True)
    d_after = cotangent[...].astype(f32) + unit_back(hat, inverse, grad * (1.0 + gains[2:3, :]))
    d_after_out[...] = d_after
    hat, inverse = unit(projected[...])
    mix_grad[...] = jnp.sum(d_after * hat, axis=0, keepdims=True)
    d_projected = unit_back(hat, inverse, d_after * (1.0 + gains[1:2, :])).astype(bf16)
    d_projected_out[...] = d_projected
    finish(output_copies)
    d_mixed = nt(d_projected, output_full[...]).astype(bf16)
    d_mixed_out[...] = d_mixed
    heads = total.shape[1] // lanes
    head_dim = attended.shape[1] // heads
    tokens = attended.shape[0]
    lane = lax.broadcasted_iota(jnp.int32, (tokens, lanes), 1)
    table = jnp.zeros((tokens, lanes), f32)
    for head in range(heads):
        part = slice(head * head_dim, (head + 1) * head_dim)
        delta = jnp.sum(d_mixed[:, part].astype(f32) * attended[:, part], axis=1, keepdims=True)
        table = jnp.where(lane == head, delta, table)
        share = 1.0 / total[:, head * lanes : (head + 1) * lanes]
        table = jnp.where(lane == heads + head, share, table)
    rows_out[...] = table.T[: rows_out.shape[0], :]


def attend_back_kernel(first, count, info, queries, d_mixed, table, places, *refs):
    chunks = refs[:count]
    refs = refs[count:]
    if not first:
        query_in = refs[0]
        refs = refs[1:]
    query_grads = refs[0]
    chunk_grads = refs[1 : 1 + count]
    key_sum, value_sum = refs[1 + count :]
    tokens = queries.shape[0]
    head_dim = chunks[0].shape[1] // 2
    heads = queries.shape[1] // head_dim
    if first:
        query_grads[...] = jnp.zeros_like(query_grads)
    else:
        query_grads[...] = query_in[...]
    first_row = info[1]
    for number, (chunk, chunk_grad) in enumerate(zip(chunks, chunk_grads)):
        base = info[2 + number]
        chunk_grad[...] = jnp.zeros_like(chunk_grad)

        @pl.loop(0, chunk.shape[0] // tokens)
        def _(step):
            start = base + step * tokens

            @pl.when((start >= 0) & (start <= first_row))
            def _():
                local = pl.ds(pl.multiple_of(step * tokens, tokens), tokens)
                row = first_row + lax.broadcasted_iota(jnp.int32, (tokens, tokens), 1)
                col = start + lax.broadcasted_iota(jnp.int32, (tokens, tokens), 0)
                allowed = (col <= row) & (col >= row - places[...])
                keys = chunk[local, :head_dim]
                values = chunk[local, head_dim:]
                for head in range(heads):
                    part = slice(head * head_dim, (head + 1) * head_dim)
                    query = queries[:, part]
                    grad = d_mixed[:, part]
                    expo = jnp.where(allowed, jnp.exp(nt(keys, query)), 0.0)
                    probs = expo * table[heads + head : heads + head + 1, :]
                    back = nt(values, grad) - table[head : head + 1, :]
                    d_scores = (probs * back).astype(bf16)
                    d_value = nn(probs.astype(bf16), grad)
                    d_key = nn(d_scores, query)
                    if head == 0:
                        key_sum[...] = d_key
                        value_sum[...] = d_value
                    else:
                        key_sum[...] += d_key
                        value_sum[...] += d_value
                    query_grads[:, part] += tn(d_scores, keys)
                chunk_grad[local, :head_dim] = key_sum[...].astype(bf16)
                chunk_grad[local, head_dim:] = value_sum[...].astype(bf16)


def unspin(value, cosine, sine):
    half = value.shape[-1] // 2
    first, second = value[:, :half], value[:, half:]
    return jnp.concatenate(
        [first * cosine + second * sine, second * cosine - first * sine], axis=-1
    )


def query_back_kernel(
    info, query_grads, raw, cosine, sine, gains, normed, mixed, d_projected,
    q0, q1,
    d_normed_out, gain_grad, keep, send,
    query_full, d_raw, turned, sems,
):
    index = info[0]
    copies = place(index, (q0, q1), query_full, sems)
    head_dim = 2 * cosine.shape[1]
    wide = raw.shape[1]
    scale = 1.0 + gains[4:5, :head_dim]
    gain_sum = jnp.zeros((1, head_dim), f32)
    for start in range(0, wide, head_dim):
        part = slice(start, start + head_dim)
        hat, inverse = unit(raw[:, part])
        grad = unspin(query_grads[:, part] * head_dim ** (-0.5), cosine[...], sine[...])
        gain_sum += jnp.sum(grad * hat, axis=0, keepdims=True)
        d_raw[:, part] = unit_back(hat, inverse, grad * scale).astype(bf16)
    gain_grad[...] = gain_sum
    turned[...] = normed[...].astype(f32).T.astype(bf16)
    rows = normed.shape[1] // 4
    mixed_rows = mixed.shape[1] // 4
    for slot, step in enumerate(order):
        owner = index ^ step
        lhs = turned[pl.ds(pl.multiple_of(owner * rows, 16), rows), :]
        store_columns(keep, send, slot, 0, rows, nn(lhs, d_raw[...]))
        left = mixed[:, pl.ds(pl.multiple_of(owner * mixed_rows, lanes), mixed_rows)]
        store_columns(
            keep, send, slot, (wide // lanes) * rows, mixed_rows, tn(left, d_projected[...])
        )
    finish(copies)
    d_normed_out[...] = nt(d_raw[...], query_full[...])


def key_back_kernel(
    count, info, cosine, sine, gains, raw, normed, hidden, d_after, d_normed_query,
    mix_grad, feed_grad, final_grad, query_grad, keep_in, send_in, b0, b1, *refs,
):
    parts = refs[:count]
    (
        input_grad, keep, send,
        both_full, d_both, turned, gain_grads, sems,
    ) = refs[count:]
    index = info[0]
    copies = place(index, (b0, b1), both_full, sems)
    width = raw.shape[1]
    both = parts[0][...].astype(f32)
    for piece in parts[1:]:
        both = both + piece[...].astype(f32)
    hat, inverse = unit(raw[...])
    grad = unspin(both[:, :width], cosine[...], sine[...])
    gain_grads[...] = jnp.zeros_like(gain_grads)
    gain_grads[5:6, :width] = jnp.sum(grad * hat, axis=0, keepdims=True)
    d_both[:, :width] = unit_back(hat, inverse, grad * (1.0 + gains[5:6, :width])).astype(bf16)
    d_both[:, width:] = both[:, width:].astype(bf16)
    turned[...] = normed[...].astype(f32).T.astype(bf16)
    rows = normed.shape[1] // 4
    base = keep_in.shape[1]
    keep[:, :base, :] = keep_in[...]
    send[:, :base, :] = send_in[...]
    for slot, step in enumerate(order):
        owner = index ^ step
        lhs = turned[pl.ds(pl.multiple_of(owner * rows, 16), rows), :]
        store_columns(keep, send, slot, base, rows, nn(lhs, d_both[...]))
    finish(copies)
    d_normed = d_normed_query[...] + nt(d_both[...], both_full[...])
    hat, inverse = unit(hidden[...].astype(f32))
    gain_grads[0:1, :] = jnp.sum(d_normed * hat, axis=0, keepdims=True)
    gain_grads[1:2, :] = mix_grad[...]
    gain_grads[2:3, :] = feed_grad[...]
    gain_grads[3:4, :] = final_grad[...]
    gain_grads[4:5, :width] = query_grad[...]
    input_grad[...] = d_after[...] + unit_back(hat, inverse, d_normed * (1.0 + gains[0:1, :]))
    model = normed.shape[1]
    piece = width // 4
    span = 2 * lanes
    line = lax.broadcasted_iota(jnp.int32, (model, span), 0)
    column = lax.broadcasted_iota(jnp.int32, (model, span), 1)
    values = gain_grads[...].astype(bf16)
    base += (2 * width // lanes) * rows
    for slot, step in enumerate(order):
        target = keep if slot < 2 else send
        owner = index ^ step
        spots = (line == column + owner * rows) & (column < rows)
        wide_part = nn(values, spots.astype(f32).astype(bf16)).astype(bf16)
        spots = (line == column + owner * piece) & (column < piece)
        head_part = nn(values, spots.astype(f32).astype(bf16)).astype(bf16)
        begin = base
        for part in (wide_part[:, :lanes], wide_part[:, lanes:], head_part[:, :lanes]):
            target[slot % 2, begin : begin + gain_pad, :] = part
            begin += gain_pad
        target[slot % 2, begin:, :] = jnp.zeros((target.shape[1] - begin, lanes), bf16)


def unpack_kernel(shapes, count, *refs):
    packs, outs = refs[:count], refs[count:]
    number, base = 0, 0
    for out, (rows, width) in zip(outs, shapes):
        for start in range(0, width, lanes):
            if base == packs[number].shape[0]:
                number, base = number + 1, 0
            out[:, start : start + lanes] = packs[number][base : base + rows, :].astype(f32)
            base += rows


def flip(value, axis, bit):
    size = lax.axis_size(axis)
    return lax.ppermute(value, axis, [(i, i ^ bit) for i in range(size)])


def pair_up(shard, far):
    both = jnp.concatenate([shard, far], axis=0)
    return both, flip(both, "fsdp", 1)


def add_low(*values):
    total = values[0].astype(f32)
    for value in values[1:]:
        total = total + value.astype(f32)
    return total.astype(bf16)


def take_half(value, which):
    axis = value.ndim - 2
    half = value.shape[axis] // 2
    return lax.dynamic_slice_in_dim(value, which * half, half, axis)


def ctx_bits():
    return [1 << i for i in range(lax.axis_size("ctx").bit_length() - 1)]


def scatter_step(value, bit):
    mine = (lax.axis_index("ctx") // bit) % 2
    sent = flip(take_half(value, 1 - mine), "ctx", bit)
    return add_low(take_half(value, mine), sent)


def gather_step(value, bit):
    mine = (lax.axis_index("ctx") // bit) % 2
    other = flip(value, "ctx", bit)
    low = jnp.where(mine == 0, value, other)
    high = jnp.where(mine == 0, other, value)
    return jnp.concatenate([low, high], axis=0)


def send_on(value, shift, groups):
    return lax.ppermute(value, "ctx", [(i, i + shift) for i in range(groups - shift)])


def send_back(value, shift, groups):
    return lax.ppermute(value, "ctx", [(i + shift, i) for i in range(groups - shift)])


def on_device(
    hidden_in, positions, query_weight, key_weight, value_weight, output_weight, gate_weight,
    up_weight, down_weight, input_gain, mixer_gain, feed_gain, final_gain, query_gain, key_gain,
    out_grad,
):
    tokens = hidden_in.shape[1]
    model = hidden_in.shape[2]
    rows = key_weight.shape[0]
    head_dim = key_weight.shape[1]
    wide = query_weight.shape[1]
    heads = wide // head_dim
    feed = gate_weight.shape[1]
    mixed_rows = output_weight.shape[0]
    down_rows = down_weight.shape[0]
    me = lax.axis_index("fsdp")
    ctx = lax.axis_index("ctx")
    groups = lax.axis_size("ctx")
    first_row = ctx * tokens

    gains = jnp.zeros((gain_pad, 2 * head_dim), bf16)
    shards = (input_gain, mixer_gain, feed_gain, final_gain, query_gain, key_gain)
    for number, gain in enumerate(shards):
        gains = gains + jnp.pad(
            gain[None], ((number, gain_pad - 1 - number), (0, 2 * head_dim - gain.shape[0]))
        )
    both_shard = jnp.concatenate(
        [jnp.concatenate([key_weight, value_weight], axis=1), gains], axis=0
    )
    far_both = flip(both_shard, "fsdp", 2)
    far_query = flip(query_weight, "fsdp", 2)
    far_both, output_weight = tie(far_both, output_weight)
    far_output = flip(output_weight, "fsdp", 2)
    both_blocks = pair_up(both_shard, far_both)
    feed_pair = jnp.concatenate([gate_weight, up_weight], axis=1)

    hidden = hidden_in[0]
    cotangent = out_grad[0]
    places = positions[0]
    place_col = places[:, None]
    place_row = places[None, :]
    half = head_dim // 2
    freqs = rope_base ** (-(jnp.arange(half, dtype=f32) * 2.0) / head_dim)
    angles = places.astype(f32)[:, None] * freqs[None, :]
    cosine, sine = jnp.cos(angles), jnp.sin(angles)

    def facts(*starts):
        return jnp.stack([me, first_row, *starts]).astype(jnp.int32)

    info = facts()
    sem = pltpu.SemaphoreType.DMA
    token_flops = 2 * tokens * model

    normed, key_raw, kv, gains = call(
        kv_kernel,
        (info, hidden, cosine, sine, *both_blocks),
        [SMEM] + [VMEM] * 3 + [ANY] * 2,
        [
            ((tokens, model), bf16),
            ((tokens, head_dim), f32),
            ((tokens, 2 * head_dim), bf16),
            ((gain_pad, model), f32),
        ],
        [
            pltpu.VMEM((model, 2 * head_dim), bf16),
            pltpu.VMEM((4 * gain_pad, 2 * head_dim), bf16),
            sem((2, 4)),
        ],
        flops=token_flops * 2 * head_dim,
        name="key_value",
    )
    normed, far_query = tie(normed, far_query)

    ring = groups == 8
    if ring:
        side = ctx % 2
        stage = ctx // 2
        moved = [kv, send_on(kv, 2, groups)]
        others = [flip(kv, "ctx", 1)]
        moved[1], far_output, feed_pair = tie(moved[1], far_output, feed_pair)
        moved.append(send_on(moved[1], 2, groups))
        others.append(flip(moved[1], "ctx", 1))
    else:
        gathered = lax.all_gather(kv, "ctx", axis=0, tiled=True)
    query_blocks = pair_up(query_weight, far_query)
    query_raw, queries = call(
        query_kernel,
        (info, normed, gains, cosine, sine, *query_blocks),
        [SMEM] + [VMEM] * 4 + [ANY] * 2,
        [((tokens, wide), f32), ((tokens, wide), bf16)],
        [pltpu.VMEM((model, wide), bf16), sem((4,))],
        flops=token_flops * wide,
        name="query",
    )

    far_feed = flip(feed_pair, "fsdp", 2)
    if ring:
        queries, moved[2], others[1] = tie(queries, moved[2], others[1])
        moved.append(send_on(moved[2], 2, groups))
        others.append(flip(moved[2], "ctx", 1))

    state = ()
    chunk_flops = 4 * tokens * tokens * wide
    sources = []
    for number in range(groups // 2 if ring else 1):
        if ring:
            if number == 1:
                moved[3], total, far_output = tie(moved[3], state[1], far_output)
                state = (state[0], total)
                others.append(flip(moved[3], "ctx", 1))
                output_blocks = pair_up(output_weight, far_output)
            if number == 2:
                total, others[2] = tie(state[1], others[2])
                state = (state[0], total)
            if number == 3:
                far_feed, down_weight, total, output_blocks, others[3] = tie(
                    far_feed, down_weight, state[1], output_blocks, others[3]
                )
                state = (state[0], total)
                feed_blocks = pair_up(feed_pair, far_feed)
                far_down = flip(down_weight, "fsdp", 2)
            arrays = (moved[number], others[number])
            base = (stage - number) * 2
            starts = ((base + side) * tokens, (base + 1 - side) * tokens)
        else:
            arrays, starts = (gathered,), (jnp.int32(0),)
        sources.append((arrays, starts))
        first = number == 0
        count = len(arrays)

        def attend(*args, first=first, count=count):
            attend_kernel(first, count, *args)

        state = call(
            attend,
            (facts(*starts), queries, place_col, *arrays, *state),
            [SMEM] + [VMEM] * (2 + count + len(state)),
            [((tokens, wide), f32), ((tokens, heads * lanes), f32)],
            flops=chunk_flops * 2,
            limit=vmem_bytes if ring else 48 * 1024 * 1024,
            name="attend",
        )
    weighted, total = state
    if not ring:
        output_blocks = pair_up(output_weight, far_output)
        feed_blocks = pair_up(feed_pair, far_feed)
        far_down = flip(down_weight, "fsdp", 2)

    attended, mixed, projected, after, normed_feed, gate_value, up_value, activated = call(
        mix_kernel,
        (
            info, weighted, total, hidden, gains,
            *output_blocks, *feed_blocks,
        ),
        [SMEM] + [VMEM] * 4 + [ANY] * 4,
        [
            ((tokens, wide), f32),
            ((tokens, wide), bf16),
            ((tokens, model), f32),
            ((tokens, model), f32),
            ((tokens, model), bf16),
            ((tokens, feed), f32),
            ((tokens, feed), f32),
            ((tokens, feed), bf16),
        ],
        [
            pltpu.VMEM((wide, model), bf16),
            pltpu.VMEM((model, feed), bf16),
            pltpu.VMEM((model, feed), bf16),
            sem((3, 4)),
        ],
        flops=token_flops * (wide + 2 * feed),
        limit=large_bytes,
        name="mix",
    )
    far_down, mixed = tie(far_down, mixed)
    down_blocks = pair_up(down_weight, far_down)
    feed_rows = 2 * (feed // lanes) * rows + (model // lanes) * down_rows
    hidden_out, d_gate, d_up, grad_final, feed_keep, feed_send = call(
        feed_kernel,
        (
            info, activated, gate_value, up_value, normed_feed, after, cotangent, gains,
            *down_blocks,
        ),
        [SMEM] + [VMEM] * 7 + [ANY] * 2,
        [
            ((tokens, model), bf16),
            ((tokens, feed), bf16),
            ((tokens, feed), bf16),
            ((1, model), f32),
            ((2, feed_rows, lanes), bf16),
            ((2, feed_rows, lanes), bf16),
        ],
        [
            pltpu.VMEM((feed, model), bf16),
            pltpu.VMEM((tokens, model), bf16),
            pltpu.VMEM((model, tokens), bf16),
            sem((4,)),
        ],
        flops=token_flops * 5 * feed,
        limit=large_bytes,
        name="feed",
    )
    feed_near = flip(feed_send, "fsdp", 1)

    d_after, d_projected, d_mixed, table, grad_feed_gain, grad_mix_gain = call(
        feed_back_kernel,
        (
            info, d_gate, d_up, after, projected, attended, total, cotangent, gains,
            *feed_blocks, *output_blocks,
        ),
        [SMEM] + [VMEM] * 8 + [ANY] * 4,
        [
            ((tokens, model), f32),
            ((tokens, model), bf16),
            ((tokens, wide), bf16),
            ((2 * heads, tokens), f32),
            ((1, model), f32),
            ((1, model), f32),
        ],
        [
            pltpu.VMEM((model, feed), bf16),
            pltpu.VMEM((model, feed), bf16),
            pltpu.VMEM((wide, model), bf16),
            pltpu.VMEM((tokens, model), f32),
            sem((3, 4)),
        ],
        flops=token_flops * (2 * feed + wide),
        limit=large_bytes,
        name="feed_back",
    )

    feed_near, d_mixed = tie(feed_near, d_mixed)
    gate_rows = (feed // lanes) * rows
    half_rows = feed_rows // 2
    feed_sum = add_low(feed_keep[1], feed_near[1])
    d_mixed, feed_sum = tie(d_mixed, feed_sum)
    feed_far = flip(feed_sum, "fsdp", 2)
    bits = ctx_bits()
    steps = len(bits)
    turned = [bits[1], bits[0], *bits[2:]]

    query_grads = ()
    arrived = []
    waiting = None
    last = len(sources) - 1
    for number, (arrays, starts) in enumerate(reversed(sources)):
        first = number == 0
        count = len(arrays)

        def attend_back(*args, first=first, count=count):
            attend_back_kernel(first, count, *args)

        results = call(
            attend_back,
            (facts(*starts), queries, d_mixed, table, place_row, *arrays, *query_grads),
            [SMEM] + [VMEM] * (4 + count + len(query_grads)),
            [((tokens, wide), f32)] + [(a.shape, bf16) for a in arrays],
            [pltpu.VMEM((tokens, head_dim), f32), pltpu.VMEM((tokens, head_dim), f32)],
            flops=chunk_flops * 5,
            limit=vmem_bytes if ring else 48 * 1024 * 1024,
            name="attend_back",
        )
        query_grads = results[:1]
        if not ring:
            arrived.append(
                lax.psum_scatter(results[1], "ctx", scatter_dimension=0, tiled=True)
            )
            continue
        shift = last - number
        own, other = results[1:]
        if waiting is not None:
            crossed, held, *arrived = tie(waiting[1], query_grads[0], *arrived)
            query_grads = (held,)
            arrived = [send_back(add_low(waiting[0], crossed, *arrived), 2, groups)]
        waiting = (own, flip(other, "ctx", 1))
    if ring:
        arrived += list(waiting)

    query_rows = (wide // lanes) * rows
    output_rows = (model // lanes) * mixed_rows
    both_rows = (2 * head_dim // lanes) * rows + lanes
    pack_rows = query_rows + output_rows + both_rows
    d_normed_query, grad_query_gain, query_keep, query_send = call(
        query_back_kernel,
        (
            info, query_grads[0], query_raw, cosine, sine, gains, normed, mixed, d_projected,
            *query_blocks,
        ),
        [SMEM] + [VMEM] * 8 + [ANY] * 2,
        [
            ((tokens, model), f32),
            ((1, head_dim), f32),
            ((2, query_rows + output_rows, lanes), bf16),
            ((2, query_rows + output_rows, lanes), bf16),
        ],
        [
            pltpu.VMEM((model, wide), bf16),
            pltpu.VMEM((tokens, wide), bf16),
            pltpu.VMEM((model, tokens), bf16),
            sem((4,)),
        ],
        flops=token_flops * 3 * wide,
        name="query_back",
    )
    arrived_count = len(arrived)

    def key_back(*args):
        key_back_kernel(arrived_count, *args)

    grad_input, pack_keep, pack_send = call(
        key_back,
        (
            info, cosine, sine, gains, key_raw, normed, hidden, d_after,
            d_normed_query, grad_mix_gain, grad_feed_gain, grad_final, grad_query_gain,
            query_keep, query_send, *both_blocks, *arrived,
        ),
        [SMEM] + [VMEM] * 14 + [ANY] * 2 + [VMEM] * arrived_count,
        [
            ((tokens, model), f32),
            ((2, pack_rows, lanes), bf16),
            ((2, pack_rows, lanes), bf16),
        ],
        [
            pltpu.VMEM((model, 2 * head_dim), bf16),
            pltpu.VMEM((tokens, 2 * head_dim), bf16),
            pltpu.VMEM((model, tokens), bf16),
            pltpu.VMEM((gain_pad, model), f32),
            sem((4,)),
        ],
        flops=token_flops * 4 * head_dim,
        name="key_back",
    )
    pack_send, feed_far = tie(pack_send, feed_far)
    pack_near = flip(pack_send, "fsdp", 1)

    left = add_low(feed_keep[0, :half_rows], feed_near[0, :half_rows], feed_far[:half_rows])
    right = add_low(feed_keep[0, half_rows:], feed_near[0, half_rows:], feed_far[half_rows:])
    left, right, pack_near = tie(left, right, pack_near)
    pack = None
    for number in range(2 * steps + 2):
        if number < steps:
            left = scatter_step(left, bits[number])
            right = scatter_step(right, turned[number])
        elif number < 2 * steps:
            left = gather_step(left, bits[2 * steps - 1 - number])
            right = gather_step(right, turned[2 * steps - 1 - number])
        if number == 0:
            pack_far = flip(add_low(pack_keep[1], pack_near[1]), "fsdp", 2)
            left, right = tie(left, right)
        elif number == 1:
            left, right, pack_far = tie(left, right, pack_far)
            pack = add_low(pack_keep[0], pack_near[0], pack_far)
        else:
            now = number - 2
            if now < steps:
                pack = scatter_step(pack, bits[now])
            else:
                pack = gather_step(pack, bits[2 * steps - 1 - now])
            left, right, pack = tie(left, right, pack)

    def unpack(packs, shapes):
        def kernel(*args):
            unpack_kernel(shapes, len(packs), *args)

        specs = [VMEM] * len(packs)
        return call(kernel, packs, specs, [(s, f32) for s in shapes], name="unpack")

    grad_gate, grad_up, grad_down = unpack(
        (left, right), [gate_weight.shape, up_weight.shape, down_weight.shape]
    )
    grad_query, grad_output, grad_key, grad_value, wide_gains, head_gains = unpack(
        (pack,),
        [
            query_weight.shape,
            output_weight.shape,
            key_weight.shape,
            value_weight.shape,
            (gain_pad, 2 * lanes),
            (gain_pad, lanes),
        ],
    )
    gain_shards = [wide_gains[i, :rows] for i in range(4)]
    gain_shards += [head_gains[i, : query_gain.shape[0]] for i in (4, 5)]
    return (
        hidden_out[None],
        grad_input[None],
        grad_query,
        grad_key,
        grad_value,
        grad_output,
        grad_gate,
        grad_up,
        grad_down,
        *gain_shards,
    )


def solution(mesh):
    token = P("fsdp", "ctx", None)
    weight = P("fsdp", None)
    gain = P("fsdp")
    return jax.shard_map(
        on_device,
        mesh=mesh,
        in_specs=(token, P("fsdp", "ctx")) + (weight,) * 7 + (gain,) * 6 + (token,),
        out_specs=(token, token) + (weight,) * 7 + (gain,) * 6,
        check_vma=False,
    )
```

```python
import jax
import jax.numpy as jnp
from jax import lax
from jax.experimental import pallas as pl
from jax.experimental.pallas import tpu as pltpu
from jax.sharding import PartitionSpec as P

eps = 1e-06
rope_base = 1000000.0
lanes = 128
order = (0, 2, 1, 3)
vmem_bytes = 8 * 1024 * 1024
large_bytes = 12 * 1024 * 1024
gain_pad = 16
f32 = jnp.float32
bf16 = jnp.bfloat16

ANY = pl.BlockSpec(memory_space=pl.ANY)
SMEM = pl.BlockSpec(memory_space=pltpu.SMEM)
VMEM = pl.BlockSpec(memory_space=pltpu.VMEM)


def tie(*values):
    return lax.optimization_barrier(values)


def call(kernel, inputs, specs, outs, scratch=(), flops=0, limit=vmem_bytes, name=None):
    return pl.pallas_call(
        kernel,
        out_shape=tuple(jax.ShapeDtypeStruct(s, d) for s, d in outs),
        in_specs=list(specs),
        out_specs=tuple(VMEM for _ in outs),
        scratch_shapes=list(scratch),
        compiler_params=pltpu.CompilerParams(vmem_limit_bytes=limit),
        cost_estimate=pl.CostEstimate(flops=1, bytes_accessed=1, transcendentals=0),
        name=name,
    )(*inputs)


def nn(left, right):
    return lax.dot_general(left, right, (((1,), (0,)), ((), ())), preferred_element_type=f32)


def nt(left, right):
    return lax.dot_general(left, right, (((1,), (1,)), ((), ())), preferred_element_type=f32)


def tn(left, right):
    return lax.dot_general(left, right, (((0,), (0,)), ((), ())), preferred_element_type=f32)


def unit(value):
    inverse = lax.rsqrt(jnp.mean(value * value, axis=-1, keepdims=True) + eps)
    return value * inverse, inverse


def unit_back(hat, inverse, grad_hat):
    return inverse * (grad_hat - hat * jnp.mean(grad_hat * hat, axis=-1, keepdims=True))


def spin(value, cosine, sine):
    half = value.shape[-1] // 2
    first, second = value[:, :half], value[:, half:]
    return jnp.concatenate(
        [first * cosine - second * sine, second * cosine + first * sine], axis=-1
    )


def place(index, pairs, full, sems, columns=None):
    rows = full.shape[0] // 4
    pitch = pairs[0].shape[0] // 2
    copies = []
    for step in range(4):
        begin = pl.multiple_of((index ^ step) * rows, 16)
        source = pairs[step % 2].at[pl.ds((step // 2) * pitch, rows)]
        if columns is not None:
            source = source.at[:, pl.ds(columns, full.shape[1])]
        copy = pltpu.make_async_copy(source, full.at[pl.ds(begin, rows)], sems.at[step])
        copy.start()
        copies.append(copy)
    return copies


def finish(copies):
    for copy in copies:
        copy.wait()


def kv_kernel(
    info, hidden, cosine, sine,
    b0, b1,
    normed_out, key_raw_out, kv_out, gains_out,
    both_full, gain_parts, sems,
):
    index = info[0]
    copies = place(index, (b0, b1), both_full, sems.at[0])
    model = hidden.shape[1]
    rows = model // 4
    width = key_raw_out.shape[1]
    piece = width // 4
    gain_copies = []
    for step in range(4):
        begin = pl.multiple_of((index ^ step) * gain_pad, gain_pad)
        source = (b0, b1)[step % 2].at[pl.ds((step // 2) * (rows + gain_pad) + rows, gain_pad)]
        copy = pltpu.make_async_copy(
            source, gain_parts.at[pl.ds(begin, gain_pad)], sems.at[1, step]
        )
        copy.start()
        gain_copies.append(copy)
    hat, _ = unit(hidden[...].astype(f32))
    finish(gain_copies)
    span = 2 * lanes
    line = lax.broadcasted_iota(jnp.int32, (span, model), 0)
    column = lax.broadcasted_iota(jnp.int32, (span, model), 1)
    wide_gain = jnp.zeros((gain_pad, model), f32)
    head_gain = jnp.zeros((gain_pad, model), f32)
    for owner in range(4):
        values = gain_parts[owner * gain_pad : (owner + 1) * gain_pad, :span]
        spots = (column == line + owner * rows) & (line < rows)
        wide_gain += nn(values, spots.astype(f32).astype(bf16))
        spots = (column == line + owner * piece) & (line < piece)
        head_gain += nn(values, spots.astype(f32).astype(bf16))
    which = lax.broadcasted_iota(jnp.int32, (gain_pad, model), 0)
    gains = jnp.where(which < 4, wide_gain, head_gain)
    gains_out[...] = gains
    normed = (hat * (1.0 + gains[0:1, :])).astype(bf16)
    normed_out[...] = normed
    finish(copies)
    raw = nn(normed, both_full[:, :width])
    key_raw_out[...] = raw
    hat, _ = unit(raw)
    scale = 1.0 + gains[5:6, :width]
    kv_out[:, :width] = spin(hat * scale, cosine[...], sine[...]).astype(bf16)
    kv_out[:, width:] = nn(normed, both_full[:, width:]).astype(bf16)


def query_kernel(
    info, normed, gains, cosine, sine, q0, q1,
    raw_out, query_out, query_full, sems,
):
    finish(place(info[0], (q0, q1), query_full, sems))
    head_dim = 2 * cosine.shape[1]
    for start in range(0, query_full.shape[1], head_dim):
        part = slice(start, start + head_dim)
        raw = nn(normed[...], query_full[:, part])
        raw_out[:, part] = raw
        hat, _ = unit(raw)
        turned = spin(hat * (1.0 + gains[4:5, :head_dim]), cosine[...], sine[...])
        query_out[:, part] = (turned * head_dim ** (-0.5)).astype(bf16)


def attend_kernel(first, count, info, queries, places, *refs):
    chunks = refs[:count]
    refs = refs[count:]
    if not first:
        weighted_in, total_in = refs[:2]
        refs = refs[2:]
    weighted, total = refs
    tokens = queries.shape[0]
    head_dim = chunks[0].shape[1] // 2
    heads = queries.shape[1] // head_dim
    if first:
        weighted[...] = jnp.zeros_like(weighted)
        total[...] = jnp.zeros_like(total)
    else:
        weighted[...] = weighted_in[...]
        total[...] = total_in[...]
    first_row = info[1]
    for number, chunk in enumerate(chunks):
        base = info[2 + number]

        @pl.loop(0, chunk.shape[0] // tokens)
        def _(step):
            start = base + step * tokens

            @pl.when((start >= 0) & (start <= first_row))
            def _():
                local = pl.ds(pl.multiple_of(step * tokens, tokens), tokens)
                row = first_row + lax.broadcasted_iota(jnp.int32, (tokens, tokens), 0)
                col = start + lax.broadcasted_iota(jnp.int32, (tokens, tokens), 1)
                allowed = (col <= row) & (col >= row - places[...])
                keys = chunk[local, :head_dim]
                values = chunk[local, head_dim:]
                for head in range(heads):
                    part = slice(head * head_dim, (head + 1) * head_dim)
                    scores = nt(queries[:, part], keys)
                    expo = jnp.where(allowed, jnp.exp(scores), 0.0)
                    spot = slice(head * lanes, (head + 1) * lanes)
                    total[:, spot] += jnp.sum(expo, axis=1, keepdims=True)
                    weighted[:, part] += nn(expo.astype(bf16), values)


def mix_kernel(
    info, weighted, total, hidden, gains,
    o0, o1, g0, g1,
    attended_out, mixed_out, projected_out, after_out, normed_out, gate_out, up_out, act_out,
    output_full, gate_full, up_full, sems,
):
    index = info[0]
    feed = gate_full.shape[1]
    output_copies = place(index, (o0, o1), output_full, sems.at[0])
    gate_copies = place(index, (g0, g1), gate_full, sems.at[1], 0)
    up_copies = place(index, (g0, g1), up_full, sems.at[2], feed)
    heads = total.shape[1] // lanes
    head_dim = weighted.shape[1] // heads
    for head in range(heads):
        part = slice(head * head_dim, (head + 1) * head_dim)
        ratio = weighted[:, part] / total[:, head * lanes : head * lanes + 1]
        attended_out[:, part] = ratio
        mixed_out[:, part] = ratio.astype(bf16)
    finish(output_copies)
    projected = nn(mixed_out[...], output_full[...])
    projected_out[...] = projected
    hat, _ = unit(projected)
    after = hidden[...].astype(f32) + hat * (1.0 + gains[1:2, :])
    after_out[...] = after
    hat, _ = unit(after)
    normed_out[...] = (hat * (1.0 + gains[2:3, :])).astype(bf16)
    finish(gate_copies)
    finish(up_copies)
    step_width = 512

    @pl.loop(0, gate_full.shape[1] // step_width)
    def _(step):
        part = pl.ds(pl.multiple_of(step * step_width, step_width), step_width)
        gate = nn(normed_out[...], gate_full[:, part])
        up = nn(normed_out[...], up_full[:, part])
        gate_out[:, part] = gate
        up_out[:, part] = up
        inner = 0.7978845608028654 * (gate + 0.044715 * gate * gate * gate)
        act_out[:, part] = (0.5 * gate * (1.0 + jnp.tanh(inner)) * up).astype(bf16)


def store_columns(keep, send, slot, base, rows, block):
    target = keep if slot < 2 else send
    for number in range(block.shape[1] // lanes):
        target[slot % 2, base + number * rows : base + (number + 1) * rows, :] = block[
            :, number * lanes : (number + 1) * lanes
        ].astype(bf16)


def feed_kernel(
    info, act, gate, up, normed, after, cotangent, gains,
    d0, d1,
    hidden_out, d_gate, d_up, gain_grad, keep, send,
    down_full, d_down, turned, sems,
):
    index = info[0]
    finish(place(index, (d0, d1), down_full, sems))
    down = nn(act[...], down_full[...])
    hat, inverse = unit(down)
    scale = 1.0 + gains[3:4, :]
    hidden_out[...] = (after[...] + hat * scale).astype(bf16)
    grad = cotangent[...].astype(f32)
    gain_grad[...] = jnp.sum(grad * hat, axis=0, keepdims=True)
    d_down[...] = unit_back(hat, inverse, grad * scale).astype(bf16)
    turned[...] = normed[...].astype(f32).T.astype(bf16)
    step_width = 512

    @pl.loop(0, down_full.shape[0] // step_width)
    def _(step):
        part = pl.ds(pl.multiple_of(step * step_width, step_width), step_width)
        d_act = nt(d_down[...], down_full[part, :])
        x = gate[:, part]
        curve = jnp.tanh(0.7978845608028654 * (x + 0.044715 * x * x * x))
        slope = 0.5 * (1.0 + curve) + 0.5 * x * (1.0 - curve * curve) * (
            0.7978845608028654 * (1.0 + 3.0 * 0.044715 * x * x)
        )
        d_gate[:, part] = (d_act * up[:, part] * slope).astype(bf16)
        d_up[:, part] = (d_act * (0.5 * x * (1.0 + curve))).astype(bf16)

    model = normed.shape[1]
    rows = model // 4
    wide = gate.shape[1]
    down_rows = wide // 4
    part_rows = (wide // lanes) * rows
    for slot, step in enumerate(order):
        target = keep if slot < 2 else send
        owner = index ^ step
        lhs = turned[pl.ds(pl.multiple_of(owner * rows, 16), rows), :]
        for base, source in ((0, d_gate), (part_rows, d_up)):

            @pl.loop(0, wide // step_width)
            def _(move):
                part = pl.ds(pl.multiple_of(move * step_width, step_width), step_width)
                block = nn(lhs, source[:, part]).astype(bf16)
                for number in range(step_width // lanes):
                    begin = base + (move * (step_width // lanes) + number) * rows
                    target[slot % 2, pl.ds(pl.multiple_of(begin, 16), rows), :] = block[
                        :, number * lanes : (number + 1) * lanes
                    ]

        left = act[:, pl.ds(pl.multiple_of(owner * down_rows, lanes), down_rows)]
        store_columns(keep, send, slot, 2 * part_rows, down_rows, tn(left, d_down[...]))


def feed_back_kernel(
    info, d_gate, d_up, after, projected, attended, total, cotangent, gains,
    g0, g1, o0, o1,
    d_after_out, d_projected_out, d_mixed_out, rows_out, feed_grad, mix_grad,
    gate_full, up_full, output_full, total_grad, sems,
):
    index = info[0]
    gate_copies = place(index, (g0, g1), gate_full, sems.at[0], 0)
    up_copies = place(index, (g0, g1), up_full, sems.at[1], gate_full.shape[1])
    output_copies = place(index, (o0, o1), output_full, sems.at[2])
    finish(gate_copies)
    total_grad[...] = nt(d_gate[...], gate_full[...])
    finish(up_copies)
    grad = total_grad[...] + nt(d_up[...], up_full[...])
    hat, inverse = unit(after[...])
    feed_grad[...] = jnp.sum(grad * hat, axis=0, keepdims=True)
    d_after = cotangent[...].astype(f32) + unit_back(hat, inverse, grad * (1.0 + gains[2:3, :]))
    d_after_out[...] = d_after
    hat, inverse = unit(projected[...])
    mix_grad[...] = jnp.sum(d_after * hat, axis=0, keepdims=True)
    d_projected = unit_back(hat, inverse, d_after * (1.0 + gains[1:2, :])).astype(bf16)
    d_projected_out[...] = d_projected
    finish(output_copies)
    d_mixed = nt(d_projected, output_full[...]).astype(bf16)
    d_mixed_out[...] = d_mixed
    heads = total.shape[1] // lanes
    head_dim = attended.shape[1] // heads
    tokens = attended.shape[0]
    lane = lax.broadcasted_iota(jnp.int32, (tokens, lanes), 1)
    table = jnp.zeros((tokens, lanes), f32)
    for head in range(heads):
        part = slice(head * head_dim, (head + 1) * head_dim)
        delta = jnp.sum(d_mixed[:, part].astype(f32) * attended[:, part], axis=1, keepdims=True)
        table = jnp.where(lane == head, delta, table)
        share = 1.0 / total[:, head * lanes : (head + 1) * lanes]
        table = jnp.where(lane == heads + head, share, table)
    rows_out[...] = table.T[: rows_out.shape[0], :]


def attend_back_kernel(first, count, info, queries, d_mixed, table, places, *refs):
    chunks = refs[:count]
    refs = refs[count:]
    if not first:
        query_in = refs[0]
        refs = refs[1:]
    query_grads = refs[0]
    chunk_grads = refs[1 : 1 + count]
    key_sum, value_sum = refs[1 + count :]
    tokens = queries.shape[0]
    head_dim = chunks[0].shape[1] // 2
    heads = queries.shape[1] // head_dim
    if first:
        query_grads[...] = jnp.zeros_like(query_grads)
    else:
        query_grads[...] = query_in[...]
    first_row = info[1]
    for number, (chunk, chunk_grad) in enumerate(zip(chunks, chunk_grads)):
        base = info[2 + number]
        chunk_grad[...] = jnp.zeros_like(chunk_grad)

        @pl.loop(0, chunk.shape[0] // tokens)
        def _(step):
            start = base + step * tokens

            @pl.when((start >= 0) & (start <= first_row))
            def _():
                local = pl.ds(pl.multiple_of(step * tokens, tokens), tokens)
                row = first_row + lax.broadcasted_iota(jnp.int32, (tokens, tokens), 1)
                col = start + lax.broadcasted_iota(jnp.int32, (tokens, tokens), 0)
                allowed = (col <= row) & (col >= row - places[...])
                keys = chunk[local, :head_dim]
                values = chunk[local, head_dim:]
                for head in range(heads):
                    part = slice(head * head_dim, (head + 1) * head_dim)
                    query = queries[:, part]
                    grad = d_mixed[:, part]
                    expo = jnp.where(allowed, jnp.exp(nt(keys, query)), 0.0)
                    probs = expo * table[heads + head : heads + head + 1, :]
                    back = nt(values, grad) - table[head : head + 1, :]
                    d_scores = (probs * back).astype(bf16)
                    d_value = nn(probs.astype(bf16), grad)
                    d_key = nn(d_scores, query)
                    if head == 0:
                        key_sum[...] = d_key
                        value_sum[...] = d_value
                    else:
                        key_sum[...] += d_key
                        value_sum[...] += d_value
                    query_grads[:, part] += tn(d_scores, keys)
                chunk_grad[local, :head_dim] = key_sum[...].astype(bf16)
                chunk_grad[local, head_dim:] = value_sum[...].astype(bf16)


def unspin(value, cosine, sine):
    half = value.shape[-1] // 2
    first, second = value[:, :half], value[:, half:]
    return jnp.concatenate(
        [first * cosine + second * sine, second * cosine - first * sine], axis=-1
    )


def query_back_kernel(
    info, query_grads, raw, cosine, sine, gains, normed, mixed, d_projected,
    q0, q1,
    d_normed_out, gain_grad, keep, send,
    query_full, d_raw, turned, sems,
):
    index = info[0]
    copies = place(index, (q0, q1), query_full, sems)
    head_dim = 2 * cosine.shape[1]
    wide = raw.shape[1]
    scale = 1.0 + gains[4:5, :head_dim]
    gain_sum = jnp.zeros((1, head_dim), f32)
    for start in range(0, wide, head_dim):
        part = slice(start, start + head_dim)
        hat, inverse = unit(raw[:, part])
        grad = unspin(query_grads[:, part] * head_dim ** (-0.5), cosine[...], sine[...])
        gain_sum += jnp.sum(grad * hat, axis=0, keepdims=True)
        d_raw[:, part] = unit_back(hat, inverse, grad * scale).astype(bf16)
    gain_grad[...] = gain_sum
    turned[...] = normed[...].astype(f32).T.astype(bf16)
    rows = normed.shape[1] // 4
    mixed_rows = mixed.shape[1] // 4
    for slot, step in enumerate(order):
        owner = index ^ step
        lhs = turned[pl.ds(pl.multiple_of(owner * rows, 16), rows), :]
        store_columns(keep, send, slot, 0, rows, nn(lhs, d_raw[...]))
        left = mixed[:, pl.ds(pl.multiple_of(owner * mixed_rows, lanes), mixed_rows)]
        store_columns(
            keep, send, slot, (wide // lanes) * rows, mixed_rows, tn(left, d_projected[...])
        )
    finish(copies)
    d_normed_out[...] = nt(d_raw[...], query_full[...])


def key_back_kernel(
    count, info, cosine, sine, gains, raw, normed, hidden, d_after, d_normed_query,
    mix_grad, feed_grad, final_grad, query_grad, keep_in, send_in, b0, b1, *refs,
):
    parts = refs[:count]
    (
        input_grad, keep, send,
        both_full, d_both, turned, gain_grads, sems,
    ) = refs[count:]
    index = info[0]
    copies = place(index, (b0, b1), both_full, sems)
    width = raw.shape[1]
    both = parts[0][...].astype(f32)
    for piece in parts[1:]:
        both = both + piece[...].astype(f32)
    hat, inverse = unit(raw[...])
    grad = unspin(both[:, :width], cosine[...], sine[...])
    gain_grads[...] = jnp.zeros_like(gain_grads)
    gain_grads[5:6, :width] = jnp.sum(grad * hat, axis=0, keepdims=True)
    d_both[:, :width] = unit_back(hat, inverse, grad * (1.0 + gains[5:6, :width])).astype(bf16)
    d_both[:, width:] = both[:, width:].astype(bf16)
    turned[...] = normed[...].astype(f32).T.astype(bf16)
    rows = normed.shape[1] // 4
    base = keep_in.shape[1]
    keep[:, :base, :] = keep_in[...]
    send[:, :base, :] = send_in[...]
    for slot, step in enumerate(order):
        owner = index ^ step
        lhs = turned[pl.ds(pl.multiple_of(owner * rows, 16), rows), :]
        store_columns(keep, send, slot, base, rows, nn(lhs, d_both[...]))
    finish(copies)
    d_normed = d_normed_query[...] + nt(d_both[...], both_full[...])
    hat, inverse = unit(hidden[...].astype(f32))
    gain_grads[0:1, :] = jnp.sum(d_normed * hat, axis=0, keepdims=True)
    gain_grads[1:2, :] = mix_grad[...]
    gain_grads[2:3, :] = feed_grad[...]
    gain_grads[3:4, :] = final_grad[...]
    gain_grads[4:5, :width] = query_grad[...]
    input_grad[...] = d_after[...] + unit_back(hat, inverse, d_normed * (1.0 + gains[0:1, :]))
    model = normed.shape[1]
    piece = width // 4
    span = 2 * lanes
    line = lax.broadcasted_iota(jnp.int32, (model, span), 0)
    column = lax.broadcasted_iota(jnp.int32, (model, span), 1)
    values = gain_grads[...].astype(bf16)
    base += (2 * width // lanes) * rows
    for slot, step in enumerate(order):
        target = keep if slot < 2 else send
        owner = index ^ step
        spots = (line == column + owner * rows) & (column < rows)
        wide_part = nn(values, spots.astype(f32).astype(bf16)).astype(bf16)
        spots = (line == column + owner * piece) & (column < piece)
        head_part = nn(values, spots.astype(f32).astype(bf16)).astype(bf16)
        begin = base
        for part in (wide_part[:, :lanes], wide_part[:, lanes:], head_part[:, :lanes]):
            target[slot % 2, begin : begin + gain_pad, :] = part
            begin += gain_pad
        target[slot % 2, begin:, :] = jnp.zeros((target.shape[1] - begin, lanes), bf16)


def unpack_kernel(shapes, count, *refs):
    packs, outs = refs[:count], refs[count:]
    number, base = 0, 0
    for out, (rows, width) in zip(outs, shapes):
        for start in range(0, width, lanes):
            if base == packs[number].shape[0]:
                number, base = number + 1, 0
            out[:, start : start + lanes] = packs[number][base : base + rows, :].astype(f32)
            base += rows


def flip(value, axis, bit):
    size = lax.axis_size(axis)
    return lax.ppermute(value, axis, [(i, i ^ bit) for i in range(size)])


def pair_up(shard, far):
    both = jnp.concatenate([shard, far], axis=0)
    return both, flip(both, "fsdp", 1)


def add_low(*values):
    total = values[0].astype(f32)
    for value in values[1:]:
        total = total + value.astype(f32)
    return total.astype(bf16)


def take_half(value, which):
    axis = value.ndim - 2
    half = value.shape[axis] // 2
    return lax.dynamic_slice_in_dim(value, which * half, half, axis)


def ctx_bits():
    return [1 << i for i in range(lax.axis_size("ctx").bit_length() - 1)]


def scatter_step(value, bit):
    mine = (lax.axis_index("ctx") // bit) % 2
    sent = flip(take_half(value, 1 - mine), "ctx", bit)
    return add_low(take_half(value, mine), sent)


def gather_step(value, bit):
    mine = (lax.axis_index("ctx") // bit) % 2
    other = flip(value, "ctx", bit)
    low = jnp.where(mine == 0, value, other)
    high = jnp.where(mine == 0, other, value)
    return jnp.concatenate([low, high], axis=0)


def send_on(value, shift, groups):
    return lax.ppermute(value, "ctx", [(i, i + shift) for i in range(groups - shift)])


def send_back(value, shift, groups):
    return lax.ppermute(value, "ctx", [(i + shift, i) for i in range(groups - shift)])


def on_device(
    hidden_in, positions, query_weight, key_weight, value_weight, output_weight, gate_weight,
    up_weight, down_weight, input_gain, mixer_gain, feed_gain, final_gain, query_gain, key_gain,
    out_grad,
):
    tokens = hidden_in.shape[1]
    model = hidden_in.shape[2]
    rows = key_weight.shape[0]
    head_dim = key_weight.shape[1]
    wide = query_weight.shape[1]
    heads = wide // head_dim
    feed = gate_weight.shape[1]
    mixed_rows = output_weight.shape[0]
    down_rows = down_weight.shape[0]
    me = lax.axis_index("fsdp")
    ctx = lax.axis_index("ctx")
    groups = lax.axis_size("ctx")
    first_row = ctx * tokens

    gains = jnp.zeros((gain_pad, 2 * head_dim), bf16)
    shards = (input_gain, mixer_gain, feed_gain, final_gain, query_gain, key_gain)
    for number, gain in enumerate(shards):
        gains = gains + jnp.pad(
            gain[None], ((number, gain_pad - 1 - number), (0, 2 * head_dim - gain.shape[0]))
        )
    both_shard = jnp.concatenate(
        [jnp.concatenate([key_weight, value_weight], axis=1), gains], axis=0
    )
    far_both = flip(both_shard, "fsdp", 2)
    far_query = flip(query_weight, "fsdp", 2)
    far_both, output_weight = tie(far_both, output_weight)
    far_output = flip(output_weight, "fsdp", 2)
    both_blocks = pair_up(both_shard, far_both)
    feed_pair = jnp.concatenate([gate_weight, up_weight], axis=1)

    hidden = hidden_in[0]
    cotangent = out_grad[0]
    places = positions[0]
    place_col = places[:, None]
    place_row = places[None, :]
    half = head_dim // 2
    freqs = rope_base ** (-(jnp.arange(half, dtype=f32) * 2.0) / head_dim)
    angles = places.astype(f32)[:, None] * freqs[None, :]
    cosine, sine = jnp.cos(angles), jnp.sin(angles)

    def facts(*starts):
        return jnp.stack([me, first_row, *starts]).astype(jnp.int32)

    info = facts()
    sem = pltpu.SemaphoreType.DMA
    token_flops = 2 * tokens * model

    normed, key_raw, kv, gains = call(
        kv_kernel,
        (info, hidden, cosine, sine, *both_blocks),
        [SMEM] + [VMEM] * 3 + [ANY] * 2,
        [
            ((tokens, model), bf16),
            ((tokens, head_dim), f32),
            ((tokens, 2 * head_dim), bf16),
            ((gain_pad, model), f32),
        ],
        [
            pltpu.VMEM((model, 2 * head_dim), bf16),
            pltpu.VMEM((4 * gain_pad, 2 * head_dim), bf16),
            sem((2, 4)),
        ],
        flops=token_flops * 2 * head_dim,
        name="key_value",
    )
    normed, far_query = tie(normed, far_query)

    ring = groups == 8
    if ring:
        side = ctx % 2
        stage = ctx // 2
        moved = [kv, send_on(kv, 2, groups)]
        others = [flip(kv, "ctx", 1)]
        moved[1], far_output, feed_pair = tie(moved[1], far_output, feed_pair)
        moved.append(send_on(moved[1], 2, groups))
        others.append(flip(moved[1], "ctx", 1))
    else:
        gathered = lax.all_gather(kv, "ctx", axis=0, tiled=True)
    query_blocks = pair_up(query_weight, far_query)
    query_raw, queries = call(
        query_kernel,
        (info, normed, gains, cosine, sine, *query_blocks),
        [SMEM] + [VMEM] * 4 + [ANY] * 2,
        [((tokens, wide), f32), ((tokens, wide), bf16)],
        [pltpu.VMEM((model, wide), bf16), sem((4,))],
        flops=token_flops * wide,
        name="query",
    )

    far_feed = flip(feed_pair, "fsdp", 2)
    if ring:
        queries, moved[2], others[1] = tie(queries, moved[2], others[1])
        moved.append(send_on(moved[2], 2, groups))
        others.append(flip(moved[2], "ctx", 1))

    state = ()
    chunk_flops = 4 * tokens * tokens * wide
    sources = []
    for number in range(groups // 2 if ring else 1):
        if ring:
            if number == 1:
                moved[3], total, far_output = tie(moved[3], state[1], far_output)
                state = (state[0], total)
                others.append(flip(moved[3], "ctx", 1))
                output_blocks = pair_up(output_weight, far_output)
            if number == 2:
                total, others[2] = tie(state[1], others[2])
                state = (state[0], total)
            if number == 3:
                far_feed, down_weight, total, output_blocks, others[3] = tie(
                    far_feed, down_weight, state[1], output_blocks, others[3]
                )
                state = (state[0], total)
                feed_blocks = pair_up(feed_pair, far_feed)
                far_down = flip(down_weight, "fsdp", 2)
            arrays = (moved[number], others[number])
            base = (stage - number) * 2
            starts = ((base + side) * tokens, (base + 1 - side) * tokens)
        else:
            arrays, starts = (gathered,), (jnp.int32(0),)
        sources.append((arrays, starts))
        first = number == 0
        count = len(arrays)

        def attend(*args, first=first, count=count):
            attend_kernel(first, count, *args)

        state = call(
            attend,
            (facts(*starts), queries, place_col, *arrays, *state),
            [SMEM] + [VMEM] * (2 + count + len(state)),
            [((tokens, wide), f32), ((tokens, heads * lanes), f32)],
            flops=chunk_flops * 2,
            limit=vmem_bytes if ring else 48 * 1024 * 1024,
            name="attend",
        )
    weighted, total = state
    if not ring:
        output_blocks = pair_up(output_weight, far_output)
        feed_blocks = pair_up(feed_pair, far_feed)
        far_down = flip(down_weight, "fsdp", 2)

    attended, mixed, projected, after, normed_feed, gate_value, up_value, activated = call(
        mix_kernel,
        (
            info, weighted, total, hidden, gains,
            *output_blocks, *feed_blocks,
        ),
        [SMEM] + [VMEM] * 4 + [ANY] * 4,
        [
            ((tokens, wide), f32),
            ((tokens, wide), bf16),
            ((tokens, model), f32),
            ((tokens, model), f32),
            ((tokens, model), bf16),
            ((tokens, feed), f32),
            ((tokens, feed), f32),
            ((tokens, feed), bf16),
        ],
        [
            pltpu.VMEM((wide, model), bf16),
            pltpu.VMEM((model, feed), bf16),
            pltpu.VMEM((model, feed), bf16),
            sem((3, 4)),
        ],
        flops=token_flops * (wide + 2 * feed),
        limit=large_bytes,
        name="mix",
    )
    far_down, mixed = tie(far_down, mixed)
    down_blocks = pair_up(down_weight, far_down)
    feed_rows = 2 * (feed // lanes) * rows + (model // lanes) * down_rows
    hidden_out, d_gate, d_up, grad_final, feed_keep, feed_send = call(
        feed_kernel,
        (
            info, activated, gate_value, up_value, normed_feed, after, cotangent, gains,
            *down_blocks,
        ),
        [SMEM] + [VMEM] * 7 + [ANY] * 2,
        [
            ((tokens, model), bf16),
            ((tokens, feed), bf16),
            ((tokens, feed), bf16),
            ((1, model), f32),
            ((2, feed_rows, lanes), bf16),
            ((2, feed_rows, lanes), bf16),
        ],
        [
            pltpu.VMEM((feed, model), bf16),
            pltpu.VMEM((tokens, model), bf16),
            pltpu.VMEM((model, tokens), bf16),
            sem((4,)),
        ],
        flops=token_flops * 5 * feed,
        limit=large_bytes,
        name="feed",
    )
    feed_near = flip(feed_send, "fsdp", 1)

    d_after, d_projected, d_mixed, table, grad_feed_gain, grad_mix_gain = call(
        feed_back_kernel,
        (
            info, d_gate, d_up, after, projected, attended, total, cotangent, gains,
            *feed_blocks, *output_blocks,
        ),
        [SMEM] + [VMEM] * 8 + [ANY] * 4,
        [
            ((tokens, model), f32),
            ((tokens, model), bf16),
            ((tokens, wide), bf16),
            ((2 * heads, tokens), f32),
            ((1, model), f32),
            ((1, model), f32),
        ],
        [
            pltpu.VMEM((model, feed), bf16),
            pltpu.VMEM((model, feed), bf16),
            pltpu.VMEM((wide, model), bf16),
            pltpu.VMEM((tokens, model), f32),
            sem((3, 4)),
        ],
        flops=token_flops * (2 * feed + wide),
        limit=large_bytes,
        name="feed_back",
    )

    feed_near, d_mixed = tie(feed_near, d_mixed)
    gate_rows = (feed // lanes) * rows
    half_rows = feed_rows // 2
    feed_sum = add_low(feed_keep[1], feed_near[1])
    d_mixed, feed_sum = tie(d_mixed, feed_sum)
    feed_far = flip(feed_sum, "fsdp", 2)
    bits = ctx_bits()
    steps = len(bits)
    turned = [bits[1], bits[0], *bits[2:]]

    query_grads = ()
    arrived = []
    waiting = None
    last = len(sources) - 1
    for number, (arrays, starts) in enumerate(reversed(sources)):
        first = number == 0
        count = len(arrays)

        def attend_back(*args, first=first, count=count):
            attend_back_kernel(first, count, *args)

        results = call(
            attend_back,
            (facts(*starts), queries, d_mixed, table, place_row, *arrays, *query_grads),
            [SMEM] + [VMEM] * (4 + count + len(query_grads)),
            [((tokens, wide), f32)] + [(a.shape, bf16) for a in arrays],
            [pltpu.VMEM((tokens, head_dim), f32), pltpu.VMEM((tokens, head_dim), f32)],
            flops=chunk_flops * 5,
            limit=vmem_bytes if ring else 48 * 1024 * 1024,
            name="attend_back",
        )
        query_grads = results[:1]
        if not ring:
            arrived.append(
                lax.psum_scatter(results[1], "ctx", scatter_dimension=0, tiled=True)
            )
            continue
        shift = last - number
        own, other = results[1:]
        if waiting is not None:
            crossed, held, *arrived = tie(waiting[1], query_grads[0], *arrived)
            query_grads = (held,)
            arrived = [send_back(add_low(waiting[0], crossed, *arrived), 2, groups)]
        waiting = (own, flip(other, "ctx", 1))
    if ring:
        arrived += list(waiting)

    query_rows = (wide // lanes) * rows
    output_rows = (model // lanes) * mixed_rows
    both_rows = (2 * head_dim // lanes) * rows + lanes
    pack_rows = query_rows + output_rows + both_rows
    d_normed_query, grad_query_gain, query_keep, query_send = call(
        query_back_kernel,
        (
            info, query_grads[0], query_raw, cosine, sine, gains, normed, mixed, d_projected,
            *query_blocks,
        ),
        [SMEM] + [VMEM] * 8 + [ANY] * 2,
        [
            ((tokens, model), f32),
            ((1, head_dim), f32),
            ((2, query_rows + output_rows, lanes), bf16),
            ((2, query_rows + output_rows, lanes), bf16),
        ],
        [
            pltpu.VMEM((model, wide), bf16),
            pltpu.VMEM((tokens, wide), bf16),
            pltpu.VMEM((model, tokens), bf16),
            sem((4,)),
        ],
        flops=token_flops * 3 * wide,
        name="query_back",
    )
    arrived_count = len(arrived)

    def key_back(*args):
        key_back_kernel(arrived_count, *args)

    grad_input, pack_keep, pack_send = call(
        key_back,
        (
            info, cosine, sine, gains, key_raw, normed, hidden, d_after,
            d_normed_query, grad_mix_gain, grad_feed_gain, grad_final, grad_query_gain,
            query_keep, query_send, *both_blocks, *arrived,
        ),
        [SMEM] + [VMEM] * 14 + [ANY] * 2 + [VMEM] * arrived_count,
        [
            ((tokens, model), f32),
            ((2, pack_rows, lanes), bf16),
            ((2, pack_rows, lanes), bf16),
        ],
        [
            pltpu.VMEM((model, 2 * head_dim), bf16),
            pltpu.VMEM((tokens, 2 * head_dim), bf16),
            pltpu.VMEM((model, tokens), bf16),
            pltpu.VMEM((gain_pad, model), f32),
            sem((4,)),
        ],
        flops=token_flops * 4 * head_dim,
        name="key_back",
    )
    pack_send, feed_far = tie(pack_send, feed_far)
    pack_near = flip(pack_send, "fsdp", 1)

    left = add_low(feed_keep[0, :half_rows], feed_near[0, :half_rows], feed_far[:half_rows])
    right = add_low(feed_keep[0, half_rows:], feed_near[0, half_rows:], feed_far[half_rows:])
    def unpack(packs, shapes):
        def kernel(*args):
            unpack_kernel(shapes, len(packs), *args)

        specs = [VMEM] * len(packs)
        return call(kernel, packs, specs, [(s, f32) for s in shapes], name="unpack")

    left, right, pack_near = tie(left, right, pack_near)
    pack = None
    for number in range(2 * steps + 2):
        if number < steps:
            left = scatter_step(left, bits[number])
            right = scatter_step(right, turned[number])
        elif number < 2 * steps:
            left = gather_step(left, bits[2 * steps - 1 - number])
            right = gather_step(right, turned[2 * steps - 1 - number])
        if number == 0:
            pack_far = flip(add_low(pack_keep[1], pack_near[1]), "fsdp", 2)
            left, right = tie(left, right)
        elif number == 1:
            left, right, pack_far = tie(left, right, pack_far)
            pack = add_low(pack_keep[0], pack_near[0], pack_far)
        else:
            now = number - 2
            if now < steps:
                pack = scatter_step(pack, bits[now])
            else:
                pack = gather_step(pack, bits[2 * steps - 1 - now])
            if number == 2 * steps:
                grad_gate, grad_up, grad_down = unpack(
                    (left, right), [gate_weight.shape, up_weight.shape, down_weight.shape]
                )
                pack, grad_gate, grad_up, grad_down = tie(pack, grad_gate, grad_up, grad_down)
            elif number < 2 * steps:
                left, right, pack = tie(left, right, pack)

    grad_query, grad_output, grad_key, grad_value, wide_gains, head_gains = unpack(
        (pack,),
        [
            query_weight.shape,
            output_weight.shape,
            key_weight.shape,
            value_weight.shape,
            (gain_pad, 2 * lanes),
            (gain_pad, lanes),
        ],
    )
    gain_shards = [wide_gains[i, :rows] for i in range(4)]
    gain_shards += [head_gains[i, : query_gain.shape[0]] for i in (4, 5)]
    return (
        hidden_out[None],
        grad_input[None],
        grad_query,
        grad_key,
        grad_value,
        grad_output,
        grad_gate,
        grad_up,
        grad_down,
        *gain_shards,
    )


def solution(mesh):
    token = P("fsdp", "ctx", None)
    weight = P("fsdp", None)
    gain = P("fsdp")
    return jax.shard_map(
        on_device,
        mesh=mesh,
        in_specs=(token, P("fsdp", "ctx")) + (weight,) * 7 + (gain,) * 6 + (token,),
        out_specs=(token, token) + (weight,) * 7 + (gain,) * 6,
        check_vma=False,
    )
```
